32 devices in a mesh: dp: 4 (over x, core), space: 2 (over y), tm: 4 (over z).
Axes of the slice: x: 2, y: 2, z: 4, core: 2. Of those that a mesh axis runs over, the one named last changes fastest.
Arguments:
- inputs: bfloat16 [4, 32, 64, 512], P('dp', 'tm', None, 'space'), may hold values from -6 to 6
- grad_out: bfloat16 [4, 32, 64, 512], P('dp', 'tm', None, 'space'), may hold values from -6 to 6
- conv_w: bfloat16 [2, 128, 64], replicated, may hold values from -0.5 to 0.5
- conv_b: float32 [128], replicated, may hold values from -3 to 3
- mix_w: bfloat16 [3, 64, 64], replicated, may hold values from -0.4375 to 0.4375
- mix_b: float32 [64], replicated, may hold values from -3 to 3
- adj_tiles: bfloat16 [4, 8, 128, 128], P('space'), may hold values from -0.1875 to 0.1875
- tile_cols: int32 [4, 8], P('space'), may hold values from 0 to 2, as said below
- send_rows: int32 [2, 2, 64], P('space'), may hold values from 0 to 255
- counts: int32 [2, 2], P('space'), may hold values from 0 to 64, as said below
Outputs:
- outputs: bfloat16 [4, 32, 64, 512], P('dp', 'tm', None, 'space')
- grad_inputs: bfloat16 [4, 32, 64, 512], P('dp', 'tm', None, 'space')
- grad_conv_w: float32 [2, 128, 64], replicated
- grad_conv_b: float32 [128], replicated
- grad_mix_w: float32 [3, 64, 64], replicated
- grad_mix_b: float32 [64], replicated
The draws below stay inside these ranges and needn't reach their ends.
Inputs may be any that keep to these rules, and one draw needn't show every extreme that they name: counts[s, s] = 0; counts[0, 1] = 64. `tile_cols`: column blocks below 2 are the part's own sensor blocks, 2 + i the i-th block of 128 received slots in order of source part and slot; in each row block the first 4 ids are below 2, the others are not.
All inputs are finite; a program needn't handle non-finite values.
Results may differ from the reference program's by a relative error of at most 0.0058.
Values may be sent and summed in bfloat16 or wider, within the bound.
No kernel may reach another device: no remote copies, remote signals or barrier semaphores. Data moves between devices by JAX's collectives and lax.ppermute only.
A program may use at most 64 MiB of HBM per device.

```python
import math
import jax
import jax.numpy as jnp
from jax import lax

CH = 64
TILE = 128
KT = 8
DILATION_SIZE = 2
NS_DEV = 256
BMAX = 64
RB = 2
HALO = 128
HB = 1
BATCH = 4
TIME = 32
SENSORS = 512
CELLS = 65536
N_SPACE = 2


def draw_counts(key, part):
    loaded = jax.random.randint(jax.random.fold_in(key, 11), (N_SPACE, N_SPACE), BMAX // 4, BMAX + 1)
    source = lax.broadcasted_iota(jnp.int32, (N_SPACE, N_SPACE), 0)
    target = lax.broadcasted_iota(jnp.int32, (N_SPACE, N_SPACE), 1)
    filled = jnp.where((source == 0) & (target == 1), BMAX, loaded)
    return jnp.where(target == source, 0, filled).astype(jnp.int32)


def draw_tile_cols(key, part):
    half_slots = KT // 2
    row_total = N_SPACE * RB
    own_cols = jax.random.randint(jax.random.fold_in(key, 21), (row_total, half_slots), 0, RB)
    offsets = jax.random.randint(jax.random.fold_in(key, 22), (N_SPACE,), 0, HB)
    row_ids = lax.broadcasted_iota(jnp.int32, (row_total, half_slots), 0)
    slot_ids = lax.broadcasted_iota(jnp.int32, (row_total, half_slots), 1)
    local_row = row_ids % RB
    own_cols = jnp.where(slot_ids == 0, local_row, own_cols)
    remote_cols = RB + (local_row * half_slots + slot_ids + offsets[row_ids // RB]) % HB
    return jnp.concatenate([own_cols, remote_cols], 1).astype(jnp.int32)


def plant(result, key, low, top_value):
    dims = result.shape
    spot = [jax.random.randint(jax.random.fold_in(key, axis), (), 0, dims[axis]) for axis in range(len(dims))]
    result = result.at[tuple(spot)].set(low)
    longest = dims.index(max(dims))
    spot[longest] = (spot[longest] + 1) % dims[longest]
    return result.at[tuple(spot)].set(top_value)


def steps_of(key, shape, split, smallest, high):
    def one(dim, parts):
        draws = jax.random.uniform(jax.random.fold_in(jax.random.fold_in(key, 6), dim), (parts,), jnp.float32, smallest / len(split), high / len(split))
        return jnp.repeat(jnp.exp(draws), shape[dim] // parts).reshape((-1,) + (1,) * (len(shape) - dim - 1))

    level = one(*split[0])
    for cut in split[1:]:
        level = level * one(*cut)
    return level


def centred(own_key, dims, spread, limit, pieces=(), held_as=jnp.bfloat16):
    loudness = steps_of(own_key, dims, pieces, -0.22, 0.18) if pieces else 1.0
    result = jax.random.normal(own_key, dims, jnp.float32) * spread * loudness
    return jnp.minimum(jnp.maximum(result, -limit), limit).astype(held_as)


def setup_inputs(seed: int = 0) -> dict:
    splits = jax.random.split(jax.random.key(seed), 11)
    inputs = centred(splits[0], (BATCH, TIME, CH, SENSORS), 1.0, 6.0, ((0, 4), (1, 4), (3, 2)))
    grad_out = centred(splits[1], (BATCH, TIME, CH, SENSORS), 1.0, 6.0, ((0, 4), (1, 4), (3, 2)))
    conv_w = centred(splits[2], (2, 2 * CH, CH), (2 * CH) ** -0.5, 0.5)
    conv_b = centred(splits[3], (2 * CH,), 0.5, 3.0, (), jnp.float32)
    mix_w = centred(splits[4], (3, CH, CH), (3 * CH) ** -0.5, 0.4375)
    mix_b = centred(splits[5], (CH,), 0.5, 3.0, (), jnp.float32)
    adj_tiles = centred(splits[6], (N_SPACE * RB, KT, TILE, TILE), (KT * TILE) ** -0.5, 0.1875, ((0, 2),))
    tile_cols = draw_tile_cols(jax.random.fold_in(splits[10], 71), 0)
    send_rows = plant(jax.random.randint(splits[8], (N_SPACE, N_SPACE, BMAX), 0, NS_DEV), jax.random.fold_in(splits[8], 1), 0, NS_DEV - 1).astype(jnp.int32)
    counts = draw_counts(jax.random.fold_in(splits[10], 71), 0)
    return dict(inputs=inputs, grad_out=grad_out, conv_w=conv_w, conv_b=conv_b, mix_w=mix_w, mix_b=mix_b, adj_tiles=adj_tiles, tile_cols=tile_cols, send_rows=send_rows, counts=counts)


def boundary_rows(field, send_rows, counts):
    owners = jnp.arange(N_SPACE, dtype=jnp.int32)
    global_idx = owners[:, None, None] * NS_DEV + send_rows
    slots = jnp.arange(BMAX, dtype=jnp.int32)
    live_slots = (slots[None, None, :] < counts[:, :, None]).astype(field.dtype)
    return field[:, :, global_idx] * live_slots

def diffuse(field, adj_tiles, tile_cols, send_rows, counts):
    timestep_count, chan_count = (field.shape[0], field.shape[1])
    gathered = boundary_rows(field, send_rows, counts)

    def per_part(part):
        local_rows = lax.dynamic_slice_in_dim(field, part * NS_DEV, NS_DEV, 2)
        halo_rows = jnp.take(gathered, part, axis=3).reshape(timestep_count, chan_count, HALO)
        extended = jnp.concatenate([local_rows, halo_rows], axis=2)
        blocks = extended.reshape(timestep_count, chan_count, RB + HB, TILE)
        part_cols = lax.dynamic_slice_in_dim(tile_cols, part * RB, RB, 0)
        part_tiles = lax.dynamic_slice_in_dim(adj_tiles, part * RB, RB, 0).astype(jnp.float32)
        picked = blocks[:, :, part_cols].astype(jnp.float32)
        product = jnp.einsum('tcrkj,rkij->tcri', picked, part_tiles)
        return product.reshape(timestep_count, chan_count, NS_DEV).astype(jnp.bfloat16)
    results = lax.map(per_part, jnp.arange(N_SPACE, dtype=jnp.int32))
    return jnp.transpose(results, (1, 2, 0, 3)).reshape(field.shape)

def diffuse_back(grad, adj_tiles, tile_cols, send_rows, counts):
    timestep_count, chan_count = (grad.shape[0], grad.shape[1])

    def per_part(part):
        local_rows = lax.dynamic_slice_in_dim(grad, part * NS_DEV, NS_DEV, 2)
        blocks = local_rows.reshape(timestep_count, chan_count, RB, TILE).astype(jnp.float32)
        part_cols = lax.dynamic_slice_in_dim(tile_cols, part * RB, RB, 0)
        part_tiles = lax.dynamic_slice_in_dim(adj_tiles, part * RB, RB, 0).astype(jnp.float32)
        product = jnp.einsum('tcri,rkij->tcrkj', blocks, part_tiles)
        extended = jnp.zeros((timestep_count, chan_count, RB + HB, TILE), jnp.float32)
        extended = extended.at[:, :, part_cols].add(product)
        extended = extended.reshape(timestep_count, chan_count, NS_DEV + HALO)
        return (extended[:, :, :NS_DEV], extended[:, :, NS_DEV:].astype(jnp.bfloat16))
    local_parts, halo_parts = lax.map(per_part, jnp.arange(N_SPACE, dtype=jnp.int32))
    total = jnp.transpose(local_parts, (1, 2, 0, 3)).reshape(grad.shape)
    halo_parts = halo_parts.reshape(N_SPACE, timestep_count, chan_count, N_SPACE, BMAX)
    halo_parts = jnp.transpose(halo_parts, (1, 2, 3, 0, 4)).astype(jnp.float32)
    owners = jnp.arange(N_SPACE, dtype=jnp.int32)
    global_idx = owners[:, None, None] * NS_DEV + send_rows
    slots = jnp.arange(BMAX, dtype=jnp.int32)
    live_slots = (slots[None, None, :] < counts[:, :, None]).astype(jnp.float32)
    return total.at[:, :, global_idx].add(halo_parts * live_slots)

def reference(inputs, grad_out, conv_w, conv_b, mix_w, mix_b, adj_tiles, tile_cols, send_rows, counts):
    conv_f = conv_w.astype(jnp.float32)
    mix_f = mix_w.astype(jnp.float32)

    def per_sample(pair):
        sample_input, sample_grad = pair
        timestep_count = sample_input.shape[0]
        zero_border_slice = jnp.zeros((DILATION_SIZE,) + sample_input.shape[1:], jnp.bfloat16)
        preceding_window = jnp.concatenate([zero_border_slice, sample_input[:timestep_count - DILATION_SIZE]], 0)
        input_f = sample_input.astype(jnp.float32)
        previous_f = preceding_window.astype(jnp.float32)
        preact = jnp.einsum('oc,tcn->ton', conv_f[1], input_f) + jnp.einsum('oc,tcn->ton', conv_f[0], previous_f)
        preact = preact + conv_b[None, :, None]
        filtered = jnp.tanh(preact[:, :CH])
        gating = jax.nn.sigmoid(preact[:, CH:])
        hidden = (filtered * gating).astype(jnp.bfloat16)
        hop_one = diffuse(hidden, adj_tiles, tile_cols, send_rows, counts)
        hop_two = diffuse(hop_one, adj_tiles, tile_cols, send_rows, counts)
        fields = (hidden, hop_one, hop_two)
        mixed = mix_b[None, :, None] + input_f
        for index in range(3):
            mixed = mixed + jnp.einsum('oc,tcn->ton', mix_f[index], fields[index].astype(jnp.float32))
        outputs = mixed.astype(jnp.bfloat16)
        grad_f = sample_grad.astype(jnp.float32)
        back_two = jnp.einsum('oc,ton->tcn', mix_f[2], grad_f).astype(jnp.bfloat16)
        back_one = jnp.einsum('oc,ton->tcn', mix_f[1], grad_f) + diffuse_back(back_two, adj_tiles, tile_cols, send_rows, counts)
        back_one = back_one.astype(jnp.bfloat16)
        back_hidden = jnp.einsum('oc,ton->tcn', mix_f[0], grad_f) + diffuse_back(back_one, adj_tiles, tile_cols, send_rows, counts)
        grad_filter = back_hidden * (1.0 - filtered * filtered) * gating
        grad_gate = back_hidden * filtered * gating * (1.0 - gating)
        backward_preactivation = jnp.concatenate([grad_filter, grad_gate], 1).astype(jnp.bfloat16).astype(jnp.float32)
        following_window = jnp.concatenate([backward_preactivation[DILATION_SIZE:], jnp.zeros((DILATION_SIZE,) + backward_preactivation.shape[1:], jnp.float32)], 0)
        grad_inputs = grad_f + jnp.einsum('oc,ton->tcn', conv_f[1], backward_preactivation) + jnp.einsum('oc,ton->tcn', conv_f[0], following_window)
        grad_inputs = grad_inputs.astype(jnp.bfloat16)
        grad_conv_w = jnp.stack([jnp.einsum('ton,tcn->oc', backward_preactivation, previous_f), jnp.einsum('ton,tcn->oc', backward_preactivation, input_f)])
        grad_conv_b = lax.optimization_barrier(jnp.sum(backward_preactivation, axis=(0, 2)))
        grad_mix_w = jnp.stack([jnp.einsum('ton,tcn->oc', grad_f, item.astype(jnp.float32)) for item in fields])
        grad_mix_b = lax.optimization_barrier(jnp.sum(grad_f, axis=(0, 2)))
        return (outputs, grad_inputs, grad_conv_w, grad_conv_b, grad_mix_w, grad_mix_b)
    results = lax.map(per_sample, (inputs, grad_out))
    scale = 1.0 / math.sqrt(CELLS)
    return (results[0], results[1], lax.optimization_barrier(jnp.sum(results[2], 0)) * scale, lax.optimization_barrier(jnp.sum(results[3], 0)) * scale, lax.optimization_barrier(jnp.sum(results[4], 0)) * scale, lax.optimization_barrier(jnp.sum(results[5], 0)) * scale)
```

```python
import functools
import math

import jax
import jax.numpy as jnp
from jax import lax
from jax.experimental import pallas as pl
from jax.experimental.pallas import tpu as pltpu
from jax.sharding import PartitionSpec as P

DILATION_SIZE = 2


def from_behind(value, axis, steps):
    count = lax.axis_size(axis)
    leading, last = (max(0, -steps), min(count, count - steps))
    return lax.ppermute(value, axis, [(source, source + steps) for source in range(leading, last)])


def slot_mask(counts, slot_count, dtype):
    slots = lax.broadcasted_iota(jnp.int32, (counts.shape[1], slot_count), 1)
    return (slots < counts[0][:, None]).astype(dtype)


def pack_rows(field, send_rows, live_slots):
    picked = field[:, :, send_rows[0]] * live_slots
    return picked.reshape(field.shape[0], field.shape[1], -1)


def tile_product(extended, adj_tiles, tile_cols):
    timestep_count, chan_count = (extended.shape[0], extended.shape[1])
    blocks = extended.reshape(timestep_count, chan_count, -1, adj_tiles.shape[2])
    picked = blocks[:, :, tile_cols]
    return jnp.einsum("tcrkj,rkij->tcri", picked, adj_tiles, preferred_element_type=jnp.float32)


def forward_start(field, send_rows, live_slots):
    packed = pack_rows(field, send_rows, live_slots)
    own_part = None
    return (packed, own_part)


def forward_finish(field, received, adj_tiles, tile_cols):
    total = tile_product(jnp.concatenate([field, received], 2), adj_tiles, tile_cols)
    return total.reshape(field.shape).astype(jnp.bfloat16)


def back_start(grad, adj_tiles, tile_cols, send_rows):
    timestep_count, chan_count, sensor_count = grad.shape
    tile_size = adj_tiles.shape[2]
    row_blocks = sensor_count // tile_size
    half_slots = tile_cols.shape[1] // 2
    halo_blocks = send_rows.shape[1] * send_rows.shape[2] // tile_size
    blocks = grad.reshape(timestep_count, chan_count, row_blocks, tile_size)
    remote_terms = jnp.einsum(
        "tcri,rkij->tcrkj", blocks, adj_tiles[:, half_slots:], preferred_element_type=jnp.float32
    )
    remote_sums = jnp.zeros((timestep_count, chan_count, halo_blocks, tile_size), jnp.float32)
    remote_sums = remote_sums.at[:, :, tile_cols[:, half_slots:] - row_blocks].add(remote_terms)
    return remote_sums.reshape(timestep_count, chan_count, -1).astype(jnp.bfloat16)


def back_finish(grad, returned, adj_tiles, tile_cols, send_rows, live_slots):
    timestep_count, chan_count, sensor_count = grad.shape
    tile_size = adj_tiles.shape[2]
    row_blocks = sensor_count // tile_size
    half_slots = tile_cols.shape[1] // 2
    blocks = grad.reshape(timestep_count, chan_count, row_blocks, tile_size)
    own_terms = jnp.einsum(
        "tcri,rkij->tcrkj", blocks, adj_tiles[:, :half_slots], preferred_element_type=jnp.float32
    )
    total = jnp.zeros((timestep_count, chan_count, row_blocks, tile_size), jnp.float32)
    total = total.at[:, :, tile_cols[:, :half_slots]].add(own_terms).reshape(grad.shape)
    returned = returned.reshape(
        timestep_count, chan_count, send_rows.shape[1], send_rows.shape[2]
    ).astype(jnp.float32)
    return total.at[:, :, send_rows[0]].add(returned * live_slots.astype(jnp.float32))


def mixing_grads(sample_grad, fields):
    grad_mix_w = jnp.stack(
        [
            jnp.einsum("ton,tcn->oc", sample_grad, item, preferred_element_type=jnp.float32)
            for item in fields
        ]
    )
    grad_mix_b = jnp.sum(sample_grad.astype(jnp.float32), axis=(0, 2))
    return (grad_mix_w, grad_mix_b)


def general_body(inputs, grad_out, conv_w, conv_b, mix_w, mix_b, adj_tiles, tile_cols, send_rows, counts):
    sample_input = inputs[0]
    sample_grad = grad_out[0]
    timestep_count, chan_count, sensor_count = sample_input.shape
    live_slots = slot_mask(counts, send_rows.shape[2], jnp.bfloat16)
    prior_border_slice = from_behind(sample_input[timestep_count - DILATION_SIZE :], "tm", 1)
    preceding_window = jnp.concatenate(
        [prior_border_slice, sample_input[: timestep_count - DILATION_SIZE]], 0
    )
    preact = jnp.einsum("oc,tcn->ton", conv_w[1], sample_input, preferred_element_type=jnp.float32)
    preact = preact + jnp.einsum(
        "oc,tcn->ton", conv_w[0], preceding_window, preferred_element_type=jnp.float32
    )
    preact = preact + conv_b[None, :, None]
    filtered = jnp.tanh(preact[:, :chan_count])
    gating = jax.nn.sigmoid(preact[:, chan_count:])
    hidden = (filtered * gating).astype(jnp.bfloat16)
    grad_float = sample_grad.astype(jnp.float32)
    packed_one, early_one = forward_start(hidden, send_rows, live_slots)
    received_one = lax.all_to_all(packed_one, "space", split_axis=2, concat_axis=2, tiled=True)
    hop_one = forward_finish(hidden, received_one, adj_tiles, tile_cols)
    packed_two, early_two = forward_start(hop_one, send_rows, live_slots)
    received_two = lax.all_to_all(packed_two, "space", split_axis=2, concat_axis=2, tiled=True)
    hop_two = forward_finish(hop_one, received_two, adj_tiles, tile_cols)
    fields = (hidden, hop_one, hop_two)
    grad_mix_w, grad_mix_b = mixing_grads(sample_grad, fields)
    back_two = jnp.einsum(
        "oc,ton->tcn", mix_w[2], sample_grad, preferred_element_type=jnp.float32
    ).astype(jnp.bfloat16)
    returned_two = lax.all_to_all(
        back_start(back_two, adj_tiles, tile_cols, send_rows),
        "space",
        split_axis=2,
        concat_axis=2,
        tiled=True,
    )
    back_one = jnp.einsum("oc,ton->tcn", mix_w[1], sample_grad, preferred_element_type=jnp.float32)
    back_one = (
        back_one + back_finish(back_two, returned_two, adj_tiles, tile_cols, send_rows, live_slots)
    ).astype(jnp.bfloat16)
    returned_one = lax.all_to_all(
        back_start(back_one, adj_tiles, tile_cols, send_rows),
        "space",
        split_axis=2,
        concat_axis=2,
        tiled=True,
    )
    back_hidden = jnp.einsum(
        "oc,ton->tcn", mix_w[0], sample_grad, preferred_element_type=jnp.float32
    )
    back_hidden = back_hidden + back_finish(
        back_one, returned_one, adj_tiles, tile_cols, send_rows, live_slots
    )
    mixed = sample_input.astype(jnp.float32) + mix_b[None, :, None]
    for index in range(3):
        mixed = mixed + jnp.einsum(
            "oc,tcn->ton", mix_w[index], fields[index], preferred_element_type=jnp.float32
        )
    outputs = mixed.astype(jnp.bfloat16)[None]
    grad_filter = back_hidden * (1.0 - filtered * filtered) * gating
    grad_gate = back_hidden * filtered * gating * (1.0 - gating)
    backward_preactivation = jnp.concatenate([grad_filter, grad_gate], 1).astype(jnp.bfloat16)
    next_border_slice = from_behind(backward_preactivation[:DILATION_SIZE], "tm", -1)
    following_window = jnp.concatenate(
        [backward_preactivation[DILATION_SIZE:], next_border_slice], 0
    )
    grad_inputs = grad_float + jnp.einsum(
        "oc,ton->tcn", conv_w[1], backward_preactivation, preferred_element_type=jnp.float32
    )
    grad_inputs = grad_inputs + jnp.einsum(
        "oc,ton->tcn", conv_w[0], following_window, preferred_element_type=jnp.float32
    )
    grad_inputs = grad_inputs.astype(jnp.bfloat16)[None]
    grad_conv_w = jnp.stack(
        [
            jnp.einsum(
                "ton,tcn->oc",
                backward_preactivation,
                preceding_window,
                preferred_element_type=jnp.float32,
            ),
            jnp.einsum(
                "ton,tcn->oc",
                backward_preactivation,
                sample_input,
                preferred_element_type=jnp.float32,
            ),
        ]
    )
    grad_conv_b = jnp.sum(backward_preactivation.astype(jnp.float32), axis=(0, 2))
    grad_conv_w, grad_conv_b, grad_mix_w, grad_mix_b = lax.psum(
        (grad_conv_w, grad_conv_b, grad_mix_w, grad_mix_b), ("dp", "space", "tm")
    )
    cell_count = (
        inputs.shape[0]
        * timestep_count
        * sensor_count
        * lax.axis_size("dp")
        * lax.axis_size("space")
        * lax.axis_size("tm")
    )
    scale = 1.0 / math.sqrt(cell_count)
    return (
        outputs,
        grad_inputs,
        grad_conv_w * scale,
        grad_conv_b * scale,
        grad_mix_w * scale,
        grad_mix_b * scale,
    )


BF16 = jnp.bfloat16
F32 = jnp.float32
NT = (((1,), (1,)), ((), ()))
VMEM_BYTES = 24 * 1024 * 1024


def mm(left, right):
    return jnp.dot(left, right, preferred_element_type=F32)


def mm_nt(left, right):
    return lax.dot_general(left, right, NT, preferred_element_type=F32)


def lane_half(rows, width):
    lanes = lax.broadcasted_iota(jnp.int32, (rows, width), 1)
    return (lanes >= width // 2).astype(jnp.int32)


def slot_matrix(rows_ref, counts_ref, other, sensor_count):
    slot_count = rows_ref.shape[2]
    rows = rows_ref[0, pl.ds(other, 1), :]
    rows = jnp.concatenate([rows, rows], 1)
    lanes = lax.broadcasted_iota(jnp.int32, (1, 2 * slot_count), 1)
    slots = lanes - jnp.where(lanes >= slot_count, slot_count, 0)
    rows = jnp.where(slots < counts_ref[0, other], rows, -1)
    sensors = lax.broadcasted_iota(jnp.int32, (sensor_count, 2 * slot_count), 0)
    return jnp.where(sensors == rows, 1.0, 0.0).astype(F32)


def keep_half(matrix, half):
    return jnp.where(lane_half(*matrix.shape) == half, matrix, jnp.zeros_like(matrix))


def link_matrix(packed_ref, field_rows, other):
    small = packed_ref[field_rows:, :]
    blank = jnp.zeros_like(small)
    return jnp.concatenate(
        [jnp.where(other == 0, small, blank), jnp.where(other == 1, small, blank)], 0
    )


def column(row):
    size = row.shape[1]
    first = lax.broadcasted_iota(jnp.int32, (size, size), 0)
    second = lax.broadcasted_iota(jnp.int32, (size, size), 1)
    return jnp.sum(jnp.where(first == second, row, 0.0), axis=1, keepdims=True)


def prepare_kernel(cols_ref, counts_ref, rows_ref, adj_ref, grad_ref, packed_ref, own_ref, halo_ref):
    me = lax.axis_index("space")
    other = 1 - me
    row_blocks, slots, tile = adj_ref.shape[0], adj_ref.shape[1], adj_ref.shape[2]
    own_slots = slots // 2
    field_rows = grad_ref.shape[0]
    for r in range(row_blocks):
        at = slice(r * tile, (r + 1) * tile)
        sums = [jnp.zeros((tile, tile), F32), jnp.zeros((tile, tile), F32)]
        for k in range(own_slots):
            item = adj_ref[r, k].astype(F32)
            for block in range(2):
                share = jnp.where(cols_ref[r, k] == block, 1.0, 0.0).astype(F32)
                sums[block] = sums[block] + item * share
        own_ref[at, :] = jnp.concatenate(sums, 1).astype(BF16)
        far = adj_ref[r, own_slots].astype(F32)
        for k in range(own_slots + 1, slots):
            far = far + adj_ref[r, k].astype(F32)
        far = jnp.where(lane_half(tile, tile) == other, far, pltpu.roll(far, tile // 2, 1))
        halo_ref[at, :] = far.astype(BF16)
    own = own_ref[...]
    halo = halo_ref[...]
    halo_other = keep_half(halo, other)
    halo_mine = keep_half(halo, me)
    grad = grad_ref[...]
    first = mm(grad, own).astype(BF16)
    packed_ref[:field_rows, :] = (mm(grad, halo_other) + mm(first, halo_mine)).astype(BF16)
    chosen = slot_matrix(rows_ref, counts_ref, other, own.shape[0])
    chosen = jnp.transpose(chosen)[: chosen.shape[1] // 2].astype(BF16)
    packed_ref[field_rows:, :] = mm(chosen, halo_mine).astype(BF16)


def main_kernel(
    counts_ref,
    rows_ref,
    input_ref,
    border_ref,
    grad_ref,
    own_packed_ref,
    packed_ref,
    own_ref,
    halo_ref,
    conv_w_ref,
    conv_b_ref,
    mix_w_ref,
    kept_ref,
    given_ref,
    boundary_ref,
    hidden_ref,
    back_ref,
    border_out_ref,
    left_scr,
    right_scr,
    one_scr,
    two_scr,
):
    me = lax.axis_index("space")
    other = 1 - me
    core = lax.axis_index("dp") % 2
    steps, chans, sensors = input_ref.shape
    field_rows = steps * chans
    own = own_ref[...]
    halo = halo_ref[...]
    chosen = slot_matrix(rows_ref, counts_ref, other, sensors).astype(BF16)
    chosen_mine = keep_half(chosen, me)
    chosen_other = keep_half(chosen, other)
    link = link_matrix(packed_ref, field_rows, other)
    packed = packed_ref[:field_rows, :]
    grad = grad_ref[...]
    one = (mm(grad, own) + mm_nt(packed, chosen_mine)).astype(BF16)
    back = (packed.astype(F32) + mm(own_packed_ref[:field_rows, :], link)).astype(BF16)
    two = (mm(one, own) + mm_nt(back, chosen_other)).astype(BF16)
    one_scr[...] = one
    two_scr[...] = two
    taps = jnp.concatenate([conv_w_ref[0], conv_w_ref[1]], 1)
    bias = column(conv_b_ref[...])
    mixing = jnp.transpose(mix_w_ref[...].reshape(3 * chans, chans).astype(F32)).astype(BF16)
    ones = jnp.ones((chans, sensors), BF16)
    for t in range(steps):
        at = slice(t * chans, (t + 1) * chans)
        earlier = border_ref[t] if t < DILATION_SIZE else input_ref[t - DILATION_SIZE]
        window = jnp.concatenate([earlier, input_ref[t]], 0)
        preact = mm(taps, window) + bias
        filtered = jnp.tanh(preact[:chans])
        gating = 0.5 * jnp.tanh(0.5 * preact[chans:]) + 0.5
        hidden = (filtered * gating).astype(BF16)
        hidden_ref[at, :] = hidden
        fields = jnp.concatenate([grad_ref[at, :], one_scr[at, :], two_scr[at, :]], 0)
        back_hidden = mm(mixing, fields)
        back_pre = jnp.concatenate(
            [
                back_hidden * (1.0 - filtered * filtered) * gating,
                back_hidden * filtered * gating * (1.0 - gating),
            ],
            0,
        ).astype(BF16)
        back_ref[t] = back_pre
        if t < DILATION_SIZE:
            border_out_ref[t] = back_pre
        span = slice(t * sensors, (t + 1) * sensors)
        left_scr[: 2 * chans, span] = back_pre
        left_scr[2 * chans :, span] = fields
        right_scr[: 2 * chans, span] = window
        right_scr[2 * chans :, span] = jnp.concatenate([hidden, ones], 0)
    hidden_all = hidden_ref[...]
    hop = mm_nt(hidden_all, own).astype(BF16)
    boundary_ref[...] = (mm(hidden_all, chosen_other) + mm(hop, chosen_mine)).astype(BF16)
    sums = mm_nt(left_scr[...], right_scr[...])
    conv = sums[: 2 * chans, : 2 * chans]
    wide = 2 * chans
    zero, first, second = [
        sums[wide + k * chans : wide + (k + 1) * chans, wide:] for k in range(3)
    ]
    lanes = lax.broadcasted_iota(jnp.int32, (chans, wide), 1)
    top = jnp.where(lanes < chans, zero, pltpu.roll(first, chans, 1))
    bottom = jnp.where(lanes < chans, second, zero)
    bottom = jnp.where(lanes >= chans + chans // 4, sums[:chans, wide:], bottom)
    bottom = jnp.where(lanes >= chans + chans // 2, sums[chans:wide, wide:], bottom)
    mixes = jnp.concatenate([top, bottom], 0)
    kept_ref[...] = jnp.where(core == 0, conv, mixes)
    given_ref[...] = jnp.where(core == 0, mixes, conv)


def outputs_kernel(
    input_ref,
    hidden_ref,
    own_boundary_ref,
    boundary_ref,
    packed_ref,
    own_ref,
    halo_ref,
    mix_w_ref,
    mix_b_ref,
    out_ref,
):
    me = lax.axis_index("space")
    other = 1 - me
    steps, chans, sensors = input_ref.shape
    own = own_ref[...]
    halo = halo_ref[...]
    link = link_matrix(packed_ref, steps * chans, other)
    boundary = boundary_ref[...]
    hidden = hidden_ref[...]
    one = (mm_nt(hidden, own) + mm_nt(boundary, keep_half(halo, me))).astype(BF16)
    far = (boundary.astype(F32) + mm_nt(own_boundary_ref[...], link)).astype(BF16)
    two = (mm_nt(one, own) + mm_nt(far, keep_half(halo, other))).astype(BF16)
    bias = column(mix_b_ref[...])
    for t in range(steps):
        at = slice(t * chans, (t + 1) * chans)
        mixed = mm(mix_w_ref[0], hidden[at]) + mm(mix_w_ref[1], one[at]) + mm(mix_w_ref[2], two[at])
        out_ref[t] = (mixed + bias + input_ref[t].astype(F32)).astype(BF16)


def input_grad_kernel(grad_ref, back_ref, border_ref, conv_w_ref, out_ref):
    steps, chans, sensors = grad_ref.shape
    taps = conv_w_ref[...].reshape(4 * chans, chans).astype(F32)
    taps = jnp.transpose(taps).astype(BF16)
    for t in range(steps):
        later = t + DILATION_SIZE
        following = back_ref[later] if later < steps else border_ref[later - steps]
        both = jnp.concatenate([following, back_ref[t]], 0)
        out_ref[t] = (mm(taps, both) + grad_ref[t].astype(F32)).astype(BF16)


def final_kernel(scale, kept_ref, other_ref, conv_w_ref, conv_b_ref, mix_w_ref, mix_b_ref):
    core = lax.axis_index("dp") % 2
    kept = kept_ref[...] * scale
    other = other_ref[...] * scale
    conv = jnp.where(core == 0, kept, other)
    mixes = jnp.where(core == 0, other, kept)
    chans = conv.shape[1] // 2
    conv_w_ref[0] = conv[:, :chans]
    conv_w_ref[1] = pltpu.roll(conv, chans, 1)[:, :chans]
    mix_w_ref[0] = mixes[:chans, :chans]
    mix_w_ref[1] = pltpu.roll(mixes[:chans], chans, 1)[:, :chans]
    mix_w_ref[2] = mixes[chans:, :chans]
    turned = jnp.transpose(mixes)
    mix_b_ref[...] = turned[chans : chans + 1, chans:]
    half, quarter = chans + chans // 2, chans + chans // 4
    conv_b_ref[...] = jnp.concatenate(
        [turned[quarter : quarter + 1, chans:], turned[half : half + 1, chans:]], 1
    )


VMEM = pl.BlockSpec(memory_space=pltpu.VMEM)
SMEM = pl.BlockSpec(memory_space=pltpu.SMEM)


def call(kernel, name, in_specs, out_shape, args, scratch=(), flops=0, moved=0):
    return pl.pallas_call(
        kernel,
        out_shape=out_shape,
        in_specs=in_specs,
        out_specs=jax.tree.map(lambda _: VMEM, out_shape),
        scratch_shapes=list(scratch),
        compiler_params=pltpu.CompilerParams(vmem_limit_bytes=VMEM_BYTES),
        cost_estimate=pl.CostEstimate(flops=flops, bytes_accessed=moved, transcendentals=0),
        name=name,
    )(*args)


def swap(value, axis, bit):
    count = lax.axis_size(axis)
    return lax.ppermute(value, axis, [(source, source ^ bit) for source in range(count)])


def bits(count):
    return [1 << place for place in range(count.bit_length() - 1)]


def pair_body(inputs, grad_out, conv_w, conv_b, mix_w, mix_b, adj_tiles, tile_cols, send_rows, counts):
    sample_input = inputs[0]
    sample_grad = grad_out[0]
    steps, chans, sensors = sample_input.shape
    field_rows = steps * chans
    wide = 2 * chans
    shape = jax.ShapeDtypeStruct
    grad_flat = sample_grad.reshape(field_rows, sensors)
    packed, own, halo = call(
        prepare_kernel,
        "prepare",
        [SMEM, SMEM, VMEM, VMEM, VMEM],
        (
            shape((field_rows + chans, wide), BF16),
            shape((sensors, sensors), BF16),
            shape((sensors, wide), BF16),
        ),
        (tile_cols, counts, send_rows, adj_tiles, grad_flat),
    )
    border = from_behind(sample_input[steps - DILATION_SIZE :], "tm", 1)
    packed_far = swap(packed, "space", 1)
    kept, given, boundary, hidden, back, back_border = call(
        main_kernel,
        "main",
        [SMEM] + [VMEM] * 11,
        (
            shape((wide, wide), F32),
            shape((wide, wide), F32),
            shape((field_rows, wide), BF16),
            shape((field_rows, sensors), BF16),
            shape((steps, wide, sensors), BF16),
            shape((DILATION_SIZE, wide, sensors), BF16),
        ),
        (
            counts,
            send_rows,
            sample_input,
            border,
            grad_flat,
            packed,
            packed_far,
            own,
            halo,
            conv_w,
            conv_b.reshape(1, wide),
            mix_w,
        ),
        scratch=(
            pltpu.VMEM((5 * chans, steps * sensors), BF16),
            pltpu.VMEM((4 * chans, steps * sensors), BF16),
            pltpu.VMEM((field_rows, sensors), BF16),
            pltpu.VMEM((field_rows, sensors), BF16),
        ),
    )
    total = kept + swap(given, "dp", 1)
    boundary_far = swap(boundary, "space", 1)
    back_border_far = from_behind(back_border, "tm", -1)
    for axis, bit in (
        [("dp", bit) for bit in bits(lax.axis_size("dp"))[1:]]
        + [("space", bit) for bit in bits(lax.axis_size("space"))]
        + [("tm", bit) for bit in bits(lax.axis_size("tm"))]
    ):
        total = total + swap(total, axis, bit)
    total_far = swap(total, "dp", 1)
    outputs = call(
        outputs_kernel,
        "outputs",
        [VMEM] * 9,
        shape(sample_input.shape, BF16),
        (
            sample_input,
            hidden,
            boundary,
            boundary_far,
            packed_far,
            own,
            halo,
            mix_w,
            mix_b.reshape(1, chans),
        ),
        flops=2 * field_rows * sensors * 1000,
        moved=8 * field_rows * sensors,
    )
    grad_inputs = call(
        input_grad_kernel,
        "input_grad",
        [VMEM] * 4,
        shape(sample_grad.shape, BF16),
        (sample_grad, back, back_border_far, conv_w),
        flops=2 * field_rows * sensors * 256,
        moved=8 * field_rows * sensors,
    )
    cell_count = (
        inputs.shape[0]
        * steps
        * sensors
        * lax.axis_size("dp")
        * lax.axis_size("space")
        * lax.axis_size("tm")
    )
    scale = 1.0 / math.sqrt(cell_count)
    grad_conv_w, grad_conv_b, grad_mix_w, grad_mix_b = call(
        functools.partial(final_kernel, scale),
        "final",
        [VMEM] * 2,
        (
            shape((2, wide, chans), F32),
            shape((1, wide), F32),
            shape((3, chans, chans), F32),
            shape((1, chans), F32),
        ),
        (total, total_far),
    )
    return (
        outputs[None],
        grad_inputs[None],
        grad_conv_w,
        grad_conv_b.reshape(wide),
        grad_mix_w,
        grad_mix_b.reshape(chans),
    )


def power_of_two(count):
    return count & (count - 1) == 0


def body(inputs, grad_out, conv_w, conv_b, mix_w, mix_b, adj_tiles, tile_cols, send_rows, counts):
    tile = adj_tiles.shape[2]
    axes = [lax.axis_size(axis) for axis in ("dp", "space", "tm")]
    fits = (
        axes[1] == 2
        and axes[0] % 2 == 0
        and all(power_of_two(count) for count in axes)
        and inputs.shape[0] == 1
        and inputs.shape[3] == 2 * tile
        and inputs.shape[2] * 2 == tile
        and send_rows.shape[2] * 2 == tile
    )
    chosen = pair_body if fits else general_body
    return chosen(
        inputs, grad_out, conv_w, conv_b, mix_w, mix_b, adj_tiles, tile_cols, send_rows, counts
    )


def solution(mesh):
    in_specs = (
        P("dp", "tm", None, "space"),
        P("dp", "tm", None, "space"),
        P(),
        P(),
        P(),
        P(),
        P("space", None, None, None),
        P("space", None),
        P("space", None, None),
        P("space", None),
    )
    out_specs = (P("dp", "tm", None, "space"), P("dp", "tm", None, "space"), P(), P(), P(), P())
    return jax.shard_map(body, mesh=mesh, in_specs=in_specs, out_specs=out_specs, check_vma=False)
```

```python
import functools
import math

import jax
import jax.numpy as jnp
from jax import lax
from jax.experimental import pallas as pl
from jax.experimental.pallas import tpu as pltpu
from jax.sharding import PartitionSpec as P

DILATION_SIZE = 2


def from_behind(value, axis, steps):
    count = lax.axis_size(axis)
    leading, last = (max(0, -steps), min(count, count - steps))
    return lax.ppermute(value, axis, [(source, source + steps) for source in range(leading, last)])


def slot_mask(counts, slot_count, dtype):
    slots = lax.broadcasted_iota(jnp.int32, (counts.shape[1], slot_count), 1)
    return (slots < counts[0][:, None]).astype(dtype)


def pack_rows(field, send_rows, live_slots):
    picked = field[:, :, send_rows[0]] * live_slots
    return picked.reshape(field.shape[0], field.shape[1], -1)


def tile_product(extended, adj_tiles, tile_cols):
    timestep_count, chan_count = (extended.shape[0], extended.shape[1])
    blocks = extended.reshape(timestep_count, chan_count, -1, adj_tiles.shape[2])
    picked = blocks[:, :, tile_cols]
    return jnp.einsum("tcrkj,rkij->tcri", picked, adj_tiles, preferred_element_type=jnp.float32)


def forward_start(field, send_rows, live_slots):
    packed = pack_rows(field, send_rows, live_slots)
    own_part = None
    return (packed, own_part)


def forward_finish(field, received, adj_tiles, tile_cols):
    total = tile_product(jnp.concatenate([field, received], 2), adj_tiles, tile_cols)
    return total.reshape(field.shape).astype(jnp.bfloat16)


def back_start(grad, adj_tiles, tile_cols, send_rows):
    timestep_count, chan_count, sensor_count = grad.shape
    tile_size = adj_tiles.shape[2]
    row_blocks = sensor_count // tile_size
    half_slots = tile_cols.shape[1] // 2
    halo_blocks = send_rows.shape[1] * send_rows.shape[2] // tile_size
    blocks = grad.reshape(timestep_count, chan_count, row_blocks, tile_size)
    remote_terms = jnp.einsum(
        "tcri,rkij->tcrkj", blocks, adj_tiles[:, half_slots:], preferred_element_type=jnp.float32
    )
    remote_sums = jnp.zeros((timestep_count, chan_count, halo_blocks, tile_size), jnp.float32)
    remote_sums = remote_sums.at[:, :, tile_cols[:, half_slots:] - row_blocks].add(remote_terms)
    return remote_sums.reshape(timestep_count, chan_count, -1).astype(jnp.bfloat16)


def back_finish(grad, returned, adj_tiles, tile_cols, send_rows, live_slots):
    timestep_count, chan_count, sensor_count = grad.shape
    tile_size = adj_tiles.shape[2]
    row_blocks = sensor_count // tile_size
    half_slots = tile_cols.shape[1] // 2
    blocks = grad.reshape(timestep_count, chan_count, row_blocks, tile_size)
    own_terms = jnp.einsum(
        "tcri,rkij->tcrkj", blocks, adj_tiles[:, :half_slots], preferred_element_type=jnp.float32
    )
    total = jnp.zeros((timestep_count, chan_count, row_blocks, tile_size), jnp.float32)
    total = total.at[:, :, tile_cols[:, :half_slots]].add(own_terms).reshape(grad.shape)
    returned = returned.reshape(
        timestep_count, chan_count, send_rows.shape[1], send_rows.shape[2]
    ).astype(jnp.float32)
    return total.at[:, :, send_rows[0]].add(returned * live_slots.astype(jnp.float32))


def mixing_grads(sample_grad, fields):
    grad_mix_w = jnp.stack(
        [
            jnp.einsum("ton,tcn->oc", sample_grad, item, preferred_element_type=jnp.float32)
            for item in fields
        ]
    )
    grad_mix_b = jnp.sum(sample_grad.astype(jnp.float32), axis=(0, 2))
    return (grad_mix_w, grad_mix_b)


def general_body(inputs, grad_out, conv_w, conv_b, mix_w, mix_b, adj_tiles, tile_cols, send_rows, counts):
    sample_input = inputs[0]
    sample_grad = grad_out[0]
    timestep_count, chan_count, sensor_count = sample_input.shape
    live_slots = slot_mask(counts, send_rows.shape[2], jnp.bfloat16)
    prior_border_slice = from_behind(sample_input[timestep_count - DILATION_SIZE :], "tm", 1)
    preceding_window = jnp.concatenate(
        [prior_border_slice, sample_input[: timestep_count - DILATION_SIZE]], 0
    )
    preact = jnp.einsum("oc,tcn->ton", conv_w[1], sample_input, preferred_element_type=jnp.float32)
    preact = preact + jnp.einsum(
        "oc,tcn->ton", conv_w[0], preceding_window, preferred_element_type=jnp.float32
    )
    preact = preact + conv_b[None, :, None]
    filtered = jnp.tanh(preact[:, :chan_count])
    gating = jax.nn.sigmoid(preact[:, chan_count:])
    hidden = (filtered * gating).astype(jnp.bfloat16)
    grad_float = sample_grad.astype(jnp.float32)
    packed_one, early_one = forward_start(hidden, send_rows, live_slots)
    received_one = lax.all_to_all(packed_one, "space", split_axis=2, concat_axis=2, tiled=True)
    hop_one = forward_finish(hidden, received_one, adj_tiles, tile_cols)
    packed_two, early_two = forward_start(hop_one, send_rows, live_slots)
    received_two = lax.all_to_all(packed_two, "space", split_axis=2, concat_axis=2, tiled=True)
    hop_two = forward_finish(hop_one, received_two, adj_tiles, tile_cols)
    fields = (hidden, hop_one, hop_two)
    grad_mix_w, grad_mix_b = mixing_grads(sample_grad, fields)
    back_two = jnp.einsum(
        "oc,ton->tcn", mix_w[2], sample_grad, preferred_element_type=jnp.float32
    ).astype(jnp.bfloat16)
    returned_two = lax.all_to_all(
        back_start(back_two, adj_tiles, tile_cols, send_rows),
        "space",
        split_axis=2,
        concat_axis=2,
        tiled=True,
    )
    back_one = jnp.einsum("oc,ton->tcn", mix_w[1], sample_grad, preferred_element_type=jnp.float32)
    back_one = (
        back_one + back_finish(back_two, returned_two, adj_tiles, tile_cols, send_rows, live_slots)
    ).astype(jnp.bfloat16)
    returned_one = lax.all_to_all(
        back_start(back_one, adj_tiles, tile_cols, send_rows),
        "space",
        split_axis=2,
        concat_axis=2,
        tiled=True,
    )
    back_hidden = jnp.einsum(
        "oc,ton->tcn", mix_w[0], sample_grad, preferred_element_type=jnp.float32
    )
    back_hidden = back_hidden + back_finish(
        back_one, returned_one, adj_tiles, tile_cols, send_rows, live_slots
    )
    mixed = sample_input.astype(jnp.float32) + mix_b[None, :, None]
    for index in range(3):
        mixed = mixed + jnp.einsum(
            "oc,tcn->ton", mix_w[index], fields[index], preferred_element_type=jnp.float32
        )
    outputs = mixed.astype(jnp.bfloat16)[None]
    grad_filter = back_hidden * (1.0 - filtered * filtered) * gating
    grad_gate = back_hidden * filtered * gating * (1.0 - gating)
    backward_preactivation = jnp.concatenate([grad_filter, grad_gate], 1).astype(jnp.bfloat16)
    next_border_slice = from_behind(backward_preactivation[:DILATION_SIZE], "tm", -1)
    following_window = jnp.concatenate(
        [backward_preactivation[DILATION_SIZE:], next_border_slice], 0
    )
    grad_inputs = grad_float + jnp.einsum(
        "oc,ton->tcn", conv_w[1], backward_preactivation, preferred_element_type=jnp.float32
    )
    grad_inputs = grad_inputs + jnp.einsum(
        "oc,ton->tcn", conv_w[0], following_window, preferred_element_type=jnp.float32
    )
    grad_inputs = grad_inputs.astype(jnp.bfloat16)[None]
    grad_conv_w = jnp.stack(
        [
            jnp.einsum(
                "ton,tcn->oc",
                backward_preactivation,
                preceding_window,
                preferred_element_type=jnp.float32,
            ),
            jnp.einsum(
                "ton,tcn->oc",
                backward_preactivation,
                sample_input,
                preferred_element_type=jnp.float32,
            ),
        ]
    )
    grad_conv_b = jnp.sum(backward_preactivation.astype(jnp.float32), axis=(0, 2))
    grad_conv_w, grad_conv_b, grad_mix_w, grad_mix_b = lax.psum(
        (grad_conv_w, grad_conv_b, grad_mix_w, grad_mix_b), ("dp", "space", "tm")
    )
    cell_count = (
        inputs.shape[0]
        * timestep_count
        * sensor_count
        * lax.axis_size("dp")
        * lax.axis_size("space")
        * lax.axis_size("tm")
    )
    scale = 1.0 / math.sqrt(cell_count)
    return (
        outputs,
        grad_inputs,
        grad_conv_w * scale,
        grad_conv_b * scale,
        grad_mix_w * scale,
        grad_mix_b * scale,
    )


BF16 = jnp.bfloat16
F32 = jnp.float32
NT = (((1,), (1,)), ((), ()))
VMEM_BYTES = 24 * 1024 * 1024


def mm(left, right):
    return jnp.dot(left, right, preferred_element_type=F32)


def mm_nt(left, right):
    return lax.dot_general(left, right, NT, preferred_element_type=F32)


def upper_lanes(shape):
    return lax.broadcasted_iota(jnp.int32, shape, 1) >= shape[1] // 2


def halves(matrix):
    upper = upper_lanes(matrix.shape)
    zero = jnp.zeros_like(matrix)
    return jnp.where(upper, zero, matrix), jnp.where(upper, matrix, zero)


def fold(first, second):
    return jnp.where(upper_lanes(first.shape), second, first)


def times_halves(left, right):
    half = left.shape[0] // 2
    return fold(mm(left[:half], right), mm(left[half:], right))


def unfold_nt(folded, right):
    lower, upper = halves(right)
    return jnp.concatenate([mm_nt(folded, lower), mm_nt(folded, upper)], 0)


def link_matrix(packed):
    packed = packed.astype(F32)
    turned = pltpu.roll(packed, packed.shape[1] // 2, 1)
    low, high = halves(packed)
    turned_low, turned_high = halves(turned)
    return jnp.concatenate([low, turned_low, turned_high, high], 0).astype(BF16)


def column(row):
    size = row.shape[1]
    first = lax.broadcasted_iota(jnp.int32, (size, size), 0)
    second = lax.broadcasted_iota(jnp.int32, (size, size), 1)
    return jnp.sum(jnp.where(first == second, row, 0.0), axis=1, keepdims=True)


def fetch(pairs, sems):
    copies = [
        pltpu.make_async_copy(source, target, sems.at[index])
        for index, (source, target) in enumerate(pairs)
    ]
    for copy in copies:
        copy.start()
    return copies


def prepare_kernel(
    cols_hbm,
    counts_hbm,
    rows_hbm,
    adj_hbm,
    grad_hbm,
    input_hbm,
    packed_ref,
    own_ref,
    halo_ref,
    chosen_ref,
    grad_ref,
    tail_ref,
    adj_ref,
    cols_ref,
    counts_ref,
    rows_ref,
    sems,
):
    row_blocks, slots, tile = adj_ref.shape[:3]
    own_slots = slots // 2
    steps = input_hbm.shape[0]
    copies = fetch(
        [
            (adj_hbm.at[:, pl.ds(own_slots, own_slots)], adj_ref.at[:, pl.ds(own_slots, own_slots)]),
            (cols_hbm, cols_ref),
            (counts_hbm, counts_ref),
            (rows_hbm, rows_ref),
            (adj_hbm.at[:, pl.ds(0, own_slots)], adj_ref.at[:, pl.ds(0, own_slots)]),
            (grad_hbm, grad_ref),
            (input_hbm.at[pl.ds(steps - DILATION_SIZE, DILATION_SIZE)], tail_ref),
        ],
        sems,
    )
    other = 1 - lax.axis_index("space")
    sensors = grad_ref.shape[1]
    half_rows = grad_ref.shape[0] // 2
    slot_count = rows_ref.shape[2]
    upper = upper_lanes((tile, tile)).astype(jnp.int32)
    copies[0].wait()
    for r in range(row_blocks):
        far = adj_ref[r, own_slots].astype(F32)
        for k in range(own_slots + 1, slots):
            far = far + adj_ref[r, k].astype(F32)
        far = jnp.where(upper == other, far, pltpu.roll(far, tile // 2, 1))
        halo_ref[r * tile : (r + 1) * tile, :] = far.astype(BF16)
    for copy in copies[1:4]:
        copy.wait()
    rows = rows_ref[0, pl.ds(other, 1), :]
    rows = jnp.concatenate([rows, rows], 1)
    lanes = lax.broadcasted_iota(jnp.int32, (1, 2 * slot_count), 1)
    place = lanes - jnp.where(lanes >= slot_count, slot_count, 0)
    rows = jnp.where(place < counts_ref[0, other], rows, -1)
    sensor = lax.broadcasted_iota(jnp.int32, (sensors, 2 * slot_count), 0)
    chosen = jnp.where(sensor == rows, 1.0, 0.0).astype(F32)
    chosen_ref[...] = chosen.astype(BF16)
    turned = jnp.transpose(chosen)[:slot_count].astype(BF16)
    halo = halo_ref[...]
    packed_ref[2 * half_rows :, :] = times_halves(turned, halo).astype(BF16)
    copies[4].wait()
    for r in range(row_blocks):
        sums = [jnp.zeros((tile, tile), F32), jnp.zeros((tile, tile), F32)]
        for k in range(own_slots):
            item = adj_ref[r, k].astype(F32)
            for block in range(2):
                share = jnp.where(cols_ref[r, k] == block, 1.0, 0.0).astype(F32)
                sums[block] = sums[block] + item * share
        own_ref[r * tile : (r + 1) * tile, :] = jnp.concatenate(sums, 1).astype(BF16)
    copies[5].wait()
    grad = grad_ref[...]
    packed_ref[:half_rows, :] = times_halves(grad, halo).astype(BF16)
    first = mm(grad, own_ref[...]).astype(BF16)
    packed_ref[half_rows : 2 * half_rows, :] = times_halves(first, halo).astype(BF16)
    copies[6].wait()


def gate_step(t, earlier, input_ref, preact, hidden_ref, slopes_ref, right_ref):
    steps, chans, sensors = input_ref.shape
    at = slice(t * chans, (t + 1) * chans)
    span = slice(t * sensors, (t + 1) * sensors)
    filtered = jnp.tanh(preact[:chans])
    gating = 0.5 * jnp.tanh(0.5 * preact[chans:]) + 0.5
    product = filtered * gating
    hidden = product.astype(BF16)
    hidden_ref[at, :] = hidden
    slopes_ref[t, :chans] = (1.0 - filtered * filtered) * gating
    slopes_ref[t, chans:] = product * (1.0 - gating)
    right_ref[:chans, span] = earlier
    right_ref[chans : 2 * chans, span] = input_ref[t]
    right_ref[2 * chans : 2 * chans + 16, span] = jnp.ones((16, sensors), BF16)
    right_ref[2 * chans + 16 : 3 * chans + 16, span] = hidden
    right_ref[3 * chans + 16 :, span] = hidden


def forward_kernel(
    input_hbm,
    conv_w_hbm,
    conv_b_hbm,
    mix_w_hbm,
    mix_b_hbm,
    grad_ref,
    own_ref,
    hidden_ref,
    slopes_ref,
    right_ref,
    near_ref,
    input_ref,
    taps_ref,
    turned_taps_ref,
    bias_ref,
    mix_ref,
    mixing_ref,
    mix_bias_ref,
    sems,
):
    copies = fetch(
        [
            (input_hbm, input_ref),
            (conv_w_hbm, taps_ref),
            (conv_b_hbm, bias_ref),
            (mix_w_hbm, mix_ref),
            (mix_b_hbm, mix_bias_ref),
        ],
        sems,
    )
    steps, chans, sensors = input_ref.shape
    near_ref[...] = mm(grad_ref[...], own_ref[...])
    for copy in copies:
        copy.wait()
    mixing = jnp.transpose(mix_ref[...].reshape(3 * chans, chans).astype(F32))
    mixing_ref[...] = mixing.astype(BF16)
    taps = taps_ref[...].reshape(2 * chans, 2 * chans).astype(F32)
    taps = jnp.transpose(taps).astype(BF16)
    turned_taps_ref[...] = taps
    bias = column(bias_ref[...])
    for t in range(DILATION_SIZE, steps):
        earlier = input_ref[t - DILATION_SIZE]
        preact = mm(taps, jnp.concatenate([earlier, input_ref[t]], 0)) + bias
        gate_step(t, earlier, input_ref, preact, hidden_ref, slopes_ref, right_ref)


def backward_kernel(
    grad_ref,
    own_packed_ref,
    packed_ref,
    border_ref,
    own_ref,
    chosen_ref,
    near_ref,
    input_ref,
    taps_ref,
    turned_taps_ref,
    bias_ref,
    mixing_ref,
    hidden_old_ref,
    slopes_old_ref,
    right_old_ref,
    kept_ref,
    given_ref,
    back_ref,
    early_ref,
    hidden_ref,
    left_scr,
    one_scr,
    two_scr,
    slopes_ref,
    right_ref,
):
    steps, wide, sensors = back_ref.shape
    chans = wide // 2
    rows = steps * chans
    half_rows = rows // 2
    border_rows = DILATION_SIZE * chans
    border_span = DILATION_SIZE * sensors
    core = lax.axis_index("dp") % 2
    own = own_ref[...]
    chosen = chosen_ref[...]
    link = link_matrix(packed_ref[rows:, :])
    one = (near_ref[...] + unfold_nt(packed_ref[:half_rows, :], chosen)).astype(BF16)
    second = packed_ref[half_rows:rows, :].astype(F32) + mm(own_packed_ref[:half_rows, :], link)
    two = (mm(one, own) + unfold_nt(second.astype(BF16), chosen)).astype(BF16)
    one_scr[...] = one
    two_scr[...] = two
    bias = column(bias_ref[...])
    has_earlier = lax.axis_index("tm") > 0
    hidden_ref[border_rows:, :] = hidden_old_ref[border_rows:, :]
    for t in range(DILATION_SIZE):
        earlier = border_ref[t]
        earlier = jnp.where(has_earlier, earlier, jnp.zeros_like(earlier))
        window = jnp.concatenate([earlier, input_ref[t]], 0)
        preact = mm(turned_taps_ref[...], window) + bias
        gate_step(t, earlier, input_ref, preact, hidden_ref, slopes_ref, right_ref)
    mixing = mixing_ref[...]
    for t in range(steps):
        at = slice(t * chans, (t + 1) * chans)
        span = slice(t * sensors, (t + 1) * sensors)
        fields = jnp.concatenate([grad_ref[at, :], one_scr[at, :], two_scr[at, :]], 0)
        back_hidden = mm(mixing, fields)
        back_hidden = jnp.concatenate([back_hidden, back_hidden], 0)
        slopes = slopes_ref[t] if t < DILATION_SIZE else slopes_old_ref[t]
        back_pre = (back_hidden * slopes).astype(BF16)
        back_ref[t] = back_pre
        left_scr[:wide, span] = back_pre
        left_scr[wide:, span] = fields
        if t < DILATION_SIZE:
            early_ref[t] = mm(taps_ref[0], back_pre).astype(BF16)
    ones = wide + 16
    conv = mm_nt(right_old_ref[:ones, border_span:], left_scr[: wide + chans, border_span:])
    conv = conv + mm_nt(right_ref[:ones, :], left_scr[: wide + chans, :border_span])
    mixes = mm_nt(left_scr[wide:, border_span:], right_old_ref[ones:, border_span:])
    mixes = mixes + mm_nt(left_scr[wide:, :border_span], right_ref[ones:, :])
    sums = conv[wide : wide + 8]
    conv = conv[:wide, :wide]
    zero, first, second = [mixes[k * chans : (k + 1) * chans] for k in range(3)]
    tail = jnp.concatenate([sums[:, wide:], jnp.zeros((8, chans), F32)], 1)
    biases = jnp.concatenate(
        [
            pltpu.roll(tail, chans, 1),
            pltpu.roll(sums[:, :wide], chans, 1),
            sums[:, :wide],
            jnp.zeros((chans - 24, wide), F32),
        ],
        0,
    )
    mixes = jnp.concatenate([fold(zero, first), fold(second, biases)], 0)
    kept_ref[...] = jnp.where(core == 0, conv, mixes)
    given_ref[...] = jnp.where(core == 0, mixes, conv)


def boundary_kernel(hidden_ref, own_ref, chosen_ref, boundary_ref):
    hidden = hidden_ref[...]
    chosen = chosen_ref[...]
    hop = mm_nt(hidden, own_ref[...]).astype(BF16)
    half_rows = hidden.shape[0] // 2
    boundary_ref[:half_rows, :] = times_halves(hidden, chosen).astype(BF16)
    boundary_ref[half_rows:, :] = times_halves(hop, chosen).astype(BF16)


def outputs_kernel(
    input_ref,
    hidden_ref,
    own_boundary_ref,
    boundary_ref,
    packed_ref,
    own_ref,
    halo_ref,
    mix_ref,
    bias_ref,
    out_ref,
):
    steps, chans, sensors = input_ref.shape
    rows = steps * chans
    half_rows = rows // 2
    own = own_ref[...]
    halo = halo_ref[...]
    link = link_matrix(packed_ref[rows:, :])
    hidden = hidden_ref[...]
    one = (mm_nt(hidden, own) + unfold_nt(boundary_ref[:half_rows, :], halo)).astype(BF16)
    far = boundary_ref[half_rows:, :].astype(F32) + mm_nt(own_boundary_ref[:half_rows, :], link)
    two = (mm_nt(one, own) + unfold_nt(far.astype(BF16), halo)).astype(BF16)
    bias = column(bias_ref[...])
    for t in range(steps):
        at = slice(t * chans, (t + 1) * chans)
        mixed = mm(mix_ref[0], hidden[at]) + mm(mix_ref[1], one[at]) + mm(mix_ref[2], two[at])
        out_ref[t] = (mixed + bias + input_ref[t].astype(F32)).astype(BF16)


def input_grad_kernel(grad_ref, back_ref, early_ref, taps_ref, out_ref):
    steps, chans, sensors = out_ref.shape
    has_later = lax.axis_index("tm") < lax.axis_size("tm") - 1
    taps = jnp.concatenate([taps_ref[0], taps_ref[1]], 1)
    for t in range(steps):
        at = slice(t * chans, (t + 1) * chans)
        later = t + DILATION_SIZE
        total = grad_ref[at, :].astype(F32)
        if later < steps:
            total = total + mm(taps, jnp.concatenate([back_ref[later], back_ref[t]], 0))
        else:
            early = early_ref[later - steps].astype(F32)
            early = jnp.where(has_later, early, jnp.zeros_like(early))
            total = total + mm(taps_ref[1], back_ref[t]) + early
        out_ref[t] = total.astype(BF16)


def final_kernel(scale, kept_ref, other_ref, conv_w_ref, conv_b_ref, mix_w_ref, mix_b_ref):
    core = lax.axis_index("dp") % 2
    kept = kept_ref[...] * scale
    other = other_ref[...] * scale
    conv = jnp.where(core == 0, kept, other)
    mixes = jnp.where(core == 0, other, kept)
    chans = conv.shape[1] // 2
    conv_w_ref[0] = conv[:chans]
    conv_w_ref[1] = conv[chans:]
    mix_w_ref[0] = mixes[:chans, :chans]
    mix_w_ref[1] = pltpu.roll(mixes[:chans], chans, 1)[:, :chans]
    mix_w_ref[2] = mixes[chans:, :chans]
    biases = mixes[chans : chans + 24]
    turned = pltpu.roll(biases, chans, 1)
    mix_b_ref[...] = turned[0:1, :chans]
    conv_b_ref[...] = fold(turned[8:9], biases[16:17])


VMEM = pl.BlockSpec(memory_space=pltpu.VMEM)
HBM = pl.BlockSpec(memory_space=pltpu.HBM)
DMA = pltpu.SemaphoreType.DMA


def call(kernel, name, in_specs, out_shape, args, scratch=(), micros=1.0):
    args = [
        pltpu.with_memory_space_constraint(arg, pltpu.HBM) if spec is HBM else arg
        for spec, arg in zip(in_specs, args)
    ]
    return pl.pallas_call(
        kernel,
        out_shape=out_shape,
        in_specs=in_specs,
        out_specs=jax.tree.map(lambda _: VMEM, out_shape),
        scratch_shapes=list(scratch),
        compiler_params=pltpu.CompilerParams(vmem_limit_bytes=VMEM_BYTES),
        cost_estimate=pl.CostEstimate(
            flops=0, bytes_accessed=int(micros * 3_600_000), transcendentals=0
        ),
        name=name,
    )(*args)


def swap(value, axis, bit):
    count = lax.axis_size(axis)
    return lax.ppermute(value, axis, [(source, source ^ bit) for source in range(count)])


def shift(value, axis, steps):
    count = lax.axis_size(axis)
    return lax.ppermute(value, axis, [(source, (source + steps) % count) for source in range(count)])


def bits(count):
    return [1 << place for place in range(count.bit_length() - 1)]


def after(value, *earlier):
    return lax.optimization_barrier((value, *earlier))[0]


def pair_body(inputs, grad_out, conv_w, conv_b, mix_w, mix_b, adj_tiles, tile_cols, send_rows, counts):
    sample_input = inputs[0]
    sample_grad = grad_out[0]
    steps, chans, sensors = sample_input.shape
    rows = steps * chans
    half_rows = rows // 2
    wide = 2 * chans
    shape = jax.ShapeDtypeStruct
    grad_flat = sample_grad.reshape(rows, sensors)
    taps = jnp.transpose(conv_w, (0, 2, 1))
    packed, own, halo, chosen, grad, tail = call(
        prepare_kernel,
        "prepare",
        [HBM] * 6,
        (
            shape((rows + chans // 2, wide), BF16),
            shape((sensors, sensors), BF16),
            shape((sensors, wide), BF16),
            shape((sensors, wide), BF16),
            shape((rows, sensors), BF16),
            shape((DILATION_SIZE, chans, sensors), BF16),
        ),
        (tile_cols, counts, send_rows, adj_tiles, grad_flat, sample_input),
        scratch=(
            pltpu.VMEM(adj_tiles.shape, BF16),
            pltpu.SMEM(tile_cols.shape, jnp.int32),
            pltpu.SMEM(counts.shape, jnp.int32),
            pltpu.VMEM(send_rows.shape, jnp.int32),
            DMA((7,)),
        ),
        micros=2.0,
    )
    packed_far = swap(packed, "space", 1)
    border = from_behind(tail, "tm", 1)
    hidden_late, slopes, right, near, kept_input, kept_taps, turned_taps, bias, mix, mixing, mix_bias = call(
        forward_kernel,
        "forward",
        [HBM] * 5 + [VMEM] * 2,
        (
            shape((rows, sensors), BF16),
            shape((steps, wide, sensors), F32),
            shape((2 * wide + 16, steps * sensors), BF16),
            shape((rows, sensors), F32),
            shape(sample_input.shape, BF16),
            shape(taps.shape, BF16),
            shape((wide, wide), BF16),
            shape((1, wide), F32),
            shape(mix_w.shape, BF16),
            shape((chans, 3 * chans), BF16),
            shape((1, chans), F32),
        ),
        (
            sample_input,
            taps,
            conv_b.reshape(1, wide),
            mix_w,
            mix_b.reshape(1, chans),
            grad,
            own,
        ),
        scratch=(DMA((5,)),),
        micros=1.5,
    )
    border_span = DILATION_SIZE * sensors
    kept, given, back, early, hidden = call(
        backward_kernel,
        "backward",
        [VMEM] * 15,
        (
            shape((wide, wide), F32),
            shape((wide, wide), F32),
            shape((steps, wide, sensors), BF16),
            shape((DILATION_SIZE, chans, sensors), BF16),
            shape((rows, sensors), BF16),
        ),
        (
            grad,
            packed,
            packed_far,
            border,
            own,
            chosen,
            near,
            kept_input,
            kept_taps,
            turned_taps,
            bias,
            mixing,
            hidden_late,
            slopes,
            right,
        ),
        scratch=(
            pltpu.VMEM((wide + 3 * chans, steps * sensors), BF16),
            pltpu.VMEM((rows, sensors), BF16),
            pltpu.VMEM((rows, sensors), BF16),
            pltpu.VMEM((DILATION_SIZE, wide, sensors), F32),
            pltpu.VMEM((2 * wide + 16, border_span), BF16),
        ),
        micros=2.0,
    )
    total = kept + swap(given, "dp", 1)
    rounds = (
        [("dp", bit) for bit in bits(lax.axis_size("dp"))[1:]]
        + [("space", bit) for bit in bits(lax.axis_size("space"))]
        + [("tm", bit) for bit in bits(lax.axis_size("tm"))]
    )
    early_far = shift(early, "tm", -1)
    for index, (axis, bit) in enumerate(rounds):
        if index == 2:
            boundary = call(
                boundary_kernel,
                "boundary",
                [VMEM] * 3,
                shape((rows, wide), BF16),
                (after(hidden, total), own, chosen),
                micros=0.4,
            )
            boundary_far = swap(boundary, "space", 1)
        arrived = swap(total, axis, bit)
        if index == 2:
            grad_inputs = call(
                input_grad_kernel,
                "input_grad",
                [VMEM] * 4,
                shape(sample_grad.shape, BF16),
                (grad, back, early_far, kept_taps),
                micros=1.2,
            )
            arrived = after(arrived, grad_inputs)
        if index == 3:
            outputs = call(
                outputs_kernel,
                "outputs",
                [VMEM] * 9,
                shape(sample_input.shape, BF16),
                (kept_input, hidden, boundary, boundary_far, packed_far, own, halo, mix, mix_bias),
                micros=2.0,
            )
            arrived = after(arrived, outputs)
        total = total + arrived
    total_far = swap(total, "dp", 1)
    cell_count = (
        inputs.shape[0]
        * steps
        * sensors
        * lax.axis_size("dp")
        * lax.axis_size("space")
        * lax.axis_size("tm")
    )
    scale = 1.0 / math.sqrt(cell_count)
    grad_taps, grad_conv_b, grad_mix_w, grad_mix_b = call(
        functools.partial(final_kernel, scale),
        "final",
        [VMEM] * 2,
        (
            shape((2, chans, wide), F32),
            shape((1, wide), F32),
            shape((3, chans, chans), F32),
            shape((1, chans), F32),
        ),
        (total, total_far),
    )
    return (
        outputs[None],
        grad_inputs[None],
        jnp.transpose(grad_taps, (0, 2, 1)),
        grad_conv_b.reshape(wide),
        grad_mix_w,
        grad_mix_b.reshape(chans),
    )


def power_of_two(count):
    return count & (count - 1) == 0


def body(inputs, grad_out, conv_w, conv_b, mix_w, mix_b, adj_tiles, tile_cols, send_rows, counts):
    tile = adj_tiles.shape[2]
    axes = [lax.axis_size(axis) for axis in ("dp", "space", "tm")]
    fits = (
        axes[1] == 2
        and axes[0] % 2 == 0
        and all(power_of_two(count) for count in axes)
        and inputs.shape[0] == 1
        and inputs.shape[3] == 2 * tile
        and inputs.shape[2] * 2 == tile
        and send_rows.shape[2] * 2 == tile
    )
    chosen = pair_body if fits else general_body
    return chosen(
        inputs, grad_out, conv_w, conv_b, mix_w, mix_b, adj_tiles, tile_cols, send_rows, counts
    )


def solution(mesh):
    in_specs = (
        P("dp", "tm", None, "space"),
        P("dp", "tm", None, "space"),
        P(),
        P(),
        P(),
        P(),
        P("space", None, None, None),
        P("space", None),
        P("space", None, None),
        P("space", None),
    )
    out_specs = (P("dp", "tm", None, "space"), P("dp", "tm", None, "space"), P(), P(), P(), P())
    return jax.shard_map(body, mesh=mesh, in_specs=in_specs, out_specs=out_specs, check_vma=False)
```

```python
import functools
import itertools
import math

import jax
import jax.numpy as jnp
from jax import lax
from jax.experimental import pallas as pl
from jax.experimental.pallas import tpu as pltpu
from jax.sharding import PartitionSpec as P

DILATION_SIZE = 2


def from_behind(value, axis, steps):
    count = lax.axis_size(axis)
    leading, last = (max(0, -steps), min(count, count - steps))
    return lax.ppermute(value, axis, [(source, source + steps) for source in range(leading, last)])


def slot_mask(counts, slot_count, dtype):
    slots = lax.broadcasted_iota(jnp.int32, (counts.shape[1], slot_count), 1)
    return (slots < counts[0][:, None]).astype(dtype)


def pack_rows(field, send_rows, live_slots):
    picked = field[:, :, send_rows[0]] * live_slots
    return picked.reshape(field.shape[0], field.shape[1], -1)


def tile_product(extended, adj_tiles, tile_cols):
    timestep_count, chan_count = (extended.shape[0], extended.shape[1])
    blocks = extended.reshape(timestep_count, chan_count, -1, adj_tiles.shape[2])
    picked = blocks[:, :, tile_cols]
    return jnp.einsum("tcrkj,rkij->tcri", picked, adj_tiles, preferred_element_type=jnp.float32)


def forward_start(field, send_rows, live_slots):
    packed = pack_rows(field, send_rows, live_slots)
    own_part = None
    return (packed, own_part)


def forward_finish(field, received, adj_tiles, tile_cols):
    total = tile_product(jnp.concatenate([field, received], 2), adj_tiles, tile_cols)
    return total.reshape(field.shape).astype(jnp.bfloat16)


def back_start(grad, adj_tiles, tile_cols, send_rows):
    timestep_count, chan_count, sensor_count = grad.shape
    tile_size = adj_tiles.shape[2]
    row_blocks = sensor_count // tile_size
    half_slots = tile_cols.shape[1] // 2
    halo_blocks = send_rows.shape[1] * send_rows.shape[2] // tile_size
    blocks = grad.reshape(timestep_count, chan_count, row_blocks, tile_size)
    remote_terms = jnp.einsum(
        "tcri,rkij->tcrkj", blocks, adj_tiles[:, half_slots:], preferred_element_type=jnp.float32
    )
    remote_sums = jnp.zeros((timestep_count, chan_count, halo_blocks, tile_size), jnp.float32)
    remote_sums = remote_sums.at[:, :, tile_cols[:, half_slots:] - row_blocks].add(remote_terms)
    return remote_sums.reshape(timestep_count, chan_count, -1).astype(jnp.bfloat16)


def back_finish(grad, returned, adj_tiles, tile_cols, send_rows, live_slots):
    timestep_count, chan_count, sensor_count = grad.shape
    tile_size = adj_tiles.shape[2]
    row_blocks = sensor_count // tile_size
    half_slots = tile_cols.shape[1] // 2
    blocks = grad.reshape(timestep_count, chan_count, row_blocks, tile_size)
    own_terms = jnp.einsum(
        "tcri,rkij->tcrkj", blocks, adj_tiles[:, :half_slots], preferred_element_type=jnp.float32
    )
    total = jnp.zeros((timestep_count, chan_count, row_blocks, tile_size), jnp.float32)
    total = total.at[:, :, tile_cols[:, :half_slots]].add(own_terms).reshape(grad.shape)
    returned = returned.reshape(
        timestep_count, chan_count, send_rows.shape[1], send_rows.shape[2]
    ).astype(jnp.float32)
    return total.at[:, :, send_rows[0]].add(returned * live_slots.astype(jnp.float32))


def mixing_grads(sample_grad, fields):
    grad_mix_w = jnp.stack(
        [
            jnp.einsum("ton,tcn->oc", sample_grad, item, preferred_element_type=jnp.float32)
            for item in fields
        ]
    )
    grad_mix_b = jnp.sum(sample_grad.astype(jnp.float32), axis=(0, 2))
    return (grad_mix_w, grad_mix_b)


def general_body(inputs, grad_out, conv_w, conv_b, mix_w, mix_b, adj_tiles, tile_cols, send_rows, counts):
    sample_input = inputs[0]
    sample_grad = grad_out[0]
    timestep_count, chan_count, sensor_count = sample_input.shape
    live_slots = slot_mask(counts, send_rows.shape[2], jnp.bfloat16)
    prior_border_slice = from_behind(sample_input[timestep_count - DILATION_SIZE :], "tm", 1)
    preceding_window = jnp.concatenate(
        [prior_border_slice, sample_input[: timestep_count - DILATION_SIZE]], 0
    )
    preact = jnp.einsum("oc,tcn->ton", conv_w[1], sample_input, preferred_element_type=jnp.float32)
    preact = preact + jnp.einsum(
        "oc,tcn->ton", conv_w[0], preceding_window, preferred_element_type=jnp.float32
    )
    preact = preact + conv_b[None, :, None]
    filtered = jnp.tanh(preact[:, :chan_count])
    gating = jax.nn.sigmoid(preact[:, chan_count:])
    hidden = (filtered * gating).astype(jnp.bfloat16)
    grad_float = sample_grad.astype(jnp.float32)
    packed_one, early_one = forward_start(hidden, send_rows, live_slots)
    received_one = lax.all_to_all(packed_one, "space", split_axis=2, concat_axis=2, tiled=True)
    hop_one = forward_finish(hidden, received_one, adj_tiles, tile_cols)
    packed_two, early_two = forward_start(hop_one, send_rows, live_slots)
    received_two = lax.all_to_all(packed_two, "space", split_axis=2, concat_axis=2, tiled=True)
    hop_two = forward_finish(hop_one, received_two, adj_tiles, tile_cols)
    fields = (hidden, hop_one, hop_two)
    grad_mix_w, grad_mix_b = mixing_grads(sample_grad, fields)
    back_two = jnp.einsum(
        "oc,ton->tcn", mix_w[2], sample_grad, preferred_element_type=jnp.float32
    ).astype(jnp.bfloat16)
    returned_two = lax.all_to_all(
        back_start(back_two, adj_tiles, tile_cols, send_rows),
        "space",
        split_axis=2,
        concat_axis=2,
        tiled=True,
    )
    back_one = jnp.einsum("oc,ton->tcn", mix_w[1], sample_grad, preferred_element_type=jnp.float32)
    back_one = (
        back_one + back_finish(back_two, returned_two, adj_tiles, tile_cols, send_rows, live_slots)
    ).astype(jnp.bfloat16)
    returned_one = lax.all_to_all(
        back_start(back_one, adj_tiles, tile_cols, send_rows),
        "space",
        split_axis=2,
        concat_axis=2,
        tiled=True,
    )
    back_hidden = jnp.einsum(
        "oc,ton->tcn", mix_w[0], sample_grad, preferred_element_type=jnp.float32
    )
    back_hidden = back_hidden + back_finish(
        back_one, returned_one, adj_tiles, tile_cols, send_rows, live_slots
    )
    mixed = sample_input.astype(jnp.float32) + mix_b[None, :, None]
    for index in range(3):
        mixed = mixed + jnp.einsum(
            "oc,tcn->ton", mix_w[index], fields[index], preferred_element_type=jnp.float32
        )
    outputs = mixed.astype(jnp.bfloat16)[None]
    grad_filter = back_hidden * (1.0 - filtered * filtered) * gating
    grad_gate = back_hidden * filtered * gating * (1.0 - gating)
    backward_preactivation = jnp.concatenate([grad_filter, grad_gate], 1).astype(jnp.bfloat16)
    next_border_slice = from_behind(backward_preactivation[:DILATION_SIZE], "tm", -1)
    following_window = jnp.concatenate(
        [backward_preactivation[DILATION_SIZE:], next_border_slice], 0
    )
    grad_inputs = grad_float + jnp.einsum(
        "oc,ton->tcn", conv_w[1], backward_preactivation, preferred_element_type=jnp.float32
    )
    grad_inputs = grad_inputs + jnp.einsum(
        "oc,ton->tcn", conv_w[0], following_window, preferred_element_type=jnp.float32
    )
    grad_inputs = grad_inputs.astype(jnp.bfloat16)[None]
    grad_conv_w = jnp.stack(
        [
            jnp.einsum(
                "ton,tcn->oc",
                backward_preactivation,
                preceding_window,
                preferred_element_type=jnp.float32,
            ),
            jnp.einsum(
                "ton,tcn->oc",
                backward_preactivation,
                sample_input,
                preferred_element_type=jnp.float32,
            ),
        ]
    )
    grad_conv_b = jnp.sum(backward_preactivation.astype(jnp.float32), axis=(0, 2))
    grad_conv_w, grad_conv_b, grad_mix_w, grad_mix_b = lax.psum(
        (grad_conv_w, grad_conv_b, grad_mix_w, grad_mix_b), ("dp", "space", "tm")
    )
    cell_count = (
        inputs.shape[0]
        * timestep_count
        * sensor_count
        * lax.axis_size("dp")
        * lax.axis_size("space")
        * lax.axis_size("tm")
    )
    scale = 1.0 / math.sqrt(cell_count)
    return (
        outputs,
        grad_inputs,
        grad_conv_w * scale,
        grad_conv_b * scale,
        grad_mix_w * scale,
        grad_mix_b * scale,
    )


BF16 = jnp.bfloat16
AXES = ("dp", "space", "tm")
F32 = jnp.float32
NT = (((1,), (1,)), ((), ()))
VMEM_BYTES = 24 * 1024 * 1024


def mm(left, right):
    return jnp.dot(left, right, preferred_element_type=F32)


def mm_nt(left, right):
    return lax.dot_general(left, right, NT, preferred_element_type=F32)


def upper_lanes(shape):
    return lax.broadcasted_iota(jnp.int32, shape, 1) >= shape[1] // 2


def halves(matrix):
    upper = upper_lanes(matrix.shape)
    zero = jnp.zeros_like(matrix)
    return jnp.where(upper, zero, matrix), jnp.where(upper, matrix, zero)


def fold(first, second):
    return jnp.where(upper_lanes(first.shape), second, first)


def times_halves(left, right):
    half = left.shape[0] // 2
    return fold(mm(left[:half], right), mm(left[half:], right))


def link_matrix(packed):
    packed = packed.astype(F32)
    turned = pltpu.roll(packed, packed.shape[1] // 2, 1)
    blank = jnp.zeros_like(packed)
    return jnp.concatenate([halves(turned)[1], halves(packed)[1], blank, blank], 0).astype(BF16)


def turned_link_matrix(packed):
    packed = packed.astype(F32)
    turned = pltpu.roll(packed, packed.shape[1] // 2, 1)
    blank = jnp.zeros_like(packed)
    return jnp.concatenate([blank, blank, halves(packed)[0], halves(turned)[0]], 0).astype(BF16)


def column(row):
    size = row.shape[1]
    first = lax.broadcasted_iota(jnp.int32, (size, size), 0)
    second = lax.broadcasted_iota(jnp.int32, (size, size), 1)
    return jnp.sum(jnp.where(first == second, row, 0.0), axis=1, keepdims=True)


def fetch(pairs, sems):
    copies = [
        pltpu.make_async_copy(source, target, sems.at[index])
        for index, (source, target) in enumerate(pairs)
    ]
    for copy in copies:
        copy.start()
    return copies


def prepare_kernel(
    cols_hbm,
    counts_hbm,
    rows_hbm,
    adj_hbm,
    grad_hbm,
    input_hbm,
    packed_ref,
    own_ref,
    halo_ref,
    chosen_ref,
    grad_ref,
    tail_ref,
    adj_ref,
    cols_ref,
    counts_ref,
    rows_ref,
    sems,
):
    row_blocks, slots, tile = adj_ref.shape[:3]
    own_slots = slots // 2
    steps = input_hbm.shape[0]
    copies = fetch(
        [
            (adj_hbm.at[:, pl.ds(own_slots, own_slots)], adj_ref.at[:, pl.ds(own_slots, own_slots)]),
            (cols_hbm, cols_ref),
            (counts_hbm, counts_ref),
            (rows_hbm, rows_ref),
            (adj_hbm.at[:, pl.ds(0, own_slots)], adj_ref.at[:, pl.ds(0, own_slots)]),
            (grad_hbm, grad_ref),
            (input_hbm.at[pl.ds(steps - DILATION_SIZE, DILATION_SIZE)], tail_ref),
        ],
        sems,
    )
    other = 1 - lax.axis_index("space")
    sensors = grad_ref.shape[1]
    rows_count = grad_ref.shape[0]
    slot_count = rows_ref.shape[2]
    upper = upper_lanes((tile, tile)).astype(jnp.int32)
    copies[0].wait()
    for r in range(row_blocks):
        far = adj_ref[r, own_slots].astype(F32)
        for k in range(own_slots + 1, slots):
            far = far + adj_ref[r, k].astype(F32)
        far = jnp.where(upper == other, far, pltpu.roll(far, tile // 2, 1))
        halo_ref[r * tile : (r + 1) * tile, :] = far.astype(BF16)
    for copy in copies[1:4]:
        copy.wait()
    rows = rows_ref[0, pl.ds(other, 1), :]
    rows = jnp.concatenate([rows, rows], 1)
    lanes = lax.broadcasted_iota(jnp.int32, (1, 2 * slot_count), 1)
    place = lanes - jnp.where(lanes >= slot_count, slot_count, 0)
    rows = jnp.where(place < counts_ref[0, other], rows, -1)
    sensor = lax.broadcasted_iota(jnp.int32, (sensors, 2 * slot_count), 0)
    chosen = jnp.where(sensor == rows, 1.0, 0.0).astype(F32)
    chosen_ref[...] = chosen.astype(BF16)
    turned = jnp.transpose(chosen)[:slot_count].astype(BF16)
    halo = halo_ref[...]
    packed_ref[rows_count:, :] = times_halves(turned, halo).astype(BF16)
    copies[4].wait()
    for r in range(row_blocks):
        sums = [jnp.zeros((tile, tile), F32), jnp.zeros((tile, tile), F32)]
        for k in range(own_slots):
            item = adj_ref[r, k].astype(F32)
            for block in range(2):
                share = jnp.where(cols_ref[r, k] == block, 1.0, 0.0).astype(F32)
                sums[block] = sums[block] + item * share
        own_ref[r * tile : (r + 1) * tile, :] = jnp.concatenate(sums, 1).astype(BF16)
    both = fold(halo, mm(own_ref[...], halo).astype(BF16))
    copies[5].wait()
    packed_ref[:rows_count, :] = mm(grad_ref[...], both).astype(BF16)
    copies[6].wait()


def gate_step(t, earlier, input_ref, preact, hidden_ref, slopes_ref, right_ref):
    steps, chans, sensors = input_ref.shape
    at = slice(t * chans, (t + 1) * chans)
    span = slice(t * sensors, (t + 1) * sensors)
    filtered = jnp.tanh(preact[:chans])
    gating = 0.5 * jnp.tanh(0.5 * preact[chans:]) + 0.5
    product = filtered * gating
    hidden = product.astype(BF16)
    hidden_ref[at, :] = hidden
    slopes_ref[t, :chans] = (1.0 - filtered * filtered) * gating
    slopes_ref[t, chans:] = product * (1.0 - gating)
    right_ref[:chans, span] = earlier
    right_ref[chans : 2 * chans, span] = input_ref[t]
    right_ref[2 * chans : 2 * chans + 16, span] = jnp.ones((16, sensors), BF16)
    right_ref[2 * chans + 16 : 3 * chans + 16, span] = hidden
    right_ref[3 * chans + 16 :, span] = hidden


def forward_kernel(
    input_hbm,
    conv_w_hbm,
    conv_b_hbm,
    mix_w_hbm,
    mix_b_hbm,
    grad_ref,
    own_ref,
    hidden_ref,
    slopes_ref,
    right_ref,
    near_ref,
    input_ref,
    taps_ref,
    turned_taps_ref,
    bias_ref,
    mix_ref,
    mixing_ref,
    mix_bias_ref,
    sems,
):
    copies = fetch(
        [
            (input_hbm, input_ref),
            (conv_w_hbm, taps_ref),
            (conv_b_hbm, bias_ref),
            (mix_w_hbm, mix_ref),
            (mix_b_hbm, mix_bias_ref),
        ],
        sems,
    )
    steps, chans, sensors = input_ref.shape
    near_ref[...] = mm(grad_ref[...], own_ref[...])
    for copy in copies:
        copy.wait()
    mixing = jnp.transpose(mix_ref[...].reshape(3 * chans, chans).astype(F32))
    mixing_ref[...] = mixing.astype(BF16)
    taps = taps_ref[...].reshape(2 * chans, 2 * chans).astype(F32)
    taps = jnp.transpose(taps).astype(BF16)
    turned_taps_ref[...] = taps
    bias = column(bias_ref[...])
    for t in range(DILATION_SIZE, steps):
        earlier = input_ref[t - DILATION_SIZE]
        preact = mm(taps, jnp.concatenate([earlier, input_ref[t]], 0)) + bias
        gate_step(t, earlier, input_ref, preact, hidden_ref, slopes_ref, right_ref)


def backward_kernel(
    grad_ref,
    own_packed_ref,
    packed_ref,
    border_ref,
    own_ref,
    chosen_ref,
    near_ref,
    input_ref,
    taps_ref,
    turned_taps_ref,
    bias_ref,
    mixing_ref,
    hidden_old_ref,
    slopes_old_ref,
    right_old_ref,
    kept_ref,
    given_ref,
    back_ref,
    early_ref,
    hidden_ref,
    left_scr,
    one_scr,
    two_scr,
    slopes_ref,
    right_ref,
):
    steps, wide, sensors = back_ref.shape
    chans = wide // 2
    rows = steps * chans
    border_rows = DILATION_SIZE * chans
    border_span = DILATION_SIZE * sensors
    core = lax.axis_index("dp") % 2
    own = own_ref[...]
    chosen = chosen_ref[...]
    chosen_low, chosen_high = halves(chosen)
    packed = packed_ref[:rows, :]
    one = (near_ref[...] + mm_nt(packed, chosen_low)).astype(BF16)
    second = packed.astype(F32) + mm(own_packed_ref[:rows, :], link_matrix(packed_ref[rows:, :]))
    two = (mm(one, own) + mm_nt(second.astype(BF16), chosen_high)).astype(BF16)
    one_scr[...] = one
    two_scr[...] = two
    bias = column(bias_ref[...])
    place = lax.axis_index("tm")
    hidden_ref[border_rows:, :] = hidden_old_ref[border_rows:, :]
    for t in range(DILATION_SIZE):
        earlier = border_ref[t]
        earlier = jnp.where(place > 0, earlier, jnp.zeros_like(earlier))
        window = jnp.concatenate([earlier, input_ref[t]], 0)
        preact = mm(turned_taps_ref[...], window) + bias
        gate_step(t, earlier, input_ref, preact, hidden_ref, slopes_ref, right_ref)
    mixing = mixing_ref[...]
    for t in range(steps):
        at = slice(t * chans, (t + 1) * chans)
        span = slice(t * sensors, (t + 1) * sensors)
        fields = jnp.concatenate([grad_ref[at, :], one_scr[at, :], two_scr[at, :]], 0)
        back_hidden = mm(mixing, fields)
        back_hidden = jnp.concatenate([back_hidden, back_hidden], 0)
        slopes = slopes_ref[t] if t < DILATION_SIZE else slopes_old_ref[t]
        back_pre = (back_hidden * slopes).astype(BF16)
        back_ref[t] = back_pre
        left_scr[:wide, span] = back_pre
        left_scr[wide:, span] = fields
        if t < DILATION_SIZE:
            early_ref[t] = mm(taps_ref[0], back_pre).astype(BF16)
    ones = wide + 16
    conv = mm_nt(right_old_ref[:ones, border_span:], left_scr[: wide + chans, border_span:])
    conv = conv + mm_nt(right_ref[:ones, :], left_scr[: wide + chans, :border_span])
    mixes = mm_nt(left_scr[wide:, border_span:], right_old_ref[ones:, border_span:])
    mixes = mixes + mm_nt(left_scr[wide:, :border_span], right_ref[ones:, :])
    sums = conv[wide : wide + 8]
    conv = conv[:wide, :wide]
    zero, first, second = [mixes[k * chans : (k + 1) * chans] for k in range(3)]
    blank = jnp.zeros((chans, wide), F32)
    mixes = jnp.concatenate([fold(zero, first), fold(second, blank)], 0)
    mix_sums = jnp.concatenate([sums[:, wide:], blank[:8, :chans]], 1)
    conv = jnp.concatenate([conv, sums[:, :wide], blank[:8]], 0)
    mixes = jnp.concatenate([mixes, mix_sums, blank[:8]], 0)
    kept_ref[...] = jnp.where(core == 0, conv, mixes)
    given_ref[...] = jnp.where(core == 0, mixes, conv)


def boundary_rows(hidden, own, chosen):
    chosen_low, chosen_high = halves(chosen)
    hop = mm_nt(hidden, own).astype(BF16)
    return (mm(hidden, chosen_low) + mm(hop, chosen_high)).astype(BF16)


def boundary_kernel(hidden_ref, own_ref, chosen_ref, boundary_ref):
    hidden = hidden_ref[: boundary_ref.shape[0], :]
    boundary_ref[...] = boundary_rows(hidden, own_ref[...], chosen_ref[...])


def outputs_kernel(
    input_ref,
    hidden_ref,
    own_boundary_ref,
    boundary_ref,
    packed_ref,
    own_ref,
    halo_ref,
    mix_ref,
    bias_ref,
    out_ref,
):
    steps, chans, sensors = input_ref.shape
    rows = steps * chans
    own = own_ref[...]
    halo = halo_ref[...]
    halo_low, halo_high = halves(halo)
    link = turned_link_matrix(packed_ref[rows:, :])
    hidden = hidden_ref[...]
    own_boundary = own_boundary_ref[...]
    boundary = boundary_ref[...]
    one = (mm_nt(hidden, own) + mm_nt(boundary, halo_low)).astype(BF16)
    far = (boundary.astype(F32) + mm_nt(own_boundary, link)).astype(BF16)
    two = (mm_nt(one, own) + mm_nt(far, halo_high)).astype(BF16)
    bias = column(bias_ref[...])
    for t in range(steps):
        at = slice(t * chans, (t + 1) * chans)
        mixed = mm(mix_ref[0], hidden[at]) + mm(mix_ref[1], one[at]) + mm(mix_ref[2], two[at])
        out_ref[t] = (mixed + bias + input_ref[t].astype(F32)).astype(BF16)


def input_grad_kernel(grad_ref, back_ref, early_ref, taps_ref, out_ref):
    steps, chans, sensors = out_ref.shape
    has_later = lax.axis_index("tm") < lax.axis_size("tm") - 1
    taps = jnp.concatenate([taps_ref[0], taps_ref[1]], 1)
    for t in range(steps):
        at = slice(t * chans, (t + 1) * chans)
        later = t + DILATION_SIZE
        total = grad_ref[at, :].astype(F32)
        if later < steps:
            total = total + mm(taps, jnp.concatenate([back_ref[later], back_ref[t]], 0))
        else:
            early = early_ref[later - steps].astype(F32)
            early = jnp.where(has_later, early, jnp.zeros_like(early))
            total = total + mm(taps_ref[1], back_ref[t]) + early
        out_ref[t] = total.astype(BF16)


def final_kernel(scale, kept_ref, other_ref, conv_w_ref, conv_b_ref, mix_w_ref, mix_b_ref):
    core = lax.axis_index("dp") % 2
    kept = kept_ref[...] * scale
    other = other_ref[...] * scale
    conv = jnp.where(core == 0, kept, other)
    mixes = jnp.where(core == 0, other, kept)
    chans = conv.shape[1] // 2
    wide = 2 * chans
    conv_w_ref[0] = conv[:chans]
    conv_w_ref[1] = conv[chans:wide]
    mix_w_ref[0] = mixes[:chans, :chans]
    mix_w_ref[1] = pltpu.roll(mixes[:chans], chans, 1)[:, :chans]
    mix_w_ref[2] = mixes[chans:wide, :chans]
    conv_b_ref[...] = (conv[wide : wide + 8] + conv[wide + 8 :])[:1]
    mix_b_ref[...] = (mixes[wide : wide + 8] + mixes[wide + 8 :])[:1, :chans]


VMEM = pl.BlockSpec(memory_space=pltpu.VMEM)
HBM = pl.BlockSpec(memory_space=pltpu.HBM)
DMA = pltpu.SemaphoreType.DMA


def call(kernel, name, in_specs, out_shape, args, scratch=(), micros=1.0):
    args = [
        pltpu.with_memory_space_constraint(arg, pltpu.HBM) if spec is HBM else arg
        for spec, arg in zip(in_specs, args)
    ]
    return pl.pallas_call(
        kernel,
        out_shape=out_shape,
        in_specs=in_specs,
        out_specs=jax.tree.map(lambda _: VMEM, out_shape),
        scratch_shapes=list(scratch),
        compiler_params=pltpu.CompilerParams(vmem_limit_bytes=VMEM_BYTES),
        cost_estimate=pl.CostEstimate(
            flops=0, bytes_accessed=int(micros * 3_600_000), transcendentals=0
        ),
        name=name,
    )(*args)


def swap(value, axis, bit):
    count = lax.axis_size(axis)
    return lax.ppermute(value, axis, [(source, source ^ bit) for source in range(count)])


def shift(value, axis, steps):
    count = lax.axis_size(axis)
    return lax.ppermute(value, axis, [(source, (source + steps) % count) for source in range(count)])


def flip(value, mask):
    sizes = [lax.axis_size(axis) for axis in AXES]
    places = list(itertools.product(*[range(size) for size in sizes]))
    index = {place: number for number, place in enumerate(places)}
    pairs = [
        (index[place], index[tuple(part ^ bit for part, bit in zip(place, mask))])
        for place in places
    ]
    return lax.ppermute(value, AXES, pairs)


def groups():
    dp, space, tm = [bits(lax.axis_size(axis)) for axis in AXES]
    first = [(bit, 0, 0) for bit in dp[1:]]
    second = [(0, bit, 0) for bit in space]
    third = [(0, 0, bit) for bit in tm]
    return [closure(masks) for masks in (first + third[:1], second + third[1:]) if masks]


def closure(masks):
    found = [(0, 0, 0)]
    for mask in masks:
        found = found + [tuple(left ^ right for left, right in zip(item, mask)) for item in found]
    return found[1:]


def bits(count):
    return [1 << place for place in range(count.bit_length() - 1)]


def to_bf16(value):
    return lax.reduce_precision(value, exponent_bits=8, mantissa_bits=7)


def round_sums(sums):
    end = sums.shape[0]
    high = sums[end - 16 : end - 8]
    rest = jnp.pad(high - to_bf16(high), ((end - 8, 0), (0, 0)))
    return to_bf16(sums + rest)


def after(value, *earlier):
    return lax.optimization_barrier((value, *earlier))[0]


def pair_body(inputs, grad_out, conv_w, conv_b, mix_w, mix_b, adj_tiles, tile_cols, send_rows, counts):
    sample_input = inputs[0]
    sample_grad = grad_out[0]
    steps, chans, sensors = sample_input.shape
    rows = steps * chans
    half_rows = rows // 2
    wide = 2 * chans
    shape = jax.ShapeDtypeStruct
    border_rows = DILATION_SIZE * chans
    grad_flat = sample_grad.reshape(rows, sensors)
    taps = jnp.transpose(conv_w, (0, 2, 1))
    packed, own, halo, chosen, grad, tail = call(
        prepare_kernel,
        "prepare",
        [HBM] * 6,
        (
            shape((rows + chans // 2, wide), BF16),
            shape((sensors, sensors), BF16),
            shape((sensors, wide), BF16),
            shape((sensors, wide), BF16),
            shape((rows, sensors), BF16),
            shape((DILATION_SIZE, chans, sensors), BF16),
        ),
        (tile_cols, counts, send_rows, adj_tiles, grad_flat, sample_input),
        scratch=(
            pltpu.VMEM(adj_tiles.shape, BF16),
            pltpu.SMEM(tile_cols.shape, jnp.int32),
            pltpu.SMEM(counts.shape, jnp.int32),
            pltpu.VMEM(send_rows.shape, jnp.int32),
            DMA((7,)),
        ),
        micros=2.0,
    )
    packed_far = swap(packed, "space", 1)
    border = shift(tail, "tm", 1)
    hidden_late, slopes, right, near, kept_input, kept_taps, turned_taps, bias, mix, mixing, mix_bias = call(
        forward_kernel,
        "forward",
        [HBM] * 5 + [VMEM] * 2,
        (
            shape((rows, sensors), BF16),
            shape((steps, wide, sensors), F32),
            shape((2 * wide + 16, steps * sensors), BF16),
            shape((rows, sensors), F32),
            shape(sample_input.shape, BF16),
            shape(taps.shape, BF16),
            shape((wide, wide), BF16),
            shape((1, wide), F32),
            shape(mix_w.shape, BF16),
            shape((chans, 3 * chans), BF16),
            shape((1, chans), F32),
        ),
        (
            sample_input,
            taps,
            conv_b.reshape(1, wide),
            mix_w,
            mix_b.reshape(1, chans),
            grad,
            own,
        ),
        scratch=(DMA((5,)),),
        micros=1.5,
    )
    border_span = DILATION_SIZE * sensors
    kept, given, back, early, hidden = call(
        backward_kernel,
        "backward",
        [VMEM] * 15,
        (
            shape((wide + 16, wide), F32),
            shape((wide + 16, wide), F32),
            shape((steps, wide, sensors), BF16),
            shape((DILATION_SIZE, chans, sensors), BF16),
            shape((rows, sensors), BF16),
        ),
        (
            grad,
            packed,
            packed_far,
            border,
            own,
            chosen,
            near,
            kept_input,
            kept_taps,
            turned_taps,
            bias,
            mixing,
            hidden_late,
            slopes,
            right,
        ),
        scratch=(
            pltpu.VMEM((wide + 3 * chans, steps * sensors), BF16),
            pltpu.VMEM((rows, sensors), BF16),
            pltpu.VMEM((rows, sensors), BF16),
            pltpu.VMEM((DILATION_SIZE, wide, sensors), F32),
            pltpu.VMEM((2 * wide + 16, border_span), BF16),
        ),
        micros=2.0,
    )
    total = kept + swap(given, "dp", 1)
    rounds = groups()
    early_far = shift(early, "tm", -1)
    boundary_first = call(
        boundary_kernel,
        "boundary",
        [VMEM] * 3,
        shape((rows, wide), BF16),
        (hidden, own, chosen),
        micros=0.3,
    )
    first_far = swap(boundary_first, "space", 1)
    outputs = call(
        outputs_kernel,
        "outputs",
        [VMEM] * 9,
        shape(sample_input.shape, BF16),
        (
            kept_input,
            hidden,
            boundary_first,
            first_far,
            packed_far,
            own,
            halo,
            mix,
            mix_bias,
        ),
        micros=2.0,
    )
    grad_inputs = call(
        input_grad_kernel,
        "input_grad",
        [VMEM] * 4,
        shape(sample_grad.shape, BF16),
        (grad, back, early_far, kept_taps),
        micros=1.2,
    )
    ready = {-2: (first_far,), -1: (outputs, grad_inputs)}
    for index, group in enumerate(rounds):
        rounded = round_sums(total)
        sent = rounded.astype(BF16)
        parts = [rounded] + [flip(sent, mask).astype(F32) for mask in group]
        parts[1] = after(parts[1], *ready.get(index - len(rounds), ()))
        while len(parts) > 1:
            parts = [left + right for left, right in zip(parts[::2], parts[1::2])]
        total = parts[0]
    total_far = swap(total, "dp", 1)
    cell_count = (
        inputs.shape[0]
        * steps
        * sensors
        * lax.axis_size("dp")
        * lax.axis_size("space")
        * lax.axis_size("tm")
    )
    scale = 1.0 / math.sqrt(cell_count)
    grad_taps, grad_conv_b, grad_mix_w, grad_mix_b = call(
        functools.partial(final_kernel, scale),
        "final",
        [VMEM] * 2,
        (
            shape((2, chans, wide), F32),
            shape((1, wide), F32),
            shape((3, chans, chans), F32),
            shape((1, chans), F32),
        ),
        (total, total_far),
    )
    return (
        outputs[None],
        grad_inputs[None],
        jnp.transpose(grad_taps, (0, 2, 1)),
        grad_conv_b.reshape(wide),
        grad_mix_w,
        grad_mix_b.reshape(chans),
    )


def power_of_two(count):
    return count & (count - 1) == 0


def body(inputs, grad_out, conv_w, conv_b, mix_w, mix_b, adj_tiles, tile_cols, send_rows, counts):
    tile = adj_tiles.shape[2]
    axes = [lax.axis_size(axis) for axis in ("dp", "space", "tm")]
    fits = (
        axes[1] == 2
        and axes[0] % 2 == 0
        and all(power_of_two(count) for count in axes)
        and inputs.shape[0] == 1
        and inputs.shape[3] == 2 * tile
        and inputs.shape[2] * 2 == tile
        and send_rows.shape[2] * 2 == tile
    )
    chosen = pair_body if fits else general_body
    return chosen(
        inputs, grad_out, conv_w, conv_b, mix_w, mix_b, adj_tiles, tile_cols, send_rows, counts
    )


def solution(mesh):
    in_specs = (
        P("dp", "tm", None, "space"),
        P("dp", "tm", None, "space"),
        P(),
        P(),
        P(),
        P(),
        P("space", None, None, None),
        P("space", None),
        P("space", None, None),
        P("space", None),
    )
    out_specs = (P("dp", "tm", None, "space"), P("dp", "tm", None, "space"), P(), P(), P(), P())
    return jax.shard_map(body, mesh=mesh, in_specs=in_specs, out_specs=out_specs, check_vma=False)
```

```python
import functools
import itertools
import math

import jax
import jax.numpy as jnp
from jax import lax
from jax.experimental import pallas as pl
from jax.experimental.pallas import tpu as pltpu
from jax.sharding import PartitionSpec as P

DILATION_SIZE = 2


def from_behind(value, axis, steps):
    count = lax.axis_size(axis)
    leading, last = (max(0, -steps), min(count, count - steps))
    return lax.ppermute(value, axis, [(source, source + steps) for source in range(leading, last)])


def slot_mask(counts, slot_count, dtype):
    slots = lax.broadcasted_iota(jnp.int32, (counts.shape[1], slot_count), 1)
    return (slots < counts[0][:, None]).astype(dtype)


def pack_rows(field, send_rows, live_slots):
    picked = field[:, :, send_rows[0]] * live_slots
    return picked.reshape(field.shape[0], field.shape[1], -1)


def tile_product(extended, adj_tiles, tile_cols):
    timestep_count, chan_count = (extended.shape[0], extended.shape[1])
    blocks = extended.reshape(timestep_count, chan_count, -1, adj_tiles.shape[2])
    picked = blocks[:, :, tile_cols]
    return jnp.einsum("tcrkj,rkij->tcri", picked, adj_tiles, preferred_element_type=jnp.float32)


def forward_start(field, send_rows, live_slots):
    packed = pack_rows(field, send_rows, live_slots)
    own_part = None
    return (packed, own_part)


def forward_finish(field, received, adj_tiles, tile_cols):
    total = tile_product(jnp.concatenate([field, received], 2), adj_tiles, tile_cols)
    return total.reshape(field.shape).astype(jnp.bfloat16)


def back_start(grad, adj_tiles, tile_cols, send_rows):
    timestep_count, chan_count, sensor_count = grad.shape
    tile_size = adj_tiles.shape[2]
    row_blocks = sensor_count // tile_size
    half_slots = tile_cols.shape[1] // 2
    halo_blocks = send_rows.shape[1] * send_rows.shape[2] // tile_size
    blocks = grad.reshape(timestep_count, chan_count, row_blocks, tile_size)
    remote_terms = jnp.einsum(
        "tcri,rkij->tcrkj", blocks, adj_tiles[:, half_slots:], preferred_element_type=jnp.float32
    )
    remote_sums = jnp.zeros((timestep_count, chan_count, halo_blocks, tile_size), jnp.float32)
    remote_sums = remote_sums.at[:, :, tile_cols[:, half_slots:] - row_blocks].add(remote_terms)
    return remote_sums.reshape(timestep_count, chan_count, -1).astype(jnp.bfloat16)


def back_finish(grad, returned, adj_tiles, tile_cols, send_rows, live_slots):
    timestep_count, chan_count, sensor_count = grad.shape
    tile_size = adj_tiles.shape[2]
    row_blocks = sensor_count // tile_size
    half_slots = tile_cols.shape[1] // 2
    blocks = grad.reshape(timestep_count, chan_count, row_blocks, tile_size)
    own_terms = jnp.einsum(
        "tcri,rkij->tcrkj", blocks, adj_tiles[:, :half_slots], preferred_element_type=jnp.float32
    )
    total = jnp.zeros((timestep_count, chan_count, row_blocks, tile_size), jnp.float32)
    total = total.at[:, :, tile_cols[:, :half_slots]].add(own_terms).reshape(grad.shape)
    returned = returned.reshape(
        timestep_count, chan_count, send_rows.shape[1], send_rows.shape[2]
    ).astype(jnp.float32)
    return total.at[:, :, send_rows[0]].add(returned * live_slots.astype(jnp.float32))


def mixing_grads(sample_grad, fields):
    grad_mix_w = jnp.stack(
        [
            jnp.einsum("ton,tcn->oc", sample_grad, item, preferred_element_type=jnp.float32)
            for item in fields
        ]
    )
    grad_mix_b = jnp.sum(sample_grad.astype(jnp.float32), axis=(0, 2))
    return (grad_mix_w, grad_mix_b)


def general_body(inputs, grad_out, conv_w, conv_b, mix_w, mix_b, adj_tiles, tile_cols, send_rows, counts):
    sample_input = inputs[0]
    sample_grad = grad_out[0]
    timestep_count, chan_count, sensor_count = sample_input.shape
    live_slots = slot_mask(counts, send_rows.shape[2], jnp.bfloat16)
    prior_border_slice = from_behind(sample_input[timestep_count - DILATION_SIZE :], "tm", 1)
    preceding_window = jnp.concatenate(
        [prior_border_slice, sample_input[: timestep_count - DILATION_SIZE]], 0
    )
    preact = jnp.einsum("oc,tcn->ton", conv_w[1], sample_input, preferred_element_type=jnp.float32)
    preact = preact + jnp.einsum(
        "oc,tcn->ton", conv_w[0], preceding_window, preferred_element_type=jnp.float32
    )
    preact = preact + conv_b[None, :, None]
    filtered = jnp.tanh(preact[:, :chan_count])
    gating = jax.nn.sigmoid(preact[:, chan_count:])
    hidden = (filtered * gating).astype(jnp.bfloat16)
    grad_float = sample_grad.astype(jnp.float32)
    packed_one, early_one = forward_start(hidden, send_rows, live_slots)
    received_one = lax.all_to_all(packed_one, "space", split_axis=2, concat_axis=2, tiled=True)
    hop_one = forward_finish(hidden, received_one, adj_tiles, tile_cols)
    packed_two, early_two = forward_start(hop_one, send_rows, live_slots)
    received_two = lax.all_to_all(packed_two, "space", split_axis=2, concat_axis=2, tiled=True)
    hop_two = forward_finish(hop_one, received_two, adj_tiles, tile_cols)
    fields = (hidden, hop_one, hop_two)
    grad_mix_w, grad_mix_b = mixing_grads(sample_grad, fields)
    back_two = jnp.einsum(
        "oc,ton->tcn", mix_w[2], sample_grad, preferred_element_type=jnp.float32
    ).astype(jnp.bfloat16)
    returned_two = lax.all_to_all(
        back_start(back_two, adj_tiles, tile_cols, send_rows),
        "space",
        split_axis=2,
        concat_axis=2,
        tiled=True,
    )
    back_one = jnp.einsum("oc,ton->tcn", mix_w[1], sample_grad, preferred_element_type=jnp.float32)
    back_one = (
        back_one + back_finish(back_two, returned_two, adj_tiles, tile_cols, send_rows, live_slots)
    ).astype(jnp.bfloat16)
    returned_one = lax.all_to_all(
        back_start(back_one, adj_tiles, tile_cols, send_rows),
        "space",
        split_axis=2,
        concat_axis=2,
        tiled=True,
    )
    back_hidden = jnp.einsum(
        "oc,ton->tcn", mix_w[0], sample_grad, preferred_element_type=jnp.float32
    )
    back_hidden = back_hidden + back_finish(
        back_one, returned_one, adj_tiles, tile_cols, send_rows, live_slots
    )
    mixed = sample_input.astype(jnp.float32) + mix_b[None, :, None]
    for index in range(3):
        mixed = mixed + jnp.einsum(
            "oc,tcn->ton", mix_w[index], fields[index], preferred_element_type=jnp.float32
        )
    outputs = mixed.astype(jnp.bfloat16)[None]
    grad_filter = back_hidden * (1.0 - filtered * filtered) * gating
    grad_gate = back_hidden * filtered * gating * (1.0 - gating)
    backward_preactivation = jnp.concatenate([grad_filter, grad_gate], 1).astype(jnp.bfloat16)
    next_border_slice = from_behind(backward_preactivation[:DILATION_SIZE], "tm", -1)
    following_window = jnp.concatenate(
        [backward_preactivation[DILATION_SIZE:], next_border_slice], 0
    )
    grad_inputs = grad_float + jnp.einsum(
        "oc,ton->tcn", conv_w[1], backward_preactivation, preferred_element_type=jnp.float32
    )
    grad_inputs = grad_inputs + jnp.einsum(
        "oc,ton->tcn", conv_w[0], following_window, preferred_element_type=jnp.float32
    )
    grad_inputs = grad_inputs.astype(jnp.bfloat16)[None]
    grad_conv_w = jnp.stack(
        [
            jnp.einsum(
                "ton,tcn->oc",
                backward_preactivation,
                preceding_window,
                preferred_element_type=jnp.float32,
            ),
            jnp.einsum(
                "ton,tcn->oc",
                backward_preactivation,
                sample_input,
                preferred_element_type=jnp.float32,
            ),
        ]
    )
    grad_conv_b = jnp.sum(backward_preactivation.astype(jnp.float32), axis=(0, 2))
    grad_conv_w, grad_conv_b, grad_mix_w, grad_mix_b = lax.psum(
        (grad_conv_w, grad_conv_b, grad_mix_w, grad_mix_b), ("dp", "space", "tm")
    )
    cell_count = (
        inputs.shape[0]
        * timestep_count
        * sensor_count
        * lax.axis_size("dp")
        * lax.axis_size("space")
        * lax.axis_size("tm")
    )
    scale = 1.0 / math.sqrt(cell_count)
    return (
        outputs,
        grad_inputs,
        grad_conv_w * scale,
        grad_conv_b * scale,
        grad_mix_w * scale,
        grad_mix_b * scale,
    )


BF16 = jnp.bfloat16
AXES = ("dp", "space", "tm")
F32 = jnp.float32
NT = (((1,), (1,)), ((), ()))
VMEM_BYTES = 24 * 1024 * 1024


def mm(left, right):
    return jnp.dot(left, right, preferred_element_type=F32)


def mm_nt(left, right):
    return lax.dot_general(left, right, NT, preferred_element_type=F32)


def upper_lanes(shape):
    return lax.broadcasted_iota(jnp.int32, shape, 1) >= shape[1] // 2


def halves(matrix):
    upper = upper_lanes(matrix.shape)
    zero = jnp.zeros_like(matrix)
    return jnp.where(upper, zero, matrix), jnp.where(upper, matrix, zero)


def fold(first, second):
    return jnp.where(upper_lanes(first.shape), second, first)


def times_halves(left, right):
    half = left.shape[0] // 2
    return fold(mm(left[:half], right), mm(left[half:], right))


def link_rows(packed):
    packed = packed.astype(F32)
    turned = pltpu.roll(packed, packed.shape[1] // 2, 1)
    return jnp.concatenate([halves(packed)[0], halves(turned)[0]], 0).astype(BF16)


def turned_link_matrix(packed):
    packed = packed.astype(F32)
    turned = pltpu.roll(packed, packed.shape[1] // 2, 1)
    blank = jnp.zeros_like(packed)
    return jnp.concatenate([blank, blank, halves(packed)[0], halves(turned)[0]], 0).astype(BF16)


def column(row):
    size = row.shape[1]
    first = lax.broadcasted_iota(jnp.int32, (size, size), 0)
    second = lax.broadcasted_iota(jnp.int32, (size, size), 1)
    return jnp.sum(jnp.where(first == second, row, 0.0), axis=1, keepdims=True)


def fetch(pairs, sems):
    copies = [
        pltpu.make_async_copy(source, target, sems.at[index])
        for index, (source, target) in enumerate(pairs)
    ]
    for copy in copies:
        copy.start()
    return copies


def prepare_kernel(
    cols_hbm,
    counts_hbm,
    rows_hbm,
    adj_hbm,
    grad_hbm,
    input_hbm,
    packed_ref,
    own_ref,
    halo_ref,
    chosen_ref,
    grad_ref,
    tail_ref,
    adj_ref,
    cols_ref,
    counts_ref,
    rows_ref,
    sems,
):
    row_blocks, slots, tile = adj_ref.shape[:3]
    own_slots = slots // 2
    steps = input_hbm.shape[0]
    copies = fetch(
        [
            (adj_hbm.at[:, pl.ds(own_slots, own_slots)], adj_ref.at[:, pl.ds(own_slots, own_slots)]),
            (cols_hbm, cols_ref),
            (counts_hbm, counts_ref),
            (rows_hbm, rows_ref),
            (adj_hbm.at[:, pl.ds(0, own_slots)], adj_ref.at[:, pl.ds(0, own_slots)]),
            (grad_hbm, grad_ref),
            (input_hbm.at[pl.ds(steps - DILATION_SIZE, DILATION_SIZE)], tail_ref),
        ],
        sems,
    )
    other = 1 - lax.axis_index("space")
    sensors = grad_ref.shape[1]
    rows_count = grad_ref.shape[0]
    slot_count = rows_ref.shape[2]
    upper = upper_lanes((tile, tile)).astype(jnp.int32)
    for copy in copies[:5]:
        copy.wait()
    for r in range(row_blocks):
        far = adj_ref[r, own_slots].astype(F32)
        for k in range(own_slots + 1, slots):
            far = far + adj_ref[r, k].astype(F32)
        far = jnp.where(upper == other, far, pltpu.roll(far, tile // 2, 1))
        halo_ref[r * tile : (r + 1) * tile, :] = far.astype(BF16)
    rows = rows_ref[0, pl.ds(other, 1), :]
    rows = jnp.concatenate([rows, rows], 1)
    lanes = lax.broadcasted_iota(jnp.int32, (1, 2 * slot_count), 1)
    place = lanes - jnp.where(lanes >= slot_count, slot_count, 0)
    rows = jnp.where(place < counts_ref[0, other], rows, -1)
    sensor = lax.broadcasted_iota(jnp.int32, (sensors, 2 * slot_count), 0)
    chosen = jnp.where(sensor == rows, 1.0, 0.0).astype(F32)
    chosen_ref[...] = chosen.astype(BF16)
    turned = jnp.transpose(chosen)[:slot_count].astype(BF16)
    halo = halo_ref[...]
    packed_ref[rows_count:, :] = times_halves(turned, halo).astype(BF16)
    for r in range(row_blocks):
        sums = [jnp.zeros((tile, tile), F32), jnp.zeros((tile, tile), F32)]
        for k in range(own_slots):
            item = adj_ref[r, k].astype(F32)
            for block in range(2):
                share = jnp.where(cols_ref[r, k] == block, 1.0, 0.0).astype(F32)
                sums[block] = sums[block] + item * share
        own_ref[r * tile : (r + 1) * tile, :] = jnp.concatenate(sums, 1).astype(BF16)
    both = fold(halo, mm(own_ref[...], halo).astype(BF16))
    copies[5].wait()
    packed_ref[:rows_count, :] = mm(grad_ref[...], both).astype(BF16)
    copies[6].wait()


def gate_step(t, earlier, input_ref, preact, hidden_ref, slopes_ref, right_ref):
    steps, chans, sensors = input_ref.shape
    at = slice(t * chans, (t + 1) * chans)
    span = slice(t * sensors, (t + 1) * sensors)
    filtered = jnp.tanh(preact[:chans])
    gating = 0.5 * jnp.tanh(0.5 * preact[chans:]) + 0.5
    product = filtered * gating
    hidden = product.astype(BF16)
    hidden_ref[at, :] = hidden
    slopes_ref[t, :chans] = (1.0 - filtered * filtered) * gating
    slopes_ref[t, chans:] = product * (1.0 - gating)
    right_ref[:chans, span] = earlier
    right_ref[chans : 2 * chans, span] = input_ref[t]
    right_ref[2 * chans : 2 * chans + 16, span] = jnp.ones((16, sensors), BF16)
    right_ref[2 * chans + 16 : 3 * chans + 16, span] = hidden
    right_ref[3 * chans + 16 :, span] = hidden


def forward_kernel(
    input_hbm,
    conv_w_hbm,
    conv_b_hbm,
    mix_w_hbm,
    mix_b_hbm,
    grad_ref,
    own_ref,
    chosen_ref,
    hidden_ref,
    slopes_ref,
    right_ref,
    near_ref,
    spread_ref,
    input_ref,
    taps_ref,
    turned_taps_ref,
    bias_ref,
    mix_ref,
    mixing_ref,
    mix_bias_ref,
    sems,
):
    copies = fetch(
        [
            (input_hbm, input_ref),
            (conv_w_hbm, taps_ref),
            (conv_b_hbm, bias_ref),
            (mix_w_hbm, mix_ref),
            (mix_b_hbm, mix_bias_ref),
        ],
        sems,
    )
    steps, chans, sensors = input_ref.shape
    own = own_ref[...]
    near = mm(grad_ref[...], own)
    near_ref[:, :sensors] = near
    near_ref[:, sensors:] = mm(near.astype(BF16), own)
    turned = jnp.transpose(chosen_ref[...].astype(F32)).astype(BF16)
    slot_count = turned.shape[0] // 2
    spread_ref[:, :sensors] = jnp.where(
        lax.broadcasted_iota(jnp.int32, turned.shape, 0) < slot_count,
        turned,
        jnp.zeros_like(turned),
    )
    spread_ref[:slot_count, sensors:] = mm(turned[:slot_count], own).astype(BF16)
    spread_ref[slot_count:, sensors:] = turned[slot_count:]
    for copy in copies:
        copy.wait()
    mixing = jnp.transpose(mix_ref[...].reshape(3 * chans, chans).astype(F32))
    mixing_ref[...] = mixing.astype(BF16)
    taps = taps_ref[...].reshape(2 * chans, 2 * chans).astype(F32)
    taps = jnp.transpose(taps).astype(BF16)
    turned_taps_ref[...] = taps
    bias = column(bias_ref[...])
    for t in range(DILATION_SIZE, steps):
        earlier = input_ref[t - DILATION_SIZE]
        preact = mm(taps, jnp.concatenate([earlier, input_ref[t]], 0)) + bias
        gate_step(t, earlier, input_ref, preact, hidden_ref, slopes_ref, right_ref)


def backward_kernel(
    grad_ref,
    own_packed_ref,
    packed_ref,
    border_ref,
    near_ref,
    spread_ref,
    input_ref,
    turned_taps_ref,
    bias_ref,
    mixing_ref,
    hidden_old_ref,
    slopes_old_ref,
    right_old_ref,
    kept_ref,
    given_ref,
    back_ref,
    hidden_ref,
    left_scr,
    both_scr,
    slopes_ref,
    right_ref,
):
    steps, wide, sensors = back_ref.shape
    chans = wide // 2
    rows = steps * chans
    border_rows = DILATION_SIZE * chans
    border_span = DILATION_SIZE * sensors
    core = lax.axis_index("dp") % 2
    linked = mm(link_rows(packed_ref[rows:, :]), spread_ref[:, :sensors]).astype(BF16)
    blank = jnp.zeros_like(linked)
    linked = jnp.concatenate([blank, linked], 1)
    spread = jnp.concatenate([spread_ref[...], linked, jnp.zeros_like(linked)], 0)
    packed = jnp.concatenate([packed_ref[:rows, :], own_packed_ref[:rows, :]], 1)
    both_scr[...] = (near_ref[...] + mm(packed, spread)).astype(BF16)
    bias = column(bias_ref[...])
    place = lax.axis_index("tm")
    hidden_ref[border_rows:, :] = hidden_old_ref[border_rows:, :]
    for t in range(DILATION_SIZE):
        earlier = border_ref[t]
        earlier = jnp.where(place > 0, earlier, jnp.zeros_like(earlier))
        window = jnp.concatenate([earlier, input_ref[t]], 0)
        preact = mm(turned_taps_ref[...], window) + bias
        gate_step(t, earlier, input_ref, preact, hidden_ref, slopes_ref, right_ref)
    mixing = mixing_ref[...]
    for t in range(steps):
        at = slice(t * chans, (t + 1) * chans)
        span = slice(t * sensors, (t + 1) * sensors)
        fields = jnp.concatenate(
            [grad_ref[at, :], both_scr[at, :sensors], both_scr[at, sensors:]], 0
        )
        back_hidden = mm(mixing, fields)
        back_hidden = jnp.concatenate([back_hidden, back_hidden], 0)
        slopes = slopes_ref[t] if t < DILATION_SIZE else slopes_old_ref[t]
        back_pre = (back_hidden * slopes).astype(BF16)
        back_ref[t] = back_pre
        left_scr[:wide, span] = back_pre
        left_scr[wide:, span] = fields
    ones = wide + 16
    conv = mm_nt(right_old_ref[:ones, border_span:], left_scr[: wide + chans, border_span:])
    conv = conv + mm_nt(right_ref[:ones, :], left_scr[: wide + chans, :border_span])
    mixes = mm_nt(left_scr[wide:, border_span:], right_old_ref[ones:, border_span:])
    mixes = mixes + mm_nt(left_scr[wide:, :border_span], right_ref[ones:, :])
    sums = conv[wide : wide + 8]
    conv = conv[:wide, :wide]
    zero, first, second = [mixes[k * chans : (k + 1) * chans] for k in range(3)]
    blank = jnp.zeros((chans, wide), F32)
    mixes = jnp.concatenate([fold(zero, first), fold(second, blank)], 0)
    mix_sums = jnp.concatenate([sums[:, wide:], blank[:8, :chans]], 1)
    conv = jnp.concatenate([conv, sums[:, :wide], blank[:8]], 0)
    mixes = jnp.concatenate([mixes, mix_sums, blank[:8]], 0)
    kept_ref[...] = jnp.where(core == 0, conv, mixes)
    given_ref[...] = jnp.where(core == 0, mixes, conv)


def boundary_rows(hidden, own, chosen):
    chosen_low, chosen_high = halves(chosen)
    hop = mm_nt(hidden, own).astype(BF16)
    return (mm(hidden, chosen_low) + mm(hop, chosen_high)).astype(BF16)


def early_kernel(back_ref, taps_ref, early_ref):
    for t in range(DILATION_SIZE):
        early_ref[t] = mm(taps_ref[0], back_ref[t]).astype(BF16)


def boundary_kernel(hidden_ref, own_ref, chosen_ref, boundary_ref):
    hidden = hidden_ref[: boundary_ref.shape[0], :]
    boundary_ref[...] = boundary_rows(hidden, own_ref[...], chosen_ref[...])


def outputs_kernel(
    input_ref,
    hidden_ref,
    own_boundary_ref,
    boundary_ref,
    packed_ref,
    own_ref,
    halo_ref,
    mix_ref,
    bias_ref,
    out_ref,
):
    steps, chans, sensors = input_ref.shape
    rows = steps * chans
    own = own_ref[...]
    halo = halo_ref[...]
    halo_low, halo_high = halves(halo)
    link = turned_link_matrix(packed_ref[rows:, :])
    hidden = hidden_ref[...]
    own_boundary = own_boundary_ref[...]
    boundary = boundary_ref[...]
    one = (mm_nt(hidden, own) + mm_nt(boundary, halo_low)).astype(BF16)
    far = (boundary.astype(F32) + mm_nt(own_boundary, link)).astype(BF16)
    two = (mm_nt(one, own) + mm_nt(far, halo_high)).astype(BF16)
    bias = column(bias_ref[...])
    for t in range(steps):
        at = slice(t * chans, (t + 1) * chans)
        mixed = mm(mix_ref[0], hidden[at]) + mm(mix_ref[1], one[at]) + mm(mix_ref[2], two[at])
        out_ref[t] = (mixed + bias + input_ref[t].astype(F32)).astype(BF16)


def input_grad_kernel(grad_ref, back_ref, early_ref, taps_ref, out_ref):
    steps, chans, sensors = out_ref.shape
    has_later = lax.axis_index("tm") < lax.axis_size("tm") - 1
    taps = jnp.concatenate([taps_ref[0], taps_ref[1]], 1)
    for t in range(steps):
        at = slice(t * chans, (t + 1) * chans)
        later = t + DILATION_SIZE
        total = grad_ref[at, :].astype(F32)
        if later < steps:
            total = total + mm(taps, jnp.concatenate([back_ref[later], back_ref[t]], 0))
        else:
            early = early_ref[later - steps].astype(F32)
            early = jnp.where(has_later, early, jnp.zeros_like(early))
            total = total + mm(taps_ref[1], back_ref[t]) + early
        out_ref[t] = total.astype(BF16)


def final_kernel(scale, kept_ref, other_ref, conv_w_ref, conv_b_ref, mix_w_ref, mix_b_ref):
    core = lax.axis_index("dp") % 2
    kept = kept_ref[...] * scale
    other = other_ref[...] * scale
    conv = jnp.where(core == 0, kept, other)
    mixes = jnp.where(core == 0, other, kept)
    chans = conv.shape[1] // 2
    wide = 2 * chans
    conv_w_ref[0] = conv[:chans]
    conv_w_ref[1] = conv[chans:wide]
    mix_w_ref[0] = mixes[:chans, :chans]
    mix_w_ref[1] = pltpu.roll(mixes[:chans], chans, 1)[:, :chans]
    mix_w_ref[2] = mixes[chans:wide, :chans]
    conv_b_ref[...] = (conv[wide : wide + 8] + conv[wide + 8 :])[:1]
    mix_b_ref[...] = (mixes[wide : wide + 8] + mixes[wide + 8 :])[:1, :chans]


VMEM = pl.BlockSpec(memory_space=pltpu.VMEM)
HBM = pl.BlockSpec(memory_space=pltpu.HBM)
DMA = pltpu.SemaphoreType.DMA


def call(kernel, name, in_specs, out_shape, args, scratch=(), micros=1.0):
    args = [
        pltpu.with_memory_space_constraint(arg, pltpu.HBM) if spec is HBM else arg
        for spec, arg in zip(in_specs, args)
    ]
    return pl.pallas_call(
        kernel,
        out_shape=out_shape,
        in_specs=in_specs,
        out_specs=jax.tree.map(lambda _: VMEM, out_shape),
        scratch_shapes=list(scratch),
        compiler_params=pltpu.CompilerParams(vmem_limit_bytes=VMEM_BYTES),
        cost_estimate=pl.CostEstimate(
            flops=0, bytes_accessed=int(micros * 3_600_000), transcendentals=0
        ),
        name=name,
    )(*args)


def swap(value, axis, bit):
    count = lax.axis_size(axis)
    return lax.ppermute(value, axis, [(source, source ^ bit) for source in range(count)])


def shift(value, axis, steps):
    count = lax.axis_size(axis)
    return lax.ppermute(value, axis, [(source, (source + steps) % count) for source in range(count)])


def flip(value, mask):
    sizes = [lax.axis_size(axis) for axis in AXES]
    places = list(itertools.product(*[range(size) for size in sizes]))
    index = {place: number for number, place in enumerate(places)}
    pairs = [
        (index[place], index[tuple(part ^ bit for part, bit in zip(place, mask))])
        for place in places
    ]
    return lax.ppermute(value, AXES, pairs)


def groups():
    dp, space, tm = [bits(lax.axis_size(axis)) for axis in AXES]
    first = [(bit, 0, 0) for bit in dp[1:]]
    second = [(0, bit, 0) for bit in space]
    third = [(0, 0, bit) for bit in tm]
    return [closure(masks) for masks in (first + second, third) if masks]


def closure(masks):
    found = [(0, 0, 0)]
    for mask in masks:
        found = found + [tuple(left ^ right for left, right in zip(item, mask)) for item in found]
    return found[1:]


def bits(count):
    return [1 << place for place in range(count.bit_length() - 1)]


def to_bf16(value):
    return lax.reduce_precision(value, exponent_bits=8, mantissa_bits=7)


def round_sums(sums):
    end = sums.shape[0]
    high = sums[end - 16 : end - 8]
    rest = jnp.pad(high - to_bf16(high), ((end - 8, 0), (0, 0)))
    return to_bf16(sums + rest)


def after(value, *earlier):
    return lax.optimization_barrier((value, *earlier))[0]


def pair_body(inputs, grad_out, conv_w, conv_b, mix_w, mix_b, adj_tiles, tile_cols, send_rows, counts):
    sample_input = inputs[0]
    sample_grad = grad_out[0]
    steps, chans, sensors = sample_input.shape
    rows = steps * chans
    half_rows = rows // 2
    wide = 2 * chans
    shape = jax.ShapeDtypeStruct
    border_rows = DILATION_SIZE * chans
    grad_flat = sample_grad.reshape(rows, sensors)
    taps = jnp.transpose(conv_w, (0, 2, 1))
    packed, own, halo, chosen, grad, tail = call(
        prepare_kernel,
        "prepare",
        [HBM] * 6,
        (
            shape((rows + chans // 2, wide), BF16),
            shape((sensors, sensors), BF16),
            shape((sensors, wide), BF16),
            shape((sensors, wide), BF16),
            shape((rows, sensors), BF16),
            shape((DILATION_SIZE, chans, sensors), BF16),
        ),
        (tile_cols, counts, send_rows, adj_tiles, grad_flat, sample_input),
        scratch=(
            pltpu.VMEM(adj_tiles.shape, BF16),
            pltpu.SMEM(tile_cols.shape, jnp.int32),
            pltpu.SMEM(counts.shape, jnp.int32),
            pltpu.VMEM(send_rows.shape, jnp.int32),
            DMA((7,)),
        ),
        micros=2.0,
    )
    packed_far = swap(packed, "space", 1)
    border = shift(tail, "tm", 1)
    hidden_late, slopes, right, near, spread, kept_input, kept_taps, turned_taps, bias, mix, mixing, mix_bias = call(
        forward_kernel,
        "forward",
        [HBM] * 5 + [VMEM] * 3,
        (
            shape((rows, sensors), BF16),
            shape((steps, wide, sensors), F32),
            shape((2 * wide + 16, steps * sensors), BF16),
            shape((rows, 2 * sensors), F32),
            shape((wide, 2 * sensors), BF16),
            shape(sample_input.shape, BF16),
            shape(taps.shape, BF16),
            shape((wide, wide), BF16),
            shape((1, wide), F32),
            shape(mix_w.shape, BF16),
            shape((chans, 3 * chans), BF16),
            shape((1, chans), F32),
        ),
        (
            sample_input,
            taps,
            conv_b.reshape(1, wide),
            mix_w,
            mix_b.reshape(1, chans),
            grad,
            own,
            chosen,
        ),
        scratch=(DMA((5,)),),
        micros=1.5,
    )
    border_span = DILATION_SIZE * sensors
    kept, given, back, hidden = call(
        backward_kernel,
        "backward",
        [VMEM] * 13,
        (
            shape((wide + 16, wide), F32),
            shape((wide + 16, wide), F32),
            shape((steps, wide, sensors), BF16),
            shape((rows, sensors), BF16),
        ),
        (
            grad,
            packed,
            packed_far,
            border,
            near,
            spread,
            kept_input,
            turned_taps,
            bias,
            mixing,
            hidden_late,
            slopes,
            right,
        ),
        scratch=(
            pltpu.VMEM((wide + 3 * chans, steps * sensors), BF16),
            pltpu.VMEM((rows, 2 * sensors), BF16),
            pltpu.VMEM((DILATION_SIZE, wide, sensors), F32),
            pltpu.VMEM((2 * wide + 16, border_span), BF16),
        ),
        micros=2.0,
    )
    total = kept + swap(given, "dp", 1)
    rounds = groups()
    early = call(
        early_kernel,
        "early",
        [VMEM] * 2,
        shape((DILATION_SIZE, chans, sensors), BF16),
        (back, kept_taps),
        micros=0.3,
    )
    early_far = shift(early, "tm", -1)
    boundary_first = call(
        boundary_kernel,
        "boundary",
        [VMEM] * 3,
        shape((rows, wide), BF16),
        (hidden, own, chosen),
        micros=0.3,
    )
    first_far = swap(boundary_first, "space", 1)
    outputs = call(
        outputs_kernel,
        "outputs",
        [VMEM] * 9,
        shape(sample_input.shape, BF16),
        (
            kept_input,
            hidden,
            boundary_first,
            first_far,
            packed_far,
            own,
            halo,
            mix,
            mix_bias,
        ),
        micros=2.0,
    )
    grad_inputs = call(
        input_grad_kernel,
        "input_grad",
        [VMEM] * 4,
        shape(sample_grad.shape, BF16),
        (grad, back, early_far, kept_taps),
        micros=1.2,
    )
    ready = {-2: (first_far,), -1: (outputs, grad_inputs)}
    for index, group in enumerate(rounds):
        rounded = round_sums(total)
        sent = rounded.astype(BF16)
        parts = [rounded] + [flip(sent, mask).astype(F32) for mask in group]
        parts[1] = after(parts[1], *ready.get(index - len(rounds), ()))
        while len(parts) > 1:
            parts = [left + right for left, right in zip(parts[::2], parts[1::2])]
        total = parts[0]
    total_far = swap(total, "dp", 1)
    cell_count = (
        inputs.shape[0]
        * steps
        * sensors
        * lax.axis_size("dp")
        * lax.axis_size("space")
        * lax.axis_size("tm")
    )
    scale = 1.0 / math.sqrt(cell_count)
    grad_taps, grad_conv_b, grad_mix_w, grad_mix_b = call(
        functools.partial(final_kernel, scale),
        "final",
        [VMEM] * 2,
        (
            shape((2, chans, wide), F32),
            shape((1, wide), F32),
            shape((3, chans, chans), F32),
            shape((1, chans), F32),
        ),
        (total, total_far),
    )
    return (
        outputs[None],
        grad_inputs[None],
        jnp.transpose(grad_taps, (0, 2, 1)),
        grad_conv_b.reshape(wide),
        grad_mix_w,
        grad_mix_b.reshape(chans),
    )


def power_of_two(count):
    return count & (count - 1) == 0


def body(inputs, grad_out, conv_w, conv_b, mix_w, mix_b, adj_tiles, tile_cols, send_rows, counts):
    tile = adj_tiles.shape[2]
    axes = [lax.axis_size(axis) for axis in ("dp", "space", "tm")]
    fits = (
        axes[1] == 2
        and axes[0] % 2 == 0
        and all(power_of_two(count) for count in axes)
        and inputs.shape[0] == 1
        and inputs.shape[3] == 2 * tile
        and inputs.shape[2] * 2 == tile
        and send_rows.shape[2] * 2 == tile
    )
    chosen = pair_body if fits else general_body
    return chosen(
        inputs, grad_out, conv_w, conv_b, mix_w, mix_b, adj_tiles, tile_cols, send_rows, counts
    )


def solution(mesh):
    in_specs = (
        P("dp", "tm", None, "space"),
        P("dp", "tm", None, "space"),
        P(),
        P(),
        P(),
        P(),
        P("space", None, None, None),
        P("space", None),
        P("space", None, None),
        P("space", None),
    )
    out_specs = (P("dp", "tm", None, "space"), P("dp", "tm", None, "space"), P(), P(), P(), P())
    return jax.shard_map(body, mesh=mesh, in_specs=in_specs, out_specs=out_specs, check_vma=False)
```

```python
import functools
import itertools
import math

import jax
import jax.numpy as jnp
from jax import lax
from jax.experimental import pallas as pl
from jax.experimental.pallas import tpu as pltpu
from jax.sharding import PartitionSpec as P

DILATION_SIZE = 2


def from_behind(value, axis, steps):
    count = lax.axis_size(axis)
    leading, last = (max(0, -steps), min(count, count - steps))
    return lax.ppermute(value, axis, [(source, source + steps) for source in range(leading, last)])


def slot_mask(counts, slot_count, dtype):
    slots = lax.broadcasted_iota(jnp.int32, (counts.shape[1], slot_count), 1)
    return (slots < counts[0][:, None]).astype(dtype)


def pack_rows(field, send_rows, live_slots):
    picked = field[:, :, send_rows[0]] * live_slots
    return picked.reshape(field.shape[0], field.shape[1], -1)


def tile_product(extended, adj_tiles, tile_cols):
    timestep_count, chan_count = (extended.shape[0], extended.shape[1])
    blocks = extended.reshape(timestep_count, chan_count, -1, adj_tiles.shape[2])
    picked = blocks[:, :, tile_cols]
    return jnp.einsum("tcrkj,rkij->tcri", picked, adj_tiles, preferred_element_type=jnp.float32)


def forward_start(field, send_rows, live_slots):
    packed = pack_rows(field, send_rows, live_slots)
    own_part = None
    return (packed, own_part)


def forward_finish(field, received, adj_tiles, tile_cols):
    total = tile_product(jnp.concatenate([field, received], 2), adj_tiles, tile_cols)
    return total.reshape(field.shape).astype(jnp.bfloat16)


def back_start(grad, adj_tiles, tile_cols, send_rows):
    timestep_count, chan_count, sensor_count = grad.shape
    tile_size = adj_tiles.shape[2]
    row_blocks = sensor_count // tile_size
    half_slots = tile_cols.shape[1] // 2
    halo_blocks = send_rows.shape[1] * send_rows.shape[2] // tile_size
    blocks = grad.reshape(timestep_count, chan_count, row_blocks, tile_size)
    remote_terms = jnp.einsum(
        "tcri,rkij->tcrkj", blocks, adj_tiles[:, half_slots:], preferred_element_type=jnp.float32
    )
    remote_sums = jnp.zeros((timestep_count, chan_count, halo_blocks, tile_size), jnp.float32)
    remote_sums = remote_sums.at[:, :, tile_cols[:, half_slots:] - row_blocks].add(remote_terms)
    return remote_sums.reshape(timestep_count, chan_count, -1).astype(jnp.bfloat16)


def back_finish(grad, returned, adj_tiles, tile_cols, send_rows, live_slots):
    timestep_count, chan_count, sensor_count = grad.shape
    tile_size = adj_tiles.shape[2]
    row_blocks = sensor_count // tile_size
    half_slots = tile_cols.shape[1] // 2
    blocks = grad.reshape(timestep_count, chan_count, row_blocks, tile_size)
    own_terms = jnp.einsum(
        "tcri,rkij->tcrkj", blocks, adj_tiles[:, :half_slots], preferred_element_type=jnp.float32
    )
    total = jnp.zeros((timestep_count, chan_count, row_blocks, tile_size), jnp.float32)
    total = total.at[:, :, tile_cols[:, :half_slots]].add(own_terms).reshape(grad.shape)
    returned = returned.reshape(
        timestep_count, chan_count, send_rows.shape[1], send_rows.shape[2]
    ).astype(jnp.float32)
    return total.at[:, :, send_rows[0]].add(returned * live_slots.astype(jnp.float32))


def mixing_grads(sample_grad, fields):
    grad_mix_w = jnp.stack(
        [
            jnp.einsum("ton,tcn->oc", sample_grad, item, preferred_element_type=jnp.float32)
            for item in fields
        ]
    )
    grad_mix_b = jnp.sum(sample_grad.astype(jnp.float32), axis=(0, 2))
    return (grad_mix_w, grad_mix_b)


def general_body(inputs, grad_out, conv_w, conv_b, mix_w, mix_b, adj_tiles, tile_cols, send_rows, counts):
    sample_input = inputs[0]
    sample_grad = grad_out[0]
    timestep_count, chan_count, sensor_count = sample_input.shape
    live_slots = slot_mask(counts, send_rows.shape[2], jnp.bfloat16)
    prior_border_slice = from_behind(sample_input[timestep_count - DILATION_SIZE :], "tm", 1)
    preceding_window = jnp.concatenate(
        [prior_border_slice, sample_input[: timestep_count - DILATION_SIZE]], 0
    )
    preact = jnp.einsum("oc,tcn->ton", conv_w[1], sample_input, preferred_element_type=jnp.float32)
    preact = preact + jnp.einsum(
        "oc,tcn->ton", conv_w[0], preceding_window, preferred_element_type=jnp.float32
    )
    preact = preact + conv_b[None, :, None]
    filtered = jnp.tanh(preact[:, :chan_count])
    gating = jax.nn.sigmoid(preact[:, chan_count:])
    hidden = (filtered * gating).astype(jnp.bfloat16)
    grad_float = sample_grad.astype(jnp.float32)
    packed_one, early_one = forward_start(hidden, send_rows, live_slots)
    received_one = lax.all_to_all(packed_one, "space", split_axis=2, concat_axis=2, tiled=True)
    hop_one = forward_finish(hidden, received_one, adj_tiles, tile_cols)
    packed_two, early_two = forward_start(hop_one, send_rows, live_slots)
    received_two = lax.all_to_all(packed_two, "space", split_axis=2, concat_axis=2, tiled=True)
    hop_two = forward_finish(hop_one, received_two, adj_tiles, tile_cols)
    fields = (hidden, hop_one, hop_two)
    grad_mix_w, grad_mix_b = mixing_grads(sample_grad, fields)
    back_two = jnp.einsum(
        "oc,ton->tcn", mix_w[2], sample_grad, preferred_element_type=jnp.float32
    ).astype(jnp.bfloat16)
    returned_two = lax.all_to_all(
        back_start(back_two, adj_tiles, tile_cols, send_rows),
        "space",
        split_axis=2,
        concat_axis=2,
        tiled=True,
    )
    back_one = jnp.einsum("oc,ton->tcn", mix_w[1], sample_grad, preferred_element_type=jnp.float32)
    back_one = (
        back_one + back_finish(back_two, returned_two, adj_tiles, tile_cols, send_rows, live_slots)
    ).astype(jnp.bfloat16)
    returned_one = lax.all_to_all(
        back_start(back_one, adj_tiles, tile_cols, send_rows),
        "space",
        split_axis=2,
        concat_axis=2,
        tiled=True,
    )
    back_hidden = jnp.einsum(
        "oc,ton->tcn", mix_w[0], sample_grad, preferred_element_type=jnp.float32
    )
    back_hidden = back_hidden + back_finish(
        back_one, returned_one, adj_tiles, tile_cols, send_rows, live_slots
    )
    mixed = sample_input.astype(jnp.float32) + mix_b[None, :, None]
    for index in range(3):
        mixed = mixed + jnp.einsum(
            "oc,tcn->ton", mix_w[index], fields[index], preferred_element_type=jnp.float32
        )
    outputs = mixed.astype(jnp.bfloat16)[None]
    grad_filter = back_hidden * (1.0 - filtered * filtered) * gating
    grad_gate = back_hidden * filtered * gating * (1.0 - gating)
    backward_preactivation = jnp.concatenate([grad_filter, grad_gate], 1).astype(jnp.bfloat16)
    next_border_slice = from_behind(backward_preactivation[:DILATION_SIZE], "tm", -1)
    following_window = jnp.concatenate(
        [backward_preactivation[DILATION_SIZE:], next_border_slice], 0
    )
    grad_inputs = grad_float + jnp.einsum(
        "oc,ton->tcn", conv_w[1], backward_preactivation, preferred_element_type=jnp.float32
    )
    grad_inputs = grad_inputs + jnp.einsum(
        "oc,ton->tcn", conv_w[0], following_window, preferred_element_type=jnp.float32
    )
    grad_inputs = grad_inputs.astype(jnp.bfloat16)[None]
    grad_conv_w = jnp.stack(
        [
            jnp.einsum(
                "ton,tcn->oc",
                backward_preactivation,
                preceding_window,
                preferred_element_type=jnp.float32,
            ),
            jnp.einsum(
                "ton,tcn->oc",
                backward_preactivation,
                sample_input,
                preferred_element_type=jnp.float32,
            ),
        ]
    )
    grad_conv_b = jnp.sum(backward_preactivation.astype(jnp.float32), axis=(0, 2))
    grad_conv_w, grad_conv_b, grad_mix_w, grad_mix_b = lax.psum(
        (grad_conv_w, grad_conv_b, grad_mix_w, grad_mix_b), ("dp", "space", "tm")
    )
    cell_count = (
        inputs.shape[0]
        * timestep_count
        * sensor_count
        * lax.axis_size("dp")
        * lax.axis_size("space")
        * lax.axis_size("tm")
    )
    scale = 1.0 / math.sqrt(cell_count)
    return (
        outputs,
        grad_inputs,
        grad_conv_w * scale,
        grad_conv_b * scale,
        grad_mix_w * scale,
        grad_mix_b * scale,
    )


BF16 = jnp.bfloat16
AXES = ("dp", "space", "tm")
F32 = jnp.float32
NT = (((1,), (1,)), ((), ()))
VMEM_BYTES = 24 * 1024 * 1024


def mm(left, right):
    return jnp.dot(left, right, preferred_element_type=F32)


def mm_nt(left, right):
    return lax.dot_general(left, right, NT, preferred_element_type=F32)


def upper_lanes(shape):
    return lax.broadcasted_iota(jnp.int32, shape, 1) >= shape[1] // 2


def halves(matrix):
    upper = upper_lanes(matrix.shape)
    zero = jnp.zeros_like(matrix)
    return jnp.where(upper, zero, matrix), jnp.where(upper, matrix, zero)


def fold(first, second):
    return jnp.where(upper_lanes(first.shape), second, first)


def times_halves(left, right):
    half = left.shape[0] // 2
    return fold(mm(left[:half], right), mm(left[half:], right))


def link_rows(packed):
    packed = packed.astype(F32)
    turned = pltpu.roll(packed, packed.shape[1] // 2, 1)
    return jnp.concatenate([halves(packed)[0], halves(turned)[0]], 0).astype(BF16)


def turned_link_matrix(packed):
    packed = packed.astype(F32)
    turned = pltpu.roll(packed, packed.shape[1] // 2, 1)
    blank = jnp.zeros_like(packed)
    return jnp.concatenate([blank, blank, halves(packed)[0], halves(turned)[0]], 0).astype(BF16)


def column(row):
    size = row.shape[1]
    first = lax.broadcasted_iota(jnp.int32, (size, size), 0)
    second = lax.broadcasted_iota(jnp.int32, (size, size), 1)
    return jnp.sum(jnp.where(first == second, row, 0.0), axis=1, keepdims=True)


def fetch(pairs, sems):
    copies = [
        pltpu.make_async_copy(source, target, sems.at[index])
        for index, (source, target) in enumerate(pairs)
    ]
    for copy in copies:
        copy.start()
    return copies


def prepare_kernel(
    cols_hbm,
    counts_hbm,
    rows_hbm,
    adj_hbm,
    grad_hbm,
    input_hbm,
    packed_ref,
    own_ref,
    halo_ref,
    chosen_ref,
    grad_ref,
    tail_ref,
    adj_ref,
    cols_ref,
    counts_ref,
    rows_ref,
    sems,
):
    row_blocks, slots, tile = adj_ref.shape[:3]
    own_slots = slots // 2
    steps = input_hbm.shape[0]
    copies = fetch(
        [
            (adj_hbm.at[:, pl.ds(own_slots, own_slots)], adj_ref.at[:, pl.ds(own_slots, own_slots)]),
            (cols_hbm, cols_ref),
            (counts_hbm, counts_ref),
            (rows_hbm, rows_ref),
            (adj_hbm.at[:, pl.ds(0, own_slots)], adj_ref.at[:, pl.ds(0, own_slots)]),
            (grad_hbm, grad_ref),
            (input_hbm.at[pl.ds(steps - DILATION_SIZE, DILATION_SIZE)], tail_ref),
        ],
        sems,
    )
    other = 1 - lax.axis_index("space")
    sensors = grad_ref.shape[1]
    rows_count = grad_ref.shape[0]
    slot_count = rows_ref.shape[2]
    upper = upper_lanes((tile, tile)).astype(jnp.int32)
    for copy in copies[:5]:
        copy.wait()
    for r in range(row_blocks):
        far = adj_ref[r, own_slots].astype(F32)
        for k in range(own_slots + 1, slots):
            far = far + adj_ref[r, k].astype(F32)
        far = jnp.where(upper == other, far, pltpu.roll(far, tile // 2, 1))
        halo_ref[r * tile : (r + 1) * tile, :] = far.astype(BF16)
    rows = rows_ref[0, pl.ds(other, 1), :]
    rows = jnp.concatenate([rows, rows], 1)
    lanes = lax.broadcasted_iota(jnp.int32, (1, 2 * slot_count), 1)
    place = lanes - jnp.where(lanes >= slot_count, slot_count, 0)
    rows = jnp.where(place < counts_ref[0, other], rows, -1)
    sensor = lax.broadcasted_iota(jnp.int32, (sensors, 2 * slot_count), 0)
    chosen = jnp.where(sensor == rows, 1.0, 0.0).astype(F32)
    chosen_ref[...] = chosen.astype(BF16)
    turned = jnp.transpose(chosen)[:slot_count].astype(BF16)
    halo = halo_ref[...]
    packed_ref[rows_count:, :] = times_halves(turned, halo).astype(BF16)
    for r in range(row_blocks):
        sums = [jnp.zeros((tile, tile), F32), jnp.zeros((tile, tile), F32)]
        for k in range(own_slots):
            item = adj_ref[r, k].astype(F32)
            for block in range(2):
                share = jnp.where(cols_ref[r, k] == block, 1.0, 0.0).astype(F32)
                sums[block] = sums[block] + item * share
        own_ref[r * tile : (r + 1) * tile, :] = jnp.concatenate(sums, 1).astype(BF16)
    both = fold(halo, mm(own_ref[...], halo).astype(BF16))
    copies[5].wait()
    packed_ref[:rows_count, :] = mm(grad_ref[...], both).astype(BF16)
    copies[6].wait()


def gate_step(t, earlier, input_ref, preact, hidden_ref, slopes_ref, right_ref):
    steps, chans, sensors = input_ref.shape
    at = slice(t * chans, (t + 1) * chans)
    span = slice(t * sensors, (t + 1) * sensors)
    filtered = jnp.tanh(preact[:chans])
    gating = 0.5 * jnp.tanh(0.5 * preact[chans:]) + 0.5
    product = filtered * gating
    hidden = product.astype(BF16)
    hidden_ref[at, :] = hidden
    slopes_ref[t, :chans] = (1.0 - filtered * filtered) * gating
    slopes_ref[t, chans:] = product * (1.0 - gating)
    right_ref[:chans, span] = earlier
    right_ref[chans : 2 * chans, span] = input_ref[t]
    right_ref[2 * chans : 2 * chans + 16, span] = jnp.ones((16, sensors), BF16)
    right_ref[2 * chans + 16 : 3 * chans + 16, span] = hidden
    right_ref[3 * chans + 16 :, span] = hidden


def forward_kernel(
    input_hbm,
    conv_w_hbm,
    conv_b_hbm,
    mix_w_hbm,
    mix_b_hbm,
    grad_ref,
    own_ref,
    chosen_ref,
    hidden_ref,
    slopes_ref,
    right_ref,
    near_ref,
    spread_ref,
    input_ref,
    taps_ref,
    turned_taps_ref,
    bias_ref,
    mix_ref,
    mixing_ref,
    mix_bias_ref,
    sems,
):
    copies = fetch(
        [
            (input_hbm, input_ref),
            (conv_w_hbm, taps_ref),
            (conv_b_hbm, bias_ref),
            (mix_w_hbm, mix_ref),
            (mix_b_hbm, mix_bias_ref),
        ],
        sems,
    )
    steps, chans, sensors = input_ref.shape
    own = own_ref[...]
    near = mm(grad_ref[...], own)
    near_ref[:, :sensors] = near
    near_ref[:, sensors:] = mm(near.astype(BF16), own)
    turned = jnp.transpose(chosen_ref[...].astype(F32)).astype(BF16)
    slot_count = turned.shape[0] // 2
    spread_ref[:, :sensors] = jnp.where(
        lax.broadcasted_iota(jnp.int32, turned.shape, 0) < slot_count,
        turned,
        jnp.zeros_like(turned),
    )
    spread_ref[:slot_count, sensors:] = mm(turned[:slot_count], own).astype(BF16)
    spread_ref[slot_count:, sensors:] = turned[slot_count:]
    for copy in copies:
        copy.wait()
    mixing = jnp.transpose(mix_ref[...].reshape(3 * chans, chans).astype(F32))
    mixing_ref[...] = mixing.astype(BF16)
    taps = taps_ref[...].reshape(2 * chans, 2 * chans).astype(F32)
    taps = jnp.transpose(taps).astype(BF16)
    turned_taps_ref[...] = taps
    bias = column(bias_ref[...])
    for t in range(DILATION_SIZE, steps):
        earlier = input_ref[t - DILATION_SIZE]
        preact = mm(taps, jnp.concatenate([earlier, input_ref[t]], 0)) + bias
        gate_step(t, earlier, input_ref, preact, hidden_ref, slopes_ref, right_ref)


def backward_kernel(
    grad_ref,
    own_packed_ref,
    packed_ref,
    border_ref,
    near_ref,
    spread_ref,
    input_ref,
    turned_taps_ref,
    bias_ref,
    mixing_ref,
    hidden_old_ref,
    slopes_old_ref,
    right_old_ref,
    kept_ref,
    given_ref,
    back_ref,
    hidden_ref,
    left_scr,
    both_scr,
    slopes_ref,
    right_ref,
):
    steps, wide, sensors = back_ref.shape
    chans = wide // 2
    rows = steps * chans
    border_rows = DILATION_SIZE * chans
    border_span = DILATION_SIZE * sensors
    core = lax.axis_index("dp") % 2
    linked = mm(link_rows(packed_ref[rows:, :]), spread_ref[:, :sensors]).astype(BF16)
    blank = jnp.zeros_like(linked)
    linked = jnp.concatenate([blank, linked], 1)
    spread = jnp.concatenate([spread_ref[...], linked, jnp.zeros_like(linked)], 0)
    packed = jnp.concatenate([packed_ref[:rows, :], own_packed_ref[:rows, :]], 1)
    both_scr[...] = (near_ref[...] + mm(packed, spread)).astype(BF16)
    bias = column(bias_ref[...])
    place = lax.axis_index("tm")
    hidden_ref[border_rows:, :] = hidden_old_ref[border_rows:, :]
    for t in range(DILATION_SIZE):
        earlier = border_ref[t]
        earlier = jnp.where(place > 0, earlier, jnp.zeros_like(earlier))
        window = jnp.concatenate([earlier, input_ref[t]], 0)
        preact = mm(turned_taps_ref[...], window) + bias
        gate_step(t, earlier, input_ref, preact, hidden_ref, slopes_ref, right_ref)
    mixing = mixing_ref[...]
    for t in range(steps):
        at = slice(t * chans, (t + 1) * chans)
        span = slice(t * sensors, (t + 1) * sensors)
        fields = jnp.concatenate(
            [grad_ref[at, :], both_scr[at, :sensors], both_scr[at, sensors:]], 0
        )
        back_hidden = mm(mixing, fields)
        back_hidden = jnp.concatenate([back_hidden, back_hidden], 0)
        slopes = slopes_ref[t] if t < DILATION_SIZE else slopes_old_ref[t]
        back_pre = (back_hidden * slopes).astype(BF16)
        back_ref[t] = back_pre
        left_scr[:wide, span] = back_pre
        left_scr[wide:, span] = fields
    ones = wide + 16
    conv = mm_nt(right_old_ref[:ones, border_span:], left_scr[: wide + chans, border_span:])
    conv = conv + mm_nt(right_ref[:ones, :], left_scr[: wide + chans, :border_span])
    mixes = mm_nt(left_scr[wide:, border_span:], right_old_ref[ones:, border_span:])
    mixes = mixes + mm_nt(left_scr[wide:, :border_span], right_ref[ones:, :])
    sums = conv[wide : wide + 8]
    conv = conv[:wide, :wide]
    zero, first, second = [mixes[k * chans : (k + 1) * chans] for k in range(3)]
    blank = jnp.zeros((chans, wide), F32)
    mixes = jnp.concatenate([fold(zero, first), fold(second, blank)], 0)
    mix_sums = jnp.concatenate([sums[:, wide:], blank[:8, :chans]], 1)
    conv = jnp.concatenate([conv, sums[:, :wide], blank[:8]], 0)
    mixes = jnp.concatenate([mixes, mix_sums, blank[:8]], 0)
    kept_ref[...] = jnp.where(core == 0, conv, mixes)
    given_ref[...] = jnp.where(core == 0, mixes, conv)


def boundary_rows(hidden, own, chosen):
    chosen_low, chosen_high = halves(chosen)
    hop = mm_nt(hidden, own).astype(BF16)
    return (mm(hidden, chosen_low) + mm(hop, chosen_high)).astype(BF16)


def early_kernel(back_ref, taps_ref, early_ref):
    for t in range(DILATION_SIZE):
        early_ref[t] = mm(taps_ref[0], back_ref[t]).astype(BF16)


def boundary_kernel(hidden_ref, own_ref, chosen_ref, boundary_ref):
    hidden = hidden_ref[: boundary_ref.shape[0], :]
    boundary_ref[...] = boundary_rows(hidden, own_ref[...], chosen_ref[...])


def outputs_kernel(
    input_ref,
    hidden_ref,
    own_boundary_ref,
    boundary_ref,
    packed_ref,
    own_ref,
    halo_ref,
    mix_ref,
    bias_ref,
    out_ref,
):
    steps, chans, sensors = input_ref.shape
    rows = steps * chans
    own = own_ref[...]
    halo = halo_ref[...]
    halo_low, halo_high = halves(halo)
    link = turned_link_matrix(packed_ref[rows:, :])
    hidden = hidden_ref[...]
    own_boundary = own_boundary_ref[...]
    boundary = boundary_ref[...]
    one = (mm_nt(hidden, own) + mm_nt(boundary, halo_low)).astype(BF16)
    far = (boundary.astype(F32) + mm_nt(own_boundary, link)).astype(BF16)
    two = (mm_nt(one, own) + mm_nt(far, halo_high)).astype(BF16)
    bias = column(bias_ref[...])
    for t in range(steps):
        at = slice(t * chans, (t + 1) * chans)
        mixed = mm(mix_ref[0], hidden[at]) + mm(mix_ref[1], one[at]) + mm(mix_ref[2], two[at])
        out_ref[t] = (mixed + bias + input_ref[t].astype(F32)).astype(BF16)


def input_grad_kernel(grad_ref, back_ref, early_ref, taps_ref, out_ref):
    steps, chans, sensors = out_ref.shape
    has_later = lax.axis_index("tm") < lax.axis_size("tm") - 1
    taps = jnp.concatenate([taps_ref[0], taps_ref[1]], 1)
    for t in range(steps):
        at = slice(t * chans, (t + 1) * chans)
        later = t + DILATION_SIZE
        total = grad_ref[at, :].astype(F32)
        if later < steps:
            total = total + mm(taps, jnp.concatenate([back_ref[later], back_ref[t]], 0))
        else:
            early = early_ref[later - steps].astype(F32)
            early = jnp.where(has_later, early, jnp.zeros_like(early))
            total = total + mm(taps_ref[1], back_ref[t]) + early
        out_ref[t] = total.astype(BF16)


def final_kernel(scale, kept_ref, other_ref, conv_w_ref, conv_b_ref, mix_w_ref, mix_b_ref):
    core = lax.axis_index("dp") % 2
    kept = kept_ref[...] * scale
    other = other_ref[...] * scale
    conv = jnp.where(core == 0, kept, other)
    mixes = jnp.where(core == 0, other, kept)
    chans = conv.shape[1] // 2
    wide = 2 * chans
    conv_w_ref[0] = conv[:chans]
    conv_w_ref[1] = conv[chans:wide]
    mix_w_ref[0] = mixes[:chans, :chans]
    mix_w_ref[1] = pltpu.roll(mixes[:chans], chans, 1)[:, :chans]
    mix_w_ref[2] = mixes[chans:wide, :chans]
    conv_b_ref[...] = (conv[wide : wide + 8] + conv[wide + 8 :])[:1]
    mix_b_ref[...] = (mixes[wide : wide + 8] + mixes[wide + 8 :])[:1, :chans]


VMEM = pl.BlockSpec(memory_space=pltpu.VMEM)
HBM = pl.BlockSpec(memory_space=pltpu.HBM)
DMA = pltpu.SemaphoreType.DMA


def call(kernel, name, in_specs, out_shape, args, scratch=(), micros=1.0):
    args = [
        pltpu.with_memory_space_constraint(arg, pltpu.HBM) if spec is HBM else arg
        for spec, arg in zip(in_specs, args)
    ]
    return pl.pallas_call(
        kernel,
        out_shape=out_shape,
        in_specs=in_specs,
        out_specs=jax.tree.map(lambda _: VMEM, out_shape),
        scratch_shapes=list(scratch),
        compiler_params=pltpu.CompilerParams(vmem_limit_bytes=VMEM_BYTES),
        cost_estimate=pl.CostEstimate(
            flops=0, bytes_accessed=int(micros * 3_600_000), transcendentals=0
        ),
        name=name,
    )(*args)


def swap(value, axis, bit):
    count = lax.axis_size(axis)
    return lax.ppermute(value, axis, [(source, source ^ bit) for source in range(count)])


def shift(value, axis, steps):
    count = lax.axis_size(axis)
    return lax.ppermute(value, axis, [(source, (source + steps) % count) for source in range(count)])


def flip(value, mask):
    sizes = [lax.axis_size(axis) for axis in AXES]
    places = list(itertools.product(*[range(size) for size in sizes]))
    index = {place: number for number, place in enumerate(places)}
    pairs = [
        (index[place], index[tuple(part ^ bit for part, bit in zip(place, mask))])
        for place in places
    ]
    return lax.ppermute(value, AXES, pairs)


def groups():
    dp, space, tm = [bits(lax.axis_size(axis)) for axis in AXES]
    first = [(bit, 0, 0) for bit in dp[1:]]
    second = [(0, bit, 0) for bit in space]
    third = [(0, 0, bit) for bit in tm]
    orders = ((2, 1, 0), (1, 0, 2))
    return [closure(masks, order) for masks, order in zip((first + second, third), orders) if masks]


def closure(masks, order):
    found = [(0, 0, 0)]
    for mask in masks:
        found = found + [tuple(left ^ right for left, right in zip(item, mask)) for item in found]
    found = found[1:]
    return [found[place] for place in order] if len(found) == len(order) else found


def bits(count):
    return [1 << place for place in range(count.bit_length() - 1)]


def to_bf16(value):
    return lax.reduce_precision(value, exponent_bits=8, mantissa_bits=7)


def round_sums(sums):
    end = sums.shape[0]
    high = sums[end - 16 : end - 8]
    rest = jnp.pad(high - to_bf16(high), ((end - 8, 0), (0, 0)))
    return to_bf16(sums + rest)


def after(value, *earlier):
    return lax.optimization_barrier((value, *earlier))[0]


def pair_body(inputs, grad_out, conv_w, conv_b, mix_w, mix_b, adj_tiles, tile_cols, send_rows, counts):
    sample_input = inputs[0]
    sample_grad = grad_out[0]
    steps, chans, sensors = sample_input.shape
    rows = steps * chans
    half_rows = rows // 2
    wide = 2 * chans
    shape = jax.ShapeDtypeStruct
    border_rows = DILATION_SIZE * chans
    grad_flat = sample_grad.reshape(rows, sensors)
    taps = jnp.transpose(conv_w, (0, 2, 1))
    packed, own, halo, chosen, grad, tail = call(
        prepare_kernel,
        "prepare",
        [HBM] * 6,
        (
            shape((rows + chans // 2, wide), BF16),
            shape((sensors, sensors), BF16),
            shape((sensors, wide), BF16),
            shape((sensors, wide), BF16),
            shape((rows, sensors), BF16),
            shape((DILATION_SIZE, chans, sensors), BF16),
        ),
        (tile_cols, counts, send_rows, adj_tiles, grad_flat, sample_input),
        scratch=(
            pltpu.VMEM(adj_tiles.shape, BF16),
            pltpu.SMEM(tile_cols.shape, jnp.int32),
            pltpu.SMEM(counts.shape, jnp.int32),
            pltpu.VMEM(send_rows.shape, jnp.int32),
            DMA((7,)),
        ),
        micros=2.0,
    )
    packed_far = swap(packed, "space", 1)
    border = shift(tail, "tm", 1)
    hidden_late, slopes, right, near, spread, kept_input, kept_taps, turned_taps, bias, mix, mixing, mix_bias = call(
        forward_kernel,
        "forward",
        [HBM] * 5 + [VMEM] * 3,
        (
            shape((rows, sensors), BF16),
            shape((steps, wide, sensors), F32),
            shape((2 * wide + 16, steps * sensors), BF16),
            shape((rows, 2 * sensors), F32),
            shape((wide, 2 * sensors), BF16),
            shape(sample_input.shape, BF16),
            shape(taps.shape, BF16),
            shape((wide, wide), BF16),
            shape((1, wide), F32),
            shape(mix_w.shape, BF16),
            shape((chans, 3 * chans), BF16),
            shape((1, chans), F32),
        ),
        (
            sample_input,
            taps,
            conv_b.reshape(1, wide),
            mix_w,
            mix_b.reshape(1, chans),
            grad,
            own,
            chosen,
        ),
        scratch=(DMA((5,)),),
        micros=1.5,
    )
    border_span = DILATION_SIZE * sensors
    kept, given, back, hidden = call(
        backward_kernel,
        "backward",
        [VMEM] * 13,
        (
            shape((wide + 16, wide), F32),
            shape((wide + 16, wide), F32),
            shape((steps, wide, sensors), BF16),
            shape((rows, sensors), BF16),
        ),
        (
            grad,
            packed,
            packed_far,
            border,
            near,
            spread,
            kept_input,
            turned_taps,
            bias,
            mixing,
            hidden_late,
            slopes,
            right,
        ),
        scratch=(
            pltpu.VMEM((wide + 3 * chans, steps * sensors), BF16),
            pltpu.VMEM((rows, 2 * sensors), BF16),
            pltpu.VMEM((DILATION_SIZE, wide, sensors), F32),
            pltpu.VMEM((2 * wide + 16, border_span), BF16),
        ),
        micros=2.0,
    )
    total = kept + swap(given, "dp", 1)
    rounds = groups()
    early = call(
        early_kernel,
        "early",
        [VMEM] * 2,
        shape((DILATION_SIZE, chans, sensors), BF16),
        (back, kept_taps),
        micros=0.3,
    )
    early_far = shift(early, "tm", -1)
    boundary_first = call(
        boundary_kernel,
        "boundary",
        [VMEM] * 3,
        shape((rows, wide), BF16),
        (hidden, own, chosen),
        micros=0.3,
    )
    first_far = swap(boundary_first, "space", 1)
    outputs = call(
        outputs_kernel,
        "outputs",
        [VMEM] * 9,
        shape(sample_input.shape, BF16),
        (
            kept_input,
            hidden,
            boundary_first,
            first_far,
            packed_far,
            own,
            halo,
            mix,
            mix_bias,
        ),
        micros=2.0,
    )
    grad_inputs = call(
        input_grad_kernel,
        "input_grad",
        [VMEM] * 4,
        shape(sample_grad.shape, BF16),
        (grad, back, early_far, kept_taps),
        micros=1.2,
    )
    ready = {-2: (first_far,), -1: (outputs, grad_inputs)}
    for index, group in enumerate(rounds):
        rounded = round_sums(total)
        sent = rounded.astype(BF16)
        parts = [rounded] + [flip(sent, mask).astype(F32) for mask in group]
        parts[1] = after(parts[1], *ready.get(index - len(rounds), ()))
        while len(parts) > 1:
            parts = [left + right for left, right in zip(parts[::2], parts[1::2])]
        total = parts[0]
    total_far = swap(total, "dp", 1)
    cell_count = (
        inputs.shape[0]
        * steps
        * sensors
        * lax.axis_size("dp")
        * lax.axis_size("space")
        * lax.axis_size("tm")
    )
    scale = 1.0 / math.sqrt(cell_count)
    grad_taps, grad_conv_b, grad_mix_w, grad_mix_b = call(
        functools.partial(final_kernel, scale),
        "final",
        [VMEM] * 2,
        (
            shape((2, chans, wide), F32),
            shape((1, wide), F32),
            shape((3, chans, chans), F32),
            shape((1, chans), F32),
        ),
        (total, total_far),
    )
    return (
        outputs[None],
        grad_inputs[None],
        jnp.transpose(grad_taps, (0, 2, 1)),
        grad_conv_b.reshape(wide),
        grad_mix_w,
        grad_mix_b.reshape(chans),
    )


def power_of_two(count):
    return count & (count - 1) == 0


def body(inputs, grad_out, conv_w, conv_b, mix_w, mix_b, adj_tiles, tile_cols, send_rows, counts):
    tile = adj_tiles.shape[2]
    axes = [lax.axis_size(axis) for axis in ("dp", "space", "tm")]
    fits = (
        axes[1] == 2
        and axes[0] % 2 == 0
        and all(power_of_two(count) for count in axes)
        and inputs.shape[0] == 1
        and inputs.shape[3] == 2 * tile
        and inputs.shape[2] * 2 == tile
        and send_rows.shape[2] * 2 == tile
    )
    chosen = pair_body if fits else general_body
    return chosen(
        inputs, grad_out, conv_w, conv_b, mix_w, mix_b, adj_tiles, tile_cols, send_rows, counts
    )


def solution(mesh):
    in_specs = (
        P("dp", "tm", None, "space"),
        P("dp", "tm", None, "space"),
        P(),
        P(),
        P(),
        P(),
        P("space", None, None, None),
        P("space", None),
        P("space", None, None),
        P("space", None),
    )
    out_specs = (P("dp", "tm", None, "space"), P("dp", "tm", None, "space"), P(), P(), P(), P())
    return jax.shard_map(body, mesh=mesh, in_specs=in_specs, out_specs=out_specs, check_vma=False)
```

```python
import functools
import itertools
import math

import jax
import jax.numpy as jnp
from jax import lax
from jax.experimental import pallas as pl
from jax.experimental.pallas import tpu as pltpu
from jax.sharding import PartitionSpec as P

DILATION_SIZE = 2


def from_behind(value, axis, steps):
    count = lax.axis_size(axis)
    leading, last = (max(0, -steps), min(count, count - steps))
    return lax.ppermute(value, axis, [(source, source + steps) for source in range(leading, last)])


def slot_mask(counts, slot_count, dtype):
    slots = lax.broadcasted_iota(jnp.int32, (counts.shape[1], slot_count), 1)
    return (slots < counts[0][:, None]).astype(dtype)


def pack_rows(field, send_rows, live_slots):
    picked = field[:, :, send_rows[0]] * live_slots
    return picked.reshape(field.shape[0], field.shape[1], -1)


def tile_product(extended, adj_tiles, tile_cols):
    timestep_count, chan_count = (extended.shape[0], extended.shape[1])
    blocks = extended.reshape(timestep_count, chan_count, -1, adj_tiles.shape[2])
    picked = blocks[:, :, tile_cols]
    return jnp.einsum("tcrkj,rkij->tcri", picked, adj_tiles, preferred_element_type=jnp.float32)


def forward_start(field, send_rows, live_slots):
    packed = pack_rows(field, send_rows, live_slots)
    own_part = None
    return (packed, own_part)


def forward_finish(field, received, adj_tiles, tile_cols):
    total = tile_product(jnp.concatenate([field, received], 2), adj_tiles, tile_cols)
    return total.reshape(field.shape).astype(jnp.bfloat16)


def back_start(grad, adj_tiles, tile_cols, send_rows):
    timestep_count, chan_count, sensor_count = grad.shape
    tile_size = adj_tiles.shape[2]
    row_blocks = sensor_count // tile_size
    half_slots = tile_cols.shape[1] // 2
    halo_blocks = send_rows.shape[1] * send_rows.shape[2] // tile_size
    blocks = grad.reshape(timestep_count, chan_count, row_blocks, tile_size)
    remote_terms = jnp.einsum(
        "tcri,rkij->tcrkj", blocks, adj_tiles[:, half_slots:], preferred_element_type=jnp.float32
    )
    remote_sums = jnp.zeros((timestep_count, chan_count, halo_blocks, tile_size), jnp.float32)
    remote_sums = remote_sums.at[:, :, tile_cols[:, half_slots:] - row_blocks].add(remote_terms)
    return remote_sums.reshape(timestep_count, chan_count, -1).astype(jnp.bfloat16)


def back_finish(grad, returned, adj_tiles, tile_cols, send_rows, live_slots):
    timestep_count, chan_count, sensor_count = grad.shape
    tile_size = adj_tiles.shape[2]
    row_blocks = sensor_count // tile_size
    half_slots = tile_cols.shape[1] // 2
    blocks = grad.reshape(timestep_count, chan_count, row_blocks, tile_size)
    own_terms = jnp.einsum(
        "tcri,rkij->tcrkj", blocks, adj_tiles[:, :half_slots], preferred_element_type=jnp.float32
    )
    total = jnp.zeros((timestep_count, chan_count, row_blocks, tile_size), jnp.float32)
    total = total.at[:, :, tile_cols[:, :half_slots]].add(own_terms).reshape(grad.shape)
    returned = returned.reshape(
        timestep_count, chan_count, send_rows.shape[1], send_rows.shape[2]
    ).astype(jnp.float32)
    return total.at[:, :, send_rows[0]].add(returned * live_slots.astype(jnp.float32))


def mixing_grads(sample_grad, fields):
    grad_mix_w = jnp.stack(
        [
            jnp.einsum("ton,tcn->oc", sample_grad, item, preferred_element_type=jnp.float32)
            for item in fields
        ]
    )
    grad_mix_b = jnp.sum(sample_grad.astype(jnp.float32), axis=(0, 2))
    return (grad_mix_w, grad_mix_b)


def general_body(inputs, grad_out, conv_w, conv_b, mix_w, mix_b, adj_tiles, tile_cols, send_rows, counts):
    sample_input = inputs[0]
    sample_grad = grad_out[0]
    timestep_count, chan_count, sensor_count = sample_input.shape
    live_slots = slot_mask(counts, send_rows.shape[2], jnp.bfloat16)
    prior_border_slice = from_behind(sample_input[timestep_count - DILATION_SIZE :], "tm", 1)
    preceding_window = jnp.concatenate(
        [prior_border_slice, sample_input[: timestep_count - DILATION_SIZE]], 0
    )
    preact = jnp.einsum("oc,tcn->ton", conv_w[1], sample_input, preferred_element_type=jnp.float32)
    preact = preact + jnp.einsum(
        "oc,tcn->ton", conv_w[0], preceding_window, preferred_element_type=jnp.float32
    )
    preact = preact + conv_b[None, :, None]
    filtered = jnp.tanh(preact[:, :chan_count])
    gating = jax.nn.sigmoid(preact[:, chan_count:])
    hidden = (filtered * gating).astype(jnp.bfloat16)
    grad_float = sample_grad.astype(jnp.float32)
    packed_one, early_one = forward_start(hidden, send_rows, live_slots)
    received_one = lax.all_to_all(packed_one, "space", split_axis=2, concat_axis=2, tiled=True)
    hop_one = forward_finish(hidden, received_one, adj_tiles, tile_cols)
    packed_two, early_two = forward_start(hop_one, send_rows, live_slots)
    received_two = lax.all_to_all(packed_two, "space", split_axis=2, concat_axis=2, tiled=True)
    hop_two = forward_finish(hop_one, received_two, adj_tiles, tile_cols)
    fields = (hidden, hop_one, hop_two)
    grad_mix_w, grad_mix_b = mixing_grads(sample_grad, fields)
    back_two = jnp.einsum(
        "oc,ton->tcn", mix_w[2], sample_grad, preferred_element_type=jnp.float32
    ).astype(jnp.bfloat16)
    returned_two = lax.all_to_all(
        back_start(back_two, adj_tiles, tile_cols, send_rows),
        "space",
        split_axis=2,
        concat_axis=2,
        tiled=True,
    )
    back_one = jnp.einsum("oc,ton->tcn", mix_w[1], sample_grad, preferred_element_type=jnp.float32)
    back_one = (
        back_one + back_finish(back_two, returned_two, adj_tiles, tile_cols, send_rows, live_slots)
    ).astype(jnp.bfloat16)
    returned_one = lax.all_to_all(
        back_start(back_one, adj_tiles, tile_cols, send_rows),
        "space",
        split_axis=2,
        concat_axis=2,
        tiled=True,
    )
    back_hidden = jnp.einsum(
        "oc,ton->tcn", mix_w[0], sample_grad, preferred_element_type=jnp.float32
    )
    back_hidden = back_hidden + back_finish(
        back_one, returned_one, adj_tiles, tile_cols, send_rows, live_slots
    )
    mixed = sample_input.astype(jnp.float32) + mix_b[None, :, None]
    for index in range(3):
        mixed = mixed + jnp.einsum(
            "oc,tcn->ton", mix_w[index], fields[index], preferred_element_type=jnp.float32
        )
    outputs = mixed.astype(jnp.bfloat16)[None]
    grad_filter = back_hidden * (1.0 - filtered * filtered) * gating
    grad_gate = back_hidden * filtered * gating * (1.0 - gating)
    backward_preactivation = jnp.concatenate([grad_filter, grad_gate], 1).astype(jnp.bfloat16)
    next_border_slice = from_behind(backward_preactivation[:DILATION_SIZE], "tm", -1)
    following_window = jnp.concatenate(
        [backward_preactivation[DILATION_SIZE:], next_border_slice], 0
    )
    grad_inputs = grad_float + jnp.einsum(
        "oc,ton->tcn", conv_w[1], backward_preactivation, preferred_element_type=jnp.float32
    )
    grad_inputs = grad_inputs + jnp.einsum(
        "oc,ton->tcn", conv_w[0], following_window, preferred_element_type=jnp.float32
    )
    grad_inputs = grad_inputs.astype(jnp.bfloat16)[None]
    grad_conv_w = jnp.stack(
        [
            jnp.einsum(
                "ton,tcn->oc",
                backward_preactivation,
                preceding_window,
                preferred_element_type=jnp.float32,
            ),
            jnp.einsum(
                "ton,tcn->oc",
                backward_preactivation,
                sample_input,
                preferred_element_type=jnp.float32,
            ),
        ]
    )
    grad_conv_b = jnp.sum(backward_preactivation.astype(jnp.float32), axis=(0, 2))
    grad_conv_w, grad_conv_b, grad_mix_w, grad_mix_b = lax.psum(
        (grad_conv_w, grad_conv_b, grad_mix_w, grad_mix_b), ("dp", "space", "tm")
    )
    cell_count = (
        inputs.shape[0]
        * timestep_count
        * sensor_count
        * lax.axis_size("dp")
        * lax.axis_size("space")
        * lax.axis_size("tm")
    )
    scale = 1.0 / math.sqrt(cell_count)
    return (
        outputs,
        grad_inputs,
        grad_conv_w * scale,
        grad_conv_b * scale,
        grad_mix_w * scale,
        grad_mix_b * scale,
    )


BF16 = jnp.bfloat16
AXES = ("dp", "space", "tm")
F32 = jnp.float32
NT = (((1,), (1,)), ((), ()))
VMEM_BYTES = 24 * 1024 * 1024


def mm(left, right):
    return jnp.dot(left, right, preferred_element_type=F32)


def mm_nt(left, right):
    return lax.dot_general(left, right, NT, preferred_element_type=F32)


def upper_lanes(shape):
    return lax.broadcasted_iota(jnp.int32, shape, 1) >= shape[1] // 2


def halves(matrix):
    upper = upper_lanes(matrix.shape)
    zero = jnp.zeros_like(matrix)
    return jnp.where(upper, zero, matrix), jnp.where(upper, matrix, zero)


def fold(first, second):
    return jnp.where(upper_lanes(first.shape), second, first)


def times_halves(left, right):
    half = left.shape[0] // 2
    return fold(mm(left[:half], right), mm(left[half:], right))


def link_rows(packed):
    packed = packed.astype(F32)
    turned = pltpu.roll(packed, packed.shape[1] // 2, 1)
    return jnp.concatenate([halves(packed)[0], halves(turned)[0]], 0).astype(BF16)


def column(row):
    size = row.shape[1]
    first = lax.broadcasted_iota(jnp.int32, (size, size), 0)
    second = lax.broadcasted_iota(jnp.int32, (size, size), 1)
    return jnp.sum(jnp.where(first == second, row, 0.0), axis=1, keepdims=True)


def fetch(pairs, sems):
    copies = [
        pltpu.make_async_copy(source, target, sems.at[index])
        for index, (source, target) in enumerate(pairs)
    ]
    for copy in copies:
        copy.start()
    return copies


def prepare_kernel(
    cols_hbm,
    counts_hbm,
    rows_hbm,
    adj_hbm,
    grad_hbm,
    input_hbm,
    packed_ref,
    own_ref,
    halo_ref,
    chosen_ref,
    grad_ref,
    tail_ref,
    adj_ref,
    cols_ref,
    counts_ref,
    rows_ref,
    sems,
):
    row_blocks, slots, tile = adj_ref.shape[:3]
    own_slots = slots // 2
    steps = input_hbm.shape[0]
    copies = fetch(
        [
            (adj_hbm.at[:, pl.ds(own_slots, own_slots)], adj_ref.at[:, pl.ds(own_slots, own_slots)]),
            (cols_hbm, cols_ref),
            (counts_hbm, counts_ref),
            (rows_hbm, rows_ref),
            (adj_hbm.at[:, pl.ds(0, own_slots)], adj_ref.at[:, pl.ds(0, own_slots)]),
            (grad_hbm, grad_ref),
            (input_hbm.at[pl.ds(steps - DILATION_SIZE, DILATION_SIZE)], tail_ref),
        ],
        sems,
    )
    other = 1 - lax.axis_index("space")
    sensors = grad_ref.shape[1]
    rows_count = grad_ref.shape[0]
    slot_count = rows_ref.shape[2]
    upper = upper_lanes((tile, tile)).astype(jnp.int32)
    for copy in copies[:5]:
        copy.wait()
    for r in range(row_blocks):
        far = adj_ref[r, own_slots].astype(F32)
        for k in range(own_slots + 1, slots):
            far = far + adj_ref[r, k].astype(F32)
        far = jnp.where(upper == other, far, pltpu.roll(far, tile // 2, 1))
        halo_ref[r * tile : (r + 1) * tile, :] = far.astype(BF16)
    rows = rows_ref[0, pl.ds(other, 1), :]
    rows = jnp.concatenate([rows, rows], 1)
    lanes = lax.broadcasted_iota(jnp.int32, (1, 2 * slot_count), 1)
    place = lanes - jnp.where(lanes >= slot_count, slot_count, 0)
    rows = jnp.where(place < counts_ref[0, other], rows, -1)
    sensor = lax.broadcasted_iota(jnp.int32, (sensors, 2 * slot_count), 0)
    chosen = jnp.where(sensor == rows, 1.0, 0.0).astype(F32)
    chosen_ref[...] = chosen.astype(BF16)
    turned = jnp.transpose(chosen)[:slot_count].astype(BF16)
    halo = halo_ref[...]
    packed_ref[rows_count:, :] = times_halves(turned, halo).astype(BF16)
    for r in range(row_blocks):
        sums = [jnp.zeros((tile, tile), F32), jnp.zeros((tile, tile), F32)]
        for k in range(own_slots):
            item = adj_ref[r, k].astype(F32)
            for block in range(2):
                share = jnp.where(cols_ref[r, k] == block, 1.0, 0.0).astype(F32)
                sums[block] = sums[block] + item * share
        own_ref[r * tile : (r + 1) * tile, :] = jnp.concatenate(sums, 1).astype(BF16)
    both = fold(halo, mm(own_ref[...], halo).astype(BF16))
    copies[5].wait()
    packed_ref[:rows_count, :] = mm(grad_ref[...], both).astype(BF16)
    copies[6].wait()


def gate_step(t, earlier, input_ref, preact, hidden_ref, slopes_ref, right_ref):
    steps, chans, sensors = input_ref.shape
    at = slice(t * chans, (t + 1) * chans)
    span = slice(t * sensors, (t + 1) * sensors)
    filtered = jnp.tanh(preact[:chans])
    gating = 0.5 * jnp.tanh(0.5 * preact[chans:]) + 0.5
    product = filtered * gating
    hidden = product.astype(BF16)
    hidden_ref[at, :] = hidden
    slopes_ref[t, :chans] = (1.0 - filtered * filtered) * gating
    slopes_ref[t, chans:] = product * (1.0 - gating)
    right_ref[:chans, span] = earlier
    right_ref[chans : 2 * chans, span] = input_ref[t]
    right_ref[2 * chans : 2 * chans + 16, span] = jnp.ones((16, sensors), BF16)
    right_ref[2 * chans + 16 : 3 * chans + 16, span] = hidden
    right_ref[3 * chans + 16 :, span] = hidden


def forward_kernel(
    input_hbm,
    conv_w_hbm,
    conv_b_hbm,
    mix_w_hbm,
    mix_b_hbm,
    grad_ref,
    own_ref,
    chosen_ref,
    hidden_ref,
    slopes_ref,
    right_ref,
    near_ref,
    spread_ref,
    input_ref,
    taps_ref,
    turned_taps_ref,
    bias_ref,
    mix_ref,
    mixing_ref,
    mix_bias_ref,
    mix_wide_ref,
    sems,
):
    copies = fetch(
        [
            (input_hbm, input_ref),
            (conv_w_hbm, taps_ref),
            (conv_b_hbm, bias_ref),
            (mix_w_hbm, mix_ref),
            (mix_b_hbm, mix_bias_ref),
        ],
        sems,
    )
    steps, chans, sensors = input_ref.shape
    own = own_ref[...]
    near = mm(grad_ref[...], own)
    near_ref[:, :sensors] = near
    near_ref[:, sensors:] = mm(near.astype(BF16), own)
    turned = jnp.transpose(chosen_ref[...].astype(F32)).astype(BF16)
    slot_count = turned.shape[0] // 2
    spread_ref[:, :sensors] = jnp.where(
        lax.broadcasted_iota(jnp.int32, turned.shape, 0) < slot_count,
        turned,
        jnp.zeros_like(turned),
    )
    spread_ref[:slot_count, sensors:] = mm(turned[:slot_count], own).astype(BF16)
    spread_ref[slot_count:, sensors:] = turned[slot_count:]
    for copy in copies:
        copy.wait()
    mixing = jnp.transpose(mix_ref[...].reshape(3 * chans, chans).astype(F32))
    mixing_ref[...] = mixing.astype(BF16)
    mix_wide_ref[...] = jnp.concatenate([mix_ref[0], mix_ref[1], mix_ref[2]], 1)
    taps = taps_ref[...].reshape(2 * chans, 2 * chans).astype(F32)
    taps = jnp.transpose(taps).astype(BF16)
    turned_taps_ref[...] = taps
    bias = column(bias_ref[...])
    for t in range(DILATION_SIZE, steps):
        earlier = input_ref[t - DILATION_SIZE]
        preact = mm(taps, jnp.concatenate([earlier, input_ref[t]], 0)) + bias
        gate_step(t, earlier, input_ref, preact, hidden_ref, slopes_ref, right_ref)


def backward_kernel(
    grad_ref,
    own_packed_ref,
    packed_ref,
    border_ref,
    near_ref,
    spread_ref,
    input_ref,
    turned_taps_ref,
    bias_ref,
    mixing_ref,
    hidden_old_ref,
    slopes_old_ref,
    right_old_ref,
    kept_ref,
    given_ref,
    back_ref,
    hidden_ref,
    left_scr,
    both_scr,
    slopes_ref,
    right_ref,
):
    steps, wide, sensors = back_ref.shape
    chans = wide // 2
    rows = steps * chans
    border_rows = DILATION_SIZE * chans
    border_span = DILATION_SIZE * sensors
    core = lax.axis_index("dp") % 2
    linked = mm(link_rows(packed_ref[rows:, :]), spread_ref[:, :sensors]).astype(BF16)
    blank = jnp.zeros_like(linked)
    linked = jnp.concatenate([blank, linked], 1)
    spread = jnp.concatenate([spread_ref[...], linked, jnp.zeros_like(linked)], 0)
    packed = jnp.concatenate([packed_ref[:rows, :], own_packed_ref[:rows, :]], 1)
    both_scr[...] = (near_ref[...] + mm(packed, spread)).astype(BF16)
    bias = column(bias_ref[...])
    place = lax.axis_index("tm")
    hidden_ref[border_rows:, :] = hidden_old_ref[border_rows:, :]
    for t in range(DILATION_SIZE):
        earlier = border_ref[t]
        earlier = jnp.where(place > 0, earlier, jnp.zeros_like(earlier))
        window = jnp.concatenate([earlier, input_ref[t]], 0)
        preact = mm(turned_taps_ref[...], window) + bias
        gate_step(t, earlier, input_ref, preact, hidden_ref, slopes_ref, right_ref)
    mixing = mixing_ref[...]
    for t in range(steps):
        at = slice(t * chans, (t + 1) * chans)
        span = slice(t * sensors, (t + 1) * sensors)
        fields = jnp.concatenate(
            [grad_ref[at, :], both_scr[at, :sensors], both_scr[at, sensors:]], 0
        )
        back_hidden = mm(mixing, fields)
        back_hidden = jnp.concatenate([back_hidden, back_hidden], 0)
        slopes = slopes_ref[t] if t < DILATION_SIZE else slopes_old_ref[t]
        back_pre = (back_hidden * slopes).astype(BF16)
        back_ref[t] = back_pre
        left_scr[:wide, span] = back_pre
        left_scr[wide:, span] = fields
    ones = wide + 16
    conv = mm_nt(right_old_ref[:ones, border_span:], left_scr[: wide + chans, border_span:])
    conv = conv + mm_nt(right_ref[:ones, :], left_scr[: wide + chans, :border_span])
    mixes = mm_nt(left_scr[wide:, border_span:], right_old_ref[ones:, border_span:])
    mixes = mixes + mm_nt(left_scr[wide:, :border_span], right_ref[ones:, :])
    sums = conv[wide : wide + 8]
    conv = conv[:wide, :wide]
    zero, first, second = [mixes[k * chans : (k + 1) * chans] for k in range(3)]
    half = chans // 2
    blank = jnp.zeros((8, wide), F32)
    mix_sums = jnp.concatenate([sums[:, wide:], blank[:, :chans]], 1)
    upper_rows = lax.broadcasted_iota(jnp.int32, blank.shape, 0) >= 4
    biases = jnp.where(upper_rows, mix_sums, sums[:, :wide])
    packed = jnp.concatenate(
        [conv, fold(zero, first), fold(second[:half], second[half:]), biases, blank], 0
    )
    cut = packed.shape[0] // 2
    kept_ref[...] = jnp.where(core == 0, packed[:cut], packed[cut:])
    given_ref[...] = jnp.where(core == 0, packed[cut:], packed[:cut])


def boundary_rows(hidden, own, chosen):
    chosen_low, chosen_high = halves(chosen)
    hop = mm_nt(hidden, own).astype(BF16)
    return (mm(hidden, chosen_low) + mm(hop, chosen_high)).astype(BF16)


def early_kernel(back_ref, taps_ref, early_ref):
    for t in range(DILATION_SIZE):
        early_ref[t] = mm(taps_ref[0], back_ref[t]).astype(BF16)


def boundary_kernel(hidden_ref, own_ref, chosen_ref, boundary_ref):
    hidden = hidden_ref[: boundary_ref.shape[0], :]
    boundary_ref[...] = boundary_rows(hidden, own_ref[...], chosen_ref[...])


def hops_kernel(hidden_ref, packed_ref, own_ref, halo_ref, base_ref, spread_ref):
    sensors = own_ref.shape[0]
    slots = halo_ref.shape[1] // 2
    rows = hidden_ref.shape[0]
    own = own_ref[...]
    one = mm_nt(hidden_ref[...], own)
    base_ref[:, :sensors] = one
    base_ref[:, sensors:] = mm_nt(one.astype(BF16), own)
    halo = halo_ref[...]
    link = link_rows(packed_ref[rows:, :])
    link = jnp.concatenate([link, jnp.zeros_like(link)], 0)
    turned = jnp.transpose(jnp.concatenate([halo.astype(F32), mm(halo, link)], 1)).astype(BF16)
    blank = jnp.zeros((slots, sensors), BF16)
    first = turned[:slots]
    spread_ref[:slots, :sensors] = first
    spread_ref[:slots, sensors:] = mm_nt(first, own).astype(BF16)
    for block in range(1, 4):
        at = slice(block * slots, (block + 1) * slots)
        spread_ref[at, :sensors] = blank
        spread_ref[at, sensors:] = turned[at] if block < 3 else blank


def finish_kernel(
    input_ref,
    hidden_ref,
    own_boundary_ref,
    boundary_ref,
    base_ref,
    spread_ref,
    mix_ref,
    bias_ref,
    grad_ref,
    back_ref,
    early_ref,
    taps_ref,
    out_hbm,
    grad_out_hbm,
    out_scr,
    grad_scr,
    both_scr,
    sems,
):
    steps, chans, sensors = input_ref.shape
    has_later = lax.axis_index("tm") < lax.axis_size("tm") - 1
    taps = jnp.concatenate([taps_ref[0], taps_ref[1]], 1)
    chunk = steps // 2
    copies = []

    def send(scratch, target, start):
        span = pl.ds(start, chunk)
        copy = pltpu.make_async_copy(scratch.at[span], target.at[span], sems.at[len(copies)])
        copy.start()
        copies.append(copy)

    for t in range(steps):
        at = slice(t * chans, (t + 1) * chans)
        later = t + DILATION_SIZE
        total = grad_ref[at, :].astype(F32)
        if later < steps:
            total = total + mm(taps, jnp.concatenate([back_ref[later], back_ref[t]], 0))
        else:
            early = early_ref[later - steps].astype(F32)
            early = jnp.where(has_later, early, jnp.zeros_like(early))
            total = total + mm(taps_ref[1], back_ref[t]) + early
        grad_scr[t] = total.astype(BF16)
        if (t + 1) % chunk == 0:
            send(grad_scr, grad_out_hbm, t + 1 - chunk)
    boundary = jnp.concatenate([boundary_ref[...], own_boundary_ref[...]], 1)
    both_scr[...] = (base_ref[...] + mm(boundary, spread_ref[...])).astype(BF16)
    bias = column(bias_ref[...])
    mix = mix_ref[...]
    for t in range(steps):
        at = slice(t * chans, (t + 1) * chans)
        fields = jnp.concatenate(
            [hidden_ref[at, :], both_scr[at, :sensors], both_scr[at, sensors:]], 0
        )
        out_scr[t] = (mm(mix, fields) + bias + input_ref[t].astype(F32)).astype(BF16)
        if (t + 1) % chunk == 0:
            send(out_scr, out_hbm, t + 1 - chunk)
    for copy in copies:
        copy.wait()


def final_kernel(scale, kept_ref, other_ref, conv_w_ref, conv_b_ref, mix_w_ref, mix_b_ref):
    core = lax.axis_index("dp") % 2
    kept = kept_ref[...] * scale
    other = other_ref[...] * scale
    lower = jnp.where(core == 0, kept, other)
    upper = jnp.where(core == 0, other, kept)
    chans, wide = conv_w_ref.shape[1:]
    half = chans // 2
    start = wide - lower.shape[0]
    conv_w_ref[0] = lower[:chans]
    conv_w_ref[1] = jnp.concatenate([lower[chans:], upper[:start]], 0)
    first = upper[start : start + chans]
    second = upper[start + chans : start + chans + half]
    mix_w_ref[0] = first[:, :chans]
    mix_w_ref[1] = pltpu.roll(first, chans, 1)[:, :chans]
    mix_w_ref[2] = jnp.concatenate([second, pltpu.roll(second, chans, 1)], 0)[:, :chans]
    start = start + chans + half
    biases = upper[start : start + 8] + upper[start + 8 :]
    conv_b_ref[...] = biases[:1]
    mix_b_ref[...] = biases[4:5, :chans]


VMEM = pl.BlockSpec(memory_space=pltpu.VMEM)
HBM = pl.BlockSpec(memory_space=pltpu.HBM)
DMA = pltpu.SemaphoreType.DMA


def call(kernel, name, in_specs, out_shape, args, scratch=(), micros=1.0, space=None):
    args = [
        pltpu.with_memory_space_constraint(arg, pltpu.HBM) if spec is HBM else arg
        for spec, arg in zip(in_specs, args)
    ]
    return pl.pallas_call(
        kernel,
        out_shape=out_shape,
        in_specs=in_specs,
        out_specs=jax.tree.map(lambda _: space or VMEM, out_shape),
        scratch_shapes=list(scratch),
        compiler_params=pltpu.CompilerParams(vmem_limit_bytes=VMEM_BYTES),
        cost_estimate=pl.CostEstimate(
            flops=0, bytes_accessed=int(micros * 3_600_000), transcendentals=0
        ),
        name=name,
    )(*args)


def swap(value, axis, bit):
    count = lax.axis_size(axis)
    return lax.ppermute(value, axis, [(source, source ^ bit) for source in range(count)])


def shift(value, axis, steps):
    count = lax.axis_size(axis)
    return lax.ppermute(value, axis, [(source, (source + steps) % count) for source in range(count)])


def flip(value, mask):
    sizes = [lax.axis_size(axis) for axis in AXES]
    places = list(itertools.product(*[range(size) for size in sizes]))
    index = {place: number for number, place in enumerate(places)}
    pairs = [
        (index[place], index[tuple(part ^ bit for part, bit in zip(place, mask))])
        for place in places
    ]
    return lax.ppermute(value, AXES, pairs)


def groups():
    dp, space, tm = [bits(lax.axis_size(axis)) for axis in AXES]
    first = [(bit, 0, 0) for bit in dp[1:]]
    second = [(0, bit, 0) for bit in space]
    third = [(0, 0, bit) for bit in tm]
    orders = ((2, 0, 1), (1, 0, 2))
    return [closure(masks, order) for masks, order in zip((first + second, third), orders) if masks]


def closure(masks, order):
    found = [(0, 0, 0)]
    for mask in masks:
        found = found + [tuple(left ^ right for left, right in zip(item, mask)) for item in found]
    found = found[1:]
    return [found[place] for place in order] if len(found) == len(order) else found


def bits(count):
    return [1 << place for place in range(count.bit_length() - 1)]


def to_bf16(value):
    return lax.reduce_precision(value, exponent_bits=8, mantissa_bits=7)


def round_sums(sums, has_biases):
    end = sums.shape[0]
    high = sums[end - 16 : end - 8]
    rest = jnp.pad((high - to_bf16(high)) * has_biases, ((end - 8, 0), (0, 0)))
    return to_bf16(sums + rest)


def after(value, *earlier):
    return lax.optimization_barrier((value, *earlier))[0]


def pair_body(inputs, grad_out, conv_w, conv_b, mix_w, mix_b, adj_tiles, tile_cols, send_rows, counts):
    sample_input = inputs[0]
    sample_grad = grad_out[0]
    steps, chans, sensors = sample_input.shape
    rows = steps * chans
    half_rows = rows // 2
    wide = 2 * chans
    shape = jax.ShapeDtypeStruct
    border_rows = DILATION_SIZE * chans
    grad_flat = sample_grad.reshape(rows, sensors)
    taps = jnp.transpose(conv_w, (0, 2, 1))
    packed, own, halo, chosen, grad, tail = call(
        prepare_kernel,
        "prepare",
        [HBM] * 6,
        (
            shape((rows + chans // 2, wide), BF16),
            shape((sensors, sensors), BF16),
            shape((sensors, wide), BF16),
            shape((sensors, wide), BF16),
            shape((rows, sensors), BF16),
            shape((DILATION_SIZE, chans, sensors), BF16),
        ),
        (tile_cols, counts, send_rows, adj_tiles, grad_flat, sample_input),
        scratch=(
            pltpu.VMEM(adj_tiles.shape, BF16),
            pltpu.SMEM(tile_cols.shape, jnp.int32),
            pltpu.SMEM(counts.shape, jnp.int32),
            pltpu.VMEM(send_rows.shape, jnp.int32),
            DMA((7,)),
        ),
        micros=2.0,
    )
    packed_far = swap(packed, "space", 1)
    border = shift(tail, "tm", 1)
    hidden_late, slopes, right, near, spread, kept_input, kept_taps, turned_taps, bias, mix, mixing, mix_bias, mix_wide = call(
        forward_kernel,
        "forward",
        [HBM] * 5 + [VMEM] * 3,
        (
            shape((rows, sensors), BF16),
            shape((steps, wide, sensors), F32),
            shape((2 * wide + 16, steps * sensors), BF16),
            shape((rows, 2 * sensors), F32),
            shape((wide, 2 * sensors), BF16),
            shape(sample_input.shape, BF16),
            shape(taps.shape, BF16),
            shape((wide, wide), BF16),
            shape((1, wide), F32),
            shape(mix_w.shape, BF16),
            shape((chans, 3 * chans), BF16),
            shape((1, chans), F32),
            shape((chans, 3 * chans), BF16),
        ),
        (
            sample_input,
            taps,
            conv_b.reshape(1, wide),
            mix_w,
            mix_b.reshape(1, chans),
            grad,
            own,
            chosen,
        ),
        scratch=(DMA((5,)),),
        micros=1.5,
    )
    border_span = DILATION_SIZE * sensors
    sum_rows = (wide + chans + chans // 2 + 16) // 2
    kept, given, back, hidden = call(
        backward_kernel,
        "backward",
        [VMEM] * 13,
        (
            shape((sum_rows, wide), F32),
            shape((sum_rows, wide), F32),
            shape((steps, wide, sensors), BF16),
            shape((rows, sensors), BF16),
        ),
        (
            grad,
            packed,
            packed_far,
            border,
            near,
            spread,
            kept_input,
            turned_taps,
            bias,
            mixing,
            hidden_late,
            slopes,
            right,
        ),
        scratch=(
            pltpu.VMEM((wide + 3 * chans, steps * sensors), BF16),
            pltpu.VMEM((rows, 2 * sensors), BF16),
            pltpu.VMEM((DILATION_SIZE, wide, sensors), F32),
            pltpu.VMEM((2 * wide + 16, border_span), BF16),
        ),
        micros=2.0,
    )
    total = kept + swap(given, "dp", 1)
    rounds = groups()
    has_biases = (lax.axis_index("dp") % 2).astype(F32)
    early = call(
        early_kernel,
        "early",
        [VMEM] * 2,
        shape((DILATION_SIZE, chans, sensors), BF16),
        (back, kept_taps),
        micros=0.3,
    )
    early_far = shift(early, "tm", -1)
    boundary_first = call(
        boundary_kernel,
        "boundary",
        [VMEM] * 3,
        shape((rows, wide), BF16),
        (hidden, own, chosen),
        micros=0.3,
    )
    first_far = swap(boundary_first, "space", 1)
    base, hop_spread = call(
        hops_kernel,
        "hops",
        [VMEM] * 4,
        (shape((rows, 2 * sensors), F32), shape((2 * wide, 2 * sensors), BF16)),
        (hidden, packed_far, own, halo),
        micros=0.5,
    )
    outputs, grad_inputs = call(
        finish_kernel,
        "finish",
        [VMEM] * 12,
        (shape(sample_input.shape, BF16), shape(sample_grad.shape, BF16)),
        (
            kept_input,
            hidden,
            boundary_first,
            first_far,
            base,
            hop_spread,
            mix_wide,
            mix_bias,
            grad,
            back,
            early_far,
            kept_taps,
        ),
        scratch=(
            pltpu.VMEM(sample_input.shape, BF16),
            pltpu.VMEM(sample_grad.shape, BF16),
            pltpu.VMEM((rows, 2 * sensors), BF16),
            DMA((4,)),
        ),
        micros=2.0,
        space=HBM,
    )
    ready = {-2: (first_far, base), -1: (outputs, grad_inputs)}
    for index, group in enumerate(rounds):
        rounded = round_sums(total, has_biases)
        sent = rounded.astype(BF16)
        parts = [rounded] + [flip(sent, mask).astype(F32) for mask in group]
        parts[1] = after(parts[1], *ready.get(index - len(rounds), ()))
        while len(parts) > 1:
            parts = [left + right for left, right in zip(parts[::2], parts[1::2])]
        total = parts[0]
    total_far = swap(total, "dp", 1)
    cell_count = (
        inputs.shape[0]
        * steps
        * sensors
        * lax.axis_size("dp")
        * lax.axis_size("space")
        * lax.axis_size("tm")
    )
    scale = 1.0 / math.sqrt(cell_count)
    grad_taps, grad_conv_b, grad_mix_w, grad_mix_b = call(
        functools.partial(final_kernel, scale),
        "final",
        [VMEM] * 2,
        (
            shape((2, chans, wide), F32),
            shape((1, wide), F32),
            shape((3, chans, chans), F32),
            shape((1, chans), F32),
        ),
        (total, total_far),
    )
    return (
        outputs[None],
        grad_inputs[None],
        jnp.transpose(grad_taps, (0, 2, 1)),
        grad_conv_b.reshape(wide),
        grad_mix_w,
        grad_mix_b.reshape(chans),
    )


def power_of_two(count):
    return count & (count - 1) == 0


def body(inputs, grad_out, conv_w, conv_b, mix_w, mix_b, adj_tiles, tile_cols, send_rows, counts):
    tile = adj_tiles.shape[2]
    axes = [lax.axis_size(axis) for axis in ("dp", "space", "tm")]
    fits = (
        axes[1] == 2
        and axes[0] % 2 == 0
        and all(power_of_two(count) for count in axes)
        and inputs.shape[0] == 1
        and inputs.shape[3] == 2 * tile
        and inputs.shape[2] * 2 == tile
        and send_rows.shape[2] * 2 == tile
    )
    chosen = pair_body if fits else general_body
    return chosen(
        inputs, grad_out, conv_w, conv_b, mix_w, mix_b, adj_tiles, tile_cols, send_rows, counts
    )


def solution(mesh):
    in_specs = (
        P("dp", "tm", None, "space"),
        P("dp", "tm", None, "space"),
        P(),
        P(),
        P(),
        P(),
        P("space", None, None, None),
        P("space", None),
        P("space", None, None),
        P("space", None),
    )
    out_specs = (P("dp", "tm", None, "space"), P("dp", "tm", None, "space"), P(), P(), P(), P())
    return jax.shard_map(body, mesh=mesh, in_specs=in_specs, out_specs=out_specs, check_vma=False)
```

```python
import functools
import itertools
import math

import jax
import jax.numpy as jnp
from jax import lax
from jax.experimental import pallas as pl
from jax.experimental.pallas import tpu as pltpu
from jax.sharding import PartitionSpec as P

DILATION_SIZE = 2


def from_behind(value, axis, steps):
    count = lax.axis_size(axis)
    leading, last = (max(0, -steps), min(count, count - steps))
    return lax.ppermute(value, axis, [(source, source + steps) for source in range(leading, last)])


def slot_mask(counts, slot_count, dtype):
    slots = lax.broadcasted_iota(jnp.int32, (counts.shape[1], slot_count), 1)
    return (slots < counts[0][:, None]).astype(dtype)


def pack_rows(field, send_rows, live_slots):
    picked = field[:, :, send_rows[0]] * live_slots
    return picked.reshape(field.shape[0], field.shape[1], -1)


def tile_product(extended, adj_tiles, tile_cols):
    timestep_count, chan_count = (extended.shape[0], extended.shape[1])
    blocks = extended.reshape(timestep_count, chan_count, -1, adj_tiles.shape[2])
    picked = blocks[:, :, tile_cols]
    return jnp.einsum("tcrkj,rkij->tcri", picked, adj_tiles, preferred_element_type=jnp.float32)


def forward_start(field, send_rows, live_slots):
    packed = pack_rows(field, send_rows, live_slots)
    own_part = None
    return (packed, own_part)


def forward_finish(field, received, adj_tiles, tile_cols):
    total = tile_product(jnp.concatenate([field, received], 2), adj_tiles, tile_cols)
    return total.reshape(field.shape).astype(jnp.bfloat16)


def back_start(grad, adj_tiles, tile_cols, send_rows):
    timestep_count, chan_count, sensor_count = grad.shape
    tile_size = adj_tiles.shape[2]
    row_blocks = sensor_count // tile_size
    half_slots = tile_cols.shape[1] // 2
    halo_blocks = send_rows.shape[1] * send_rows.shape[2] // tile_size
    blocks = grad.reshape(timestep_count, chan_count, row_blocks, tile_size)
    remote_terms = jnp.einsum(
        "tcri,rkij->tcrkj", blocks, adj_tiles[:, half_slots:], preferred_element_type=jnp.float32
    )
    remote_sums = jnp.zeros((timestep_count, chan_count, halo_blocks, tile_size), jnp.float32)
    remote_sums = remote_sums.at[:, :, tile_cols[:, half_slots:] - row_blocks].add(remote_terms)
    return remote_sums.reshape(timestep_count, chan_count, -1).astype(jnp.bfloat16)


def back_finish(grad, returned, adj_tiles, tile_cols, send_rows, live_slots):
    timestep_count, chan_count, sensor_count = grad.shape
    tile_size = adj_tiles.shape[2]
    row_blocks = sensor_count // tile_size
    half_slots = tile_cols.shape[1] // 2
    blocks = grad.reshape(timestep_count, chan_count, row_blocks, tile_size)
    own_terms = jnp.einsum(
        "tcri,rkij->tcrkj", blocks, adj_tiles[:, :half_slots], preferred_element_type=jnp.float32
    )
    total = jnp.zeros((timestep_count, chan_count, row_blocks, tile_size), jnp.float32)
    total = total.at[:, :, tile_cols[:, :half_slots]].add(own_terms).reshape(grad.shape)
    returned = returned.reshape(
        timestep_count, chan_count, send_rows.shape[1], send_rows.shape[2]
    ).astype(jnp.float32)
    return total.at[:, :, send_rows[0]].add(returned * live_slots.astype(jnp.float32))


def mixing_grads(sample_grad, fields):
    grad_mix_w = jnp.stack(
        [
            jnp.einsum("ton,tcn->oc", sample_grad, item, preferred_element_type=jnp.float32)
            for item in fields
        ]
    )
    grad_mix_b = jnp.sum(sample_grad.astype(jnp.float32), axis=(0, 2))
    return (grad_mix_w, grad_mix_b)


def general_body(inputs, grad_out, conv_w, conv_b, mix_w, mix_b, adj_tiles, tile_cols, send_rows, counts):
    sample_input = inputs[0]
    sample_grad = grad_out[0]
    timestep_count, chan_count, sensor_count = sample_input.shape
    live_slots = slot_mask(counts, send_rows.shape[2], jnp.bfloat16)
    prior_border_slice = from_behind(sample_input[timestep_count - DILATION_SIZE :], "tm", 1)
    preceding_window = jnp.concatenate(
        [prior_border_slice, sample_input[: timestep_count - DILATION_SIZE]], 0
    )
    preact = jnp.einsum("oc,tcn->ton", conv_w[1], sample_input, preferred_element_type=jnp.float32)
    preact = preact + jnp.einsum(
        "oc,tcn->ton", conv_w[0], preceding_window, preferred_element_type=jnp.float32
    )
    preact = preact + conv_b[None, :, None]
    filtered = jnp.tanh(preact[:, :chan_count])
    gating = jax.nn.sigmoid(preact[:, chan_count:])
    hidden = (filtered * gating).astype(jnp.bfloat16)
    grad_float = sample_grad.astype(jnp.float32)
    packed_one, early_one = forward_start(hidden, send_rows, live_slots)
    received_one = lax.all_to_all(packed_one, "space", split_axis=2, concat_axis=2, tiled=True)
    hop_one = forward_finish(hidden, received_one, adj_tiles, tile_cols)
    packed_two, early_two = forward_start(hop_one, send_rows, live_slots)
    received_two = lax.all_to_all(packed_two, "space", split_axis=2, concat_axis=2, tiled=True)
    hop_two = forward_finish(hop_one, received_two, adj_tiles, tile_cols)
    fields = (hidden, hop_one, hop_two)
    grad_mix_w, grad_mix_b = mixing_grads(sample_grad, fields)
    back_two = jnp.einsum(
        "oc,ton->tcn", mix_w[2], sample_grad, preferred_element_type=jnp.float32
    ).astype(jnp.bfloat16)
    returned_two = lax.all_to_all(
        back_start(back_two, adj_tiles, tile_cols, send_rows),
        "space",
        split_axis=2,
        concat_axis=2,
        tiled=True,
    )
    back_one = jnp.einsum("oc,ton->tcn", mix_w[1], sample_grad, preferred_element_type=jnp.float32)
    back_one = (
        back_one + back_finish(back_two, returned_two, adj_tiles, tile_cols, send_rows, live_slots)
    ).astype(jnp.bfloat16)
    returned_one = lax.all_to_all(
        back_start(back_one, adj_tiles, tile_cols, send_rows),
        "space",
        split_axis=2,
        concat_axis=2,
        tiled=True,
    )
    back_hidden = jnp.einsum(
        "oc,ton->tcn", mix_w[0], sample_grad, preferred_element_type=jnp.float32
    )
    back_hidden = back_hidden + back_finish(
        back_one, returned_one, adj_tiles, tile_cols, send_rows, live_slots
    )
    mixed = sample_input.astype(jnp.float32) + mix_b[None, :, None]
    for index in range(3):
        mixed = mixed + jnp.einsum(
            "oc,tcn->ton", mix_w[index], fields[index], preferred_element_type=jnp.float32
        )
    outputs = mixed.astype(jnp.bfloat16)[None]
    grad_filter = back_hidden * (1.0 - filtered * filtered) * gating
    grad_gate = back_hidden * filtered * gating * (1.0 - gating)
    backward_preactivation = jnp.concatenate([grad_filter, grad_gate], 1).astype(jnp.bfloat16)
    next_border_slice = from_behind(backward_preactivation[:DILATION_SIZE], "tm", -1)
    following_window = jnp.concatenate(
        [backward_preactivation[DILATION_SIZE:], next_border_slice], 0
    )
    grad_inputs = grad_float + jnp.einsum(
        "oc,ton->tcn", conv_w[1], backward_preactivation, preferred_element_type=jnp.float32
    )
    grad_inputs = grad_inputs + jnp.einsum(
        "oc,ton->tcn", conv_w[0], following_window, preferred_element_type=jnp.float32
    )
    grad_inputs = grad_inputs.astype(jnp.bfloat16)[None]
    grad_conv_w = jnp.stack(
        [
            jnp.einsum(
                "ton,tcn->oc",
                backward_preactivation,
                preceding_window,
                preferred_element_type=jnp.float32,
            ),
            jnp.einsum(
                "ton,tcn->oc",
                backward_preactivation,
                sample_input,
                preferred_element_type=jnp.float32,
            ),
        ]
    )
    grad_conv_b = jnp.sum(backward_preactivation.astype(jnp.float32), axis=(0, 2))
    grad_conv_w, grad_conv_b, grad_mix_w, grad_mix_b = lax.psum(
        (grad_conv_w, grad_conv_b, grad_mix_w, grad_mix_b), ("dp", "space", "tm")
    )
    cell_count = (
        inputs.shape[0]
        * timestep_count
        * sensor_count
        * lax.axis_size("dp")
        * lax.axis_size("space")
        * lax.axis_size("tm")
    )
    scale = 1.0 / math.sqrt(cell_count)
    return (
        outputs,
        grad_inputs,
        grad_conv_w * scale,
        grad_conv_b * scale,
        grad_mix_w * scale,
        grad_mix_b * scale,
    )


BF16 = jnp.bfloat16
AXES = ("dp", "space", "tm")
F32 = jnp.float32
NT = (((1,), (1,)), ((), ()))
VMEM_BYTES = 24 * 1024 * 1024


def mm(left, right):
    return jnp.dot(left, right, preferred_element_type=F32)


def mm_nt(left, right):
    return lax.dot_general(left, right, NT, preferred_element_type=F32)


def upper_lanes(shape):
    return lax.broadcasted_iota(jnp.int32, shape, 1) >= shape[1] // 2


def halves(matrix):
    upper = upper_lanes(matrix.shape)
    zero = jnp.zeros_like(matrix)
    return jnp.where(upper, zero, matrix), jnp.where(upper, matrix, zero)


def fold(first, second):
    return jnp.where(upper_lanes(first.shape), second, first)


def times_halves(left, right):
    half = left.shape[0] // 2
    return fold(mm(left[:half], right), mm(left[half:], right))


def link_rows(packed):
    packed = packed.astype(F32)
    turned = pltpu.roll(packed, packed.shape[1] // 2, 1)
    return jnp.concatenate([halves(packed)[0], halves(turned)[0]], 0).astype(BF16)


def column(row):
    size = row.shape[1]
    first = lax.broadcasted_iota(jnp.int32, (size, size), 0)
    second = lax.broadcasted_iota(jnp.int32, (size, size), 1)
    return jnp.sum(jnp.where(first == second, row, 0.0), axis=1, keepdims=True)


def fetch(pairs, sems):
    copies = [
        pltpu.make_async_copy(source, target, sems.at[index])
        for index, (source, target) in enumerate(pairs)
    ]
    for copy in copies:
        copy.start()
    return copies


def prepare_kernel(
    cols_hbm,
    counts_hbm,
    rows_hbm,
    adj_hbm,
    grad_hbm,
    input_hbm,
    packed_ref,
    own_ref,
    halo_ref,
    chosen_ref,
    grad_ref,
    tail_ref,
    adj_ref,
    cols_ref,
    counts_ref,
    rows_ref,
    sems,
):
    row_blocks, slots, tile = adj_ref.shape[:3]
    own_slots = slots // 2
    steps = input_hbm.shape[0]
    copies = fetch(
        [
            (adj_hbm.at[:, pl.ds(own_slots, own_slots)], adj_ref.at[:, pl.ds(own_slots, own_slots)]),
            (cols_hbm, cols_ref),
            (counts_hbm, counts_ref),
            (rows_hbm, rows_ref),
            (adj_hbm.at[:, pl.ds(0, own_slots)], adj_ref.at[:, pl.ds(0, own_slots)]),
            (grad_hbm, grad_ref),
            (input_hbm.at[pl.ds(steps - DILATION_SIZE, DILATION_SIZE)], tail_ref),
        ],
        sems,
    )
    other = 1 - lax.axis_index("space")
    sensors = grad_ref.shape[1]
    rows_count = grad_ref.shape[0]
    slot_count = rows_ref.shape[2]
    upper = upper_lanes((tile, tile)).astype(jnp.int32)
    for copy in copies[:5]:
        copy.wait()
    for r in range(row_blocks):
        far = adj_ref[r, own_slots].astype(F32)
        for k in range(own_slots + 1, slots):
            far = far + adj_ref[r, k].astype(F32)
        far = jnp.where(upper == other, far, pltpu.roll(far, tile // 2, 1))
        halo_ref[r * tile : (r + 1) * tile, :] = far.astype(BF16)
    rows = rows_ref[0, pl.ds(other, 1), :]
    rows = jnp.concatenate([rows, rows], 1)
    lanes = lax.broadcasted_iota(jnp.int32, (1, 2 * slot_count), 1)
    place = lanes - jnp.where(lanes >= slot_count, slot_count, 0)
    rows = jnp.where(place < counts_ref[0, other], rows, -1)
    sensor = lax.broadcasted_iota(jnp.int32, (sensors, 2 * slot_count), 0)
    chosen = jnp.where(sensor == rows, 1.0, 0.0).astype(F32)
    chosen_ref[...] = chosen.astype(BF16)
    turned = jnp.transpose(chosen)[:slot_count].astype(BF16)
    halo = halo_ref[...]
    packed_ref[rows_count:, :] = times_halves(turned, halo).astype(BF16)
    for r in range(row_blocks):
        sums = [jnp.zeros((tile, tile), F32), jnp.zeros((tile, tile), F32)]
        for k in range(own_slots):
            item = adj_ref[r, k].astype(F32)
            for block in range(2):
                share = jnp.where(cols_ref[r, k] == block, 1.0, 0.0).astype(F32)
                sums[block] = sums[block] + item * share
        own_ref[r * tile : (r + 1) * tile, :] = jnp.concatenate(sums, 1).astype(BF16)
    both = fold(halo, mm(own_ref[...], halo).astype(BF16))
    copies[5].wait()
    packed_ref[:rows_count, :] = mm(grad_ref[...], both).astype(BF16)
    copies[6].wait()


def gate_step(t, earlier, input_ref, preact, hidden_ref, slopes_ref, right_ref):
    steps, chans, sensors = input_ref.shape
    at = slice(t * chans, (t + 1) * chans)
    span = slice(t * sensors, (t + 1) * sensors)
    filtered = jnp.tanh(preact[:chans])
    gating = 0.5 * jnp.tanh(0.5 * preact[chans:]) + 0.5
    product = filtered * gating
    hidden = product.astype(BF16)
    hidden_ref[at, :] = hidden
    slopes_ref[t, :chans] = (1.0 - filtered * filtered) * gating
    slopes_ref[t, chans:] = product * (1.0 - gating)
    right_ref[:chans, span] = earlier
    right_ref[chans : 2 * chans, span] = input_ref[t]
    right_ref[2 * chans : 2 * chans + 16, span] = jnp.ones((16, sensors), BF16)
    right_ref[2 * chans + 16 : 3 * chans + 16, span] = hidden
    right_ref[3 * chans + 16 :, span] = hidden


def forward_kernel(
    input_hbm,
    conv_w_hbm,
    conv_b_hbm,
    mix_w_hbm,
    mix_b_hbm,
    grad_ref,
    own_ref,
    chosen_ref,
    hidden_ref,
    slopes_ref,
    right_ref,
    near_ref,
    spread_ref,
    input_ref,
    taps_ref,
    turned_taps_ref,
    bias_ref,
    mix_ref,
    mixing_ref,
    mix_bias_ref,
    mix_wide_ref,
    boundary_ref,
    sems,
):
    copies = fetch(
        [
            (input_hbm, input_ref),
            (conv_w_hbm, taps_ref),
            (conv_b_hbm, bias_ref),
            (mix_w_hbm, mix_ref),
            (mix_b_hbm, mix_bias_ref),
        ],
        sems,
    )
    steps, chans, sensors = input_ref.shape
    own = own_ref[...]
    near = mm(grad_ref[...], own)
    near_ref[:, :sensors] = near
    near_ref[:, sensors:] = mm(near.astype(BF16), own)
    turned = jnp.transpose(chosen_ref[...].astype(F32)).astype(BF16)
    slot_count = turned.shape[0] // 2
    spread_ref[:, :sensors] = jnp.where(
        lax.broadcasted_iota(jnp.int32, turned.shape, 0) < slot_count,
        turned,
        jnp.zeros_like(turned),
    )
    spread_ref[:slot_count, sensors:] = mm(turned[:slot_count], own).astype(BF16)
    spread_ref[slot_count:, sensors:] = turned[slot_count:]
    for copy in copies:
        copy.wait()
    mixing = jnp.transpose(mix_ref[...].reshape(3 * chans, chans).astype(F32))
    mixing_ref[...] = mixing.astype(BF16)
    mix_wide_ref[...] = jnp.concatenate([mix_ref[0], mix_ref[1], mix_ref[2]], 1)
    taps = taps_ref[...].reshape(2 * chans, 2 * chans).astype(F32)
    taps = jnp.transpose(taps).astype(BF16)
    turned_taps_ref[...] = taps
    bias = column(bias_ref[...])
    for t in range(DILATION_SIZE, steps):
        earlier = input_ref[t - DILATION_SIZE]
        preact = mm(taps, jnp.concatenate([earlier, input_ref[t]], 0)) + bias
        gate_step(t, earlier, input_ref, preact, hidden_ref, slopes_ref, right_ref)
    hidden = hidden_ref[DILATION_SIZE * chans :, :]
    boundary_ref[...] = boundary_rows(hidden, own, chosen_ref[...])


def backward_kernel(
    grad_ref,
    own_packed_ref,
    packed_ref,
    border_ref,
    near_ref,
    spread_ref,
    input_ref,
    turned_taps_ref,
    bias_ref,
    mixing_ref,
    hidden_old_ref,
    slopes_old_ref,
    right_old_ref,
    kept_ref,
    given_ref,
    back_ref,
    hidden_ref,
    left_scr,
    both_scr,
    slopes_ref,
    right_ref,
):
    steps, wide, sensors = back_ref.shape
    chans = wide // 2
    rows = steps * chans
    border_rows = DILATION_SIZE * chans
    border_span = DILATION_SIZE * sensors
    core = lax.axis_index("dp") % 2
    linked = mm(link_rows(packed_ref[rows:, :]), spread_ref[:, :sensors]).astype(BF16)
    blank = jnp.zeros_like(linked)
    linked = jnp.concatenate([blank, linked], 1)
    spread = jnp.concatenate([spread_ref[...], linked, jnp.zeros_like(linked)], 0)
    packed = jnp.concatenate([packed_ref[:rows, :], own_packed_ref[:rows, :]], 1)
    both_scr[...] = (near_ref[...] + mm(packed, spread)).astype(BF16)
    bias = column(bias_ref[...])
    place = lax.axis_index("tm")
    hidden_ref[border_rows:, :] = hidden_old_ref[border_rows:, :]
    for t in range(DILATION_SIZE):
        earlier = border_ref[t]
        earlier = jnp.where(place > 0, earlier, jnp.zeros_like(earlier))
        window = jnp.concatenate([earlier, input_ref[t]], 0)
        preact = mm(turned_taps_ref[...], window) + bias
        gate_step(t, earlier, input_ref, preact, hidden_ref, slopes_ref, right_ref)
    mixing = mixing_ref[...]
    for t in range(steps):
        at = slice(t * chans, (t + 1) * chans)
        span = slice(t * sensors, (t + 1) * sensors)
        fields = jnp.concatenate(
            [grad_ref[at, :], both_scr[at, :sensors], both_scr[at, sensors:]], 0
        )
        back_hidden = mm(mixing, fields)
        back_hidden = jnp.concatenate([back_hidden, back_hidden], 0)
        slopes = slopes_ref[t] if t < DILATION_SIZE else slopes_old_ref[t]
        back_pre = (back_hidden * slopes).astype(BF16)
        back_ref[t] = back_pre
        left_scr[:wide, span] = back_pre
        left_scr[wide:, span] = fields
    ones = wide + 16
    conv = mm_nt(right_old_ref[:ones, border_span:], left_scr[: wide + chans, border_span:])
    conv = conv + mm_nt(right_ref[:ones, :], left_scr[: wide + chans, :border_span])
    mixes = mm_nt(left_scr[wide:, border_span:], right_old_ref[ones:, border_span:])
    mixes = mixes + mm_nt(left_scr[wide:, :border_span], right_ref[ones:, :])
    sums = conv[wide : wide + 8]
    conv = conv[:wide, :wide]
    zero, first, second = [mixes[k * chans : (k + 1) * chans] for k in range(3)]
    half = chans // 2
    blank = jnp.zeros((8, wide), F32)
    mix_sums = jnp.concatenate([sums[:, wide:], blank[:, :chans]], 1)
    upper_rows = lax.broadcasted_iota(jnp.int32, blank.shape, 0) >= 4
    biases = jnp.where(upper_rows, mix_sums, sums[:, :wide])
    packed = jnp.concatenate(
        [conv, fold(zero, first), fold(second[:half], second[half:]), biases, blank], 0
    )
    cut = packed.shape[0] // 2
    kept_ref[...] = jnp.where(core == 0, packed[:cut], packed[cut:])
    given_ref[...] = jnp.where(core == 0, packed[cut:], packed[:cut])


def boundary_rows(hidden, own, chosen):
    chosen_low, chosen_high = halves(chosen)
    hop = mm_nt(hidden, own).astype(BF16)
    return (mm(hidden, chosen_low) + mm(hop, chosen_high)).astype(BF16)


def early_kernel(back_ref, taps_ref, early_ref):
    for t in range(DILATION_SIZE):
        early_ref[t] = mm(taps_ref[0], back_ref[t]).astype(BF16)


def boundary_kernel(hidden_ref, late_ref, own_ref, chosen_ref, boundary_ref):
    early_rows = boundary_ref.shape[0] - late_ref.shape[0]
    hidden = hidden_ref[:early_rows, :]
    boundary_ref[:early_rows, :] = boundary_rows(hidden, own_ref[...], chosen_ref[...])
    boundary_ref[early_rows:, :] = late_ref[...]


def hops_kernel(hidden_ref, packed_ref, own_ref, halo_ref, base_ref, spread_ref):
    sensors = own_ref.shape[0]
    slots = halo_ref.shape[1] // 2
    rows = hidden_ref.shape[0]
    own = own_ref[...]
    one = mm_nt(hidden_ref[...], own)
    base_ref[:, :sensors] = one
    base_ref[:, sensors:] = mm_nt(one.astype(BF16), own)
    halo = halo_ref[...]
    link = link_rows(packed_ref[rows:, :])
    link = jnp.concatenate([link, jnp.zeros_like(link)], 0)
    turned = jnp.transpose(jnp.concatenate([halo.astype(F32), mm(halo, link)], 1)).astype(BF16)
    blank = jnp.zeros((slots, sensors), BF16)
    first = turned[:slots]
    spread_ref[:slots, :sensors] = first
    spread_ref[:slots, sensors:] = mm_nt(first, own).astype(BF16)
    for block in range(1, 4):
        at = slice(block * slots, (block + 1) * slots)
        spread_ref[at, :sensors] = blank
        spread_ref[at, sensors:] = turned[at] if block < 3 else blank


def finish_kernel(
    input_ref,
    hidden_ref,
    own_boundary_ref,
    boundary_ref,
    base_ref,
    spread_ref,
    mix_ref,
    bias_ref,
    grad_ref,
    back_ref,
    early_ref,
    taps_ref,
    out_hbm,
    grad_out_hbm,
    out_scr,
    grad_scr,
    both_scr,
    sems,
):
    steps, chans, sensors = input_ref.shape
    has_later = lax.axis_index("tm") < lax.axis_size("tm") - 1
    taps = jnp.concatenate([taps_ref[0], taps_ref[1]], 1)
    chunk = steps // 2
    copies = []

    def send(scratch, target, start):
        span = pl.ds(start, chunk)
        copy = pltpu.make_async_copy(scratch.at[span], target.at[span], sems.at[len(copies)])
        copy.start()
        copies.append(copy)

    for t in range(steps):
        at = slice(t * chans, (t + 1) * chans)
        later = t + DILATION_SIZE
        total = grad_ref[at, :].astype(F32)
        if later < steps:
            total = total + mm(taps, jnp.concatenate([back_ref[later], back_ref[t]], 0))
        else:
            early = early_ref[later - steps].astype(F32)
            early = jnp.where(has_later, early, jnp.zeros_like(early))
            total = total + mm(taps_ref[1], back_ref[t]) + early
        grad_scr[t] = total.astype(BF16)
        if (t + 1) % chunk == 0:
            send(grad_scr, grad_out_hbm, t + 1 - chunk)
    boundary = jnp.concatenate([boundary_ref[...], own_boundary_ref[...]], 1)
    both_scr[...] = (base_ref[...] + mm(boundary, spread_ref[...])).astype(BF16)
    bias = column(bias_ref[...])
    mix = mix_ref[...]
    for t in range(steps):
        at = slice(t * chans, (t + 1) * chans)
        fields = jnp.concatenate(
            [hidden_ref[at, :], both_scr[at, :sensors], both_scr[at, sensors:]], 0
        )
        out_scr[t] = (mm(mix, fields) + bias + input_ref[t].astype(F32)).astype(BF16)
        if (t + 1) % chunk == 0:
            send(out_scr, out_hbm, t + 1 - chunk)
    for copy in copies:
        copy.wait()


def final_kernel(scale, kept_ref, other_ref, conv_w_ref, conv_b_ref, mix_w_ref, mix_b_ref):
    core = lax.axis_index("dp") % 2
    kept = kept_ref[...] * scale
    other = other_ref[...] * scale
    lower = jnp.where(core == 0, kept, other)
    upper = jnp.where(core == 0, other, kept)
    chans, wide = conv_w_ref.shape[1:]
    half = chans // 2
    start = wide - lower.shape[0]
    conv_w_ref[0] = lower[:chans]
    conv_w_ref[1] = jnp.concatenate([lower[chans:], upper[:start]], 0)
    first = upper[start : start + chans]
    second = upper[start + chans : start + chans + half]
    mix_w_ref[0] = first[:, :chans]
    mix_w_ref[1] = pltpu.roll(first, chans, 1)[:, :chans]
    mix_w_ref[2] = jnp.concatenate([second, pltpu.roll(second, chans, 1)], 0)[:, :chans]
    start = start + chans + half
    biases = upper[start : start + 8] + upper[start + 8 :]
    conv_b_ref[...] = biases[:1]
    mix_b_ref[...] = biases[4:5, :chans]


VMEM = pl.BlockSpec(memory_space=pltpu.VMEM)
HBM = pl.BlockSpec(memory_space=pltpu.HBM)
DMA = pltpu.SemaphoreType.DMA


def call(kernel, name, in_specs, out_shape, args, scratch=(), micros=1.0, space=None):
    args = [
        pltpu.with_memory_space_constraint(arg, pltpu.HBM) if spec is HBM else arg
        for spec, arg in zip(in_specs, args)
    ]
    return pl.pallas_call(
        kernel,
        out_shape=out_shape,
        in_specs=in_specs,
        out_specs=jax.tree.map(lambda _: space or VMEM, out_shape),
        scratch_shapes=list(scratch),
        compiler_params=pltpu.CompilerParams(vmem_limit_bytes=VMEM_BYTES),
        cost_estimate=pl.CostEstimate(
            flops=0, bytes_accessed=int(micros * 3_600_000), transcendentals=0
        ),
        name=name,
    )(*args)


def swap(value, axis, bit):
    count = lax.axis_size(axis)
    return lax.ppermute(value, axis, [(source, source ^ bit) for source in range(count)])


def shift(value, axis, steps):
    count = lax.axis_size(axis)
    return lax.ppermute(value, axis, [(source, (source + steps) % count) for source in range(count)])


def flip(value, mask):
    sizes = [lax.axis_size(axis) for axis in AXES]
    places = list(itertools.product(*[range(size) for size in sizes]))
    index = {place: number for number, place in enumerate(places)}
    pairs = [
        (index[place], index[tuple(part ^ bit for part, bit in zip(place, mask))])
        for place in places
    ]
    return lax.ppermute(value, AXES, pairs)


def groups():
    dp, space, tm = [bits(lax.axis_size(axis)) for axis in AXES]
    first = [(bit, 0, 0) for bit in dp[1:]]
    second = [(0, bit, 0) for bit in space]
    third = [(0, 0, bit) for bit in tm]
    orders = ((2, 0, 1), (1, 0, 2))
    return [closure(masks, order) for masks, order in zip((first + second, third), orders) if masks]


def closure(masks, order):
    found = [(0, 0, 0)]
    for mask in masks:
        found = found + [tuple(left ^ right for left, right in zip(item, mask)) for item in found]
    found = found[1:]
    return [found[place] for place in order] if len(found) == len(order) else found


def bits(count):
    return [1 << place for place in range(count.bit_length() - 1)]


def to_bf16(value):
    return lax.reduce_precision(value, exponent_bits=8, mantissa_bits=7)


def round_sums(sums, has_biases):
    end = sums.shape[0]
    high = sums[end - 16 : end - 8]
    rest = jnp.pad((high - to_bf16(high)) * has_biases, ((end - 8, 0), (0, 0)))
    return to_bf16(sums + rest)


def after(value, *earlier):
    return lax.optimization_barrier((value, *earlier))[0]


def pair_body(inputs, grad_out, conv_w, conv_b, mix_w, mix_b, adj_tiles, tile_cols, send_rows, counts):
    sample_input = inputs[0]
    sample_grad = grad_out[0]
    steps, chans, sensors = sample_input.shape
    rows = steps * chans
    half_rows = rows // 2
    wide = 2 * chans
    shape = jax.ShapeDtypeStruct
    border_rows = DILATION_SIZE * chans
    grad_flat = sample_grad.reshape(rows, sensors)
    taps = jnp.transpose(conv_w, (0, 2, 1))
    packed, own, halo, chosen, grad, tail = call(
        prepare_kernel,
        "prepare",
        [HBM] * 6,
        (
            shape((rows + chans // 2, wide), BF16),
            shape((sensors, sensors), BF16),
            shape((sensors, wide), BF16),
            shape((sensors, wide), BF16),
            shape((rows, sensors), BF16),
            shape((DILATION_SIZE, chans, sensors), BF16),
        ),
        (tile_cols, counts, send_rows, adj_tiles, grad_flat, sample_input),
        scratch=(
            pltpu.VMEM(adj_tiles.shape, BF16),
            pltpu.SMEM(tile_cols.shape, jnp.int32),
            pltpu.SMEM(counts.shape, jnp.int32),
            pltpu.VMEM(send_rows.shape, jnp.int32),
            DMA((7,)),
        ),
        micros=2.0,
    )
    packed_far = swap(packed, "space", 1)
    border = shift(tail, "tm", 1)
    hidden_late, slopes, right, near, spread, kept_input, kept_taps, turned_taps, bias, mix, mixing, mix_bias, mix_wide, boundary_late = call(
        forward_kernel,
        "forward",
        [HBM] * 5 + [VMEM] * 3,
        (
            shape((rows, sensors), BF16),
            shape((steps, wide, sensors), F32),
            shape((2 * wide + 16, steps * sensors), BF16),
            shape((rows, 2 * sensors), F32),
            shape((wide, 2 * sensors), BF16),
            shape(sample_input.shape, BF16),
            shape(taps.shape, BF16),
            shape((wide, wide), BF16),
            shape((1, wide), F32),
            shape(mix_w.shape, BF16),
            shape((chans, 3 * chans), BF16),
            shape((1, chans), F32),
            shape((chans, 3 * chans), BF16),
            shape((rows - border_rows, wide), BF16),
        ),
        (
            sample_input,
            taps,
            conv_b.reshape(1, wide),
            mix_w,
            mix_b.reshape(1, chans),
            grad,
            own,
            chosen,
        ),
        scratch=(DMA((5,)),),
        micros=1.5,
    )
    border_span = DILATION_SIZE * sensors
    sum_rows = (wide + chans + chans // 2 + 16) // 2
    kept, given, back, hidden = call(
        backward_kernel,
        "backward",
        [VMEM] * 13,
        (
            shape((sum_rows, wide), F32),
            shape((sum_rows, wide), F32),
            shape((steps, wide, sensors), BF16),
            shape((rows, sensors), BF16),
        ),
        (
            grad,
            packed,
            packed_far,
            border,
            near,
            spread,
            kept_input,
            turned_taps,
            bias,
            mixing,
            hidden_late,
            slopes,
            right,
        ),
        scratch=(
            pltpu.VMEM((wide + 3 * chans, steps * sensors), BF16),
            pltpu.VMEM((rows, 2 * sensors), BF16),
            pltpu.VMEM((DILATION_SIZE, wide, sensors), F32),
            pltpu.VMEM((2 * wide + 16, border_span), BF16),
        ),
        micros=2.0,
    )
    total = kept + swap(given, "dp", 1)
    rounds = groups()
    has_biases = (lax.axis_index("dp") % 2).astype(F32)
    early = call(
        early_kernel,
        "early",
        [VMEM] * 2,
        shape((DILATION_SIZE, chans, sensors), BF16),
        (back, kept_taps),
        micros=0.3,
    )
    early_far = shift(early, "tm", -1)
    boundary_first = call(
        boundary_kernel,
        "boundary",
        [VMEM] * 4,
        shape((rows, wide), BF16),
        (hidden, boundary_late, own, chosen),
        micros=0.3,
    )
    first_far = swap(boundary_first, "space", 1)
    base, hop_spread = call(
        hops_kernel,
        "hops",
        [VMEM] * 4,
        (shape((rows, 2 * sensors), F32), shape((2 * wide, 2 * sensors), BF16)),
        (hidden, packed_far, own, halo),
        micros=0.5,
    )
    outputs, grad_inputs = call(
        finish_kernel,
        "finish",
        [VMEM] * 12,
        (shape(sample_input.shape, BF16), shape(sample_grad.shape, BF16)),
        (
            kept_input,
            hidden,
            boundary_first,
            first_far,
            base,
            hop_spread,
            mix_wide,
            mix_bias,
            grad,
            back,
            early_far,
            kept_taps,
        ),
        scratch=(
            pltpu.VMEM(sample_input.shape, BF16),
            pltpu.VMEM(sample_grad.shape, BF16),
            pltpu.VMEM((rows, 2 * sensors), BF16),
            DMA((4,)),
        ),
        micros=2.0,
        space=HBM,
    )
    ready = {-2: (first_far, base), -1: (outputs, grad_inputs)}
    for index, group in enumerate(rounds):
        rounded = round_sums(total, has_biases)
        sent = rounded.astype(BF16)
        parts = [rounded] + [flip(sent, mask).astype(F32) for mask in group]
        parts[1] = after(parts[1], *ready.get(index - len(rounds), ()))
        while len(parts) > 1:
            parts = [left + right for left, right in zip(parts[::2], parts[1::2])]
        total = parts[0]
    total_far = swap(total, "dp", 1)
    cell_count = (
        inputs.shape[0]
        * steps
        * sensors
        * lax.axis_size("dp")
        * lax.axis_size("space")
        * lax.axis_size("tm")
    )
    scale = 1.0 / math.sqrt(cell_count)
    grad_taps, grad_conv_b, grad_mix_w, grad_mix_b = call(
        functools.partial(final_kernel, scale),
        "final",
        [VMEM] * 2,
        (
            shape((2, chans, wide), F32),
            shape((1, wide), F32),
            shape((3, chans, chans), F32),
            shape((1, chans), F32),
        ),
        (total, total_far),
    )
    return (
        outputs[None],
        grad_inputs[None],
        jnp.transpose(grad_taps, (0, 2, 1)),
        grad_conv_b.reshape(wide),
        grad_mix_w,
        grad_mix_b.reshape(chans),
    )


def power_of_two(count):
    return count & (count - 1) == 0


def body(inputs, grad_out, conv_w, conv_b, mix_w, mix_b, adj_tiles, tile_cols, send_rows, counts):
    tile = adj_tiles.shape[2]
    axes = [lax.axis_size(axis) for axis in ("dp", "space", "tm")]
    fits = (
        axes[1] == 2
        and axes[0] % 2 == 0
        and all(power_of_two(count) for count in axes)
        and inputs.shape[0] == 1
        and inputs.shape[3] == 2 * tile
        and inputs.shape[2] * 2 == tile
        and send_rows.shape[2] * 2 == tile
    )
    chosen = pair_body if fits else general_body
    return chosen(
        inputs, grad_out, conv_w, conv_b, mix_w, mix_b, adj_tiles, tile_cols, send_rows, counts
    )


def solution(mesh):
    in_specs = (
        P("dp", "tm", None, "space"),
        P("dp", "tm", None, "space"),
        P(),
        P(),
        P(),
        P(),
        P("space", None, None, None),
        P("space", None),
        P("space", None, None),
        P("space", None),
    )
    out_specs = (P("dp", "tm", None, "space"), P("dp", "tm", None, "space"), P(), P(), P(), P())
    return jax.shard_map(body, mesh=mesh, in_specs=in_specs, out_specs=out_specs, check_vma=False)
```

```python
import functools
import itertools
import math

import jax
import jax.numpy as jnp
from jax import lax
from jax.experimental import pallas as pl
from jax.experimental.pallas import tpu as pltpu
from jax.sharding import PartitionSpec as P

DILATION_SIZE = 2


def from_behind(value, axis, steps):
    count = lax.axis_size(axis)
    leading, last = (max(0, -steps), min(count, count - steps))
    return lax.ppermute(value, axis, [(source, source + steps) for source in range(leading, last)])


def slot_mask(counts, slot_count, dtype):
    slots = lax.broadcasted_iota(jnp.int32, (counts.shape[1], slot_count), 1)
    return (slots < counts[0][:, None]).astype(dtype)


def pack_rows(field, send_rows, live_slots):
    picked = field[:, :, send_rows[0]] * live_slots
    return picked.reshape(field.shape[0], field.shape[1], -1)


def tile_product(extended, adj_tiles, tile_cols):
    timestep_count, chan_count = (extended.shape[0], extended.shape[1])
    blocks = extended.reshape(timestep_count, chan_count, -1, adj_tiles.shape[2])
    picked = blocks[:, :, tile_cols]
    return jnp.einsum("tcrkj,rkij->tcri", picked, adj_tiles, preferred_element_type=jnp.float32)


def forward_start(field, send_rows, live_slots):
    packed = pack_rows(field, send_rows, live_slots)
    own_part = None
    return (packed, own_part)


def forward_finish(field, received, adj_tiles, tile_cols):
    total = tile_product(jnp.concatenate([field, received], 2), adj_tiles, tile_cols)
    return total.reshape(field.shape).astype(jnp.bfloat16)


def back_start(grad, adj_tiles, tile_cols, send_rows):
    timestep_count, chan_count, sensor_count = grad.shape
    tile_size = adj_tiles.shape[2]
    row_blocks = sensor_count // tile_size
    half_slots = tile_cols.shape[1] // 2
    halo_blocks = send_rows.shape[1] * send_rows.shape[2] // tile_size
    blocks = grad.reshape(timestep_count, chan_count, row_blocks, tile_size)
    remote_terms = jnp.einsum(
        "tcri,rkij->tcrkj", blocks, adj_tiles[:, half_slots:], preferred_element_type=jnp.float32
    )
    remote_sums = jnp.zeros((timestep_count, chan_count, halo_blocks, tile_size), jnp.float32)
    remote_sums = remote_sums.at[:, :, tile_cols[:, half_slots:] - row_blocks].add(remote_terms)
    return remote_sums.reshape(timestep_count, chan_count, -1).astype(jnp.bfloat16)


def back_finish(grad, returned, adj_tiles, tile_cols, send_rows, live_slots):
    timestep_count, chan_count, sensor_count = grad.shape
    tile_size = adj_tiles.shape[2]
    row_blocks = sensor_count // tile_size
    half_slots = tile_cols.shape[1] // 2
    blocks = grad.reshape(timestep_count, chan_count, row_blocks, tile_size)
    own_terms = jnp.einsum(
        "tcri,rkij->tcrkj", blocks, adj_tiles[:, :half_slots], preferred_element_type=jnp.float32
    )
    total = jnp.zeros((timestep_count, chan_count, row_blocks, tile_size), jnp.float32)
    total = total.at[:, :, tile_cols[:, :half_slots]].add(own_terms).reshape(grad.shape)
    returned = returned.reshape(
        timestep_count, chan_count, send_rows.shape[1], send_rows.shape[2]
    ).astype(jnp.float32)
    return total.at[:, :, send_rows[0]].add(returned * live_slots.astype(jnp.float32))


def mixing_grads(sample_grad, fields):
    grad_mix_w = jnp.stack(
        [
            jnp.einsum("ton,tcn->oc", sample_grad, item, preferred_element_type=jnp.float32)
            for item in fields
        ]
    )
    grad_mix_b = jnp.sum(sample_grad.astype(jnp.float32), axis=(0, 2))
    return (grad_mix_w, grad_mix_b)


def general_body(inputs, grad_out, conv_w, conv_b, mix_w, mix_b, adj_tiles, tile_cols, send_rows, counts):
    sample_input = inputs[0]
    sample_grad = grad_out[0]
    timestep_count, chan_count, sensor_count = sample_input.shape
    live_slots = slot_mask(counts, send_rows.shape[2], jnp.bfloat16)
    prior_border_slice = from_behind(sample_input[timestep_count - DILATION_SIZE :], "tm", 1)
    preceding_window = jnp.concatenate(
        [prior_border_slice, sample_input[: timestep_count - DILATION_SIZE]], 0
    )
    preact = jnp.einsum("oc,tcn->ton", conv_w[1], sample_input, preferred_element_type=jnp.float32)
    preact = preact + jnp.einsum(
        "oc,tcn->ton", conv_w[0], preceding_window, preferred_element_type=jnp.float32
    )
    preact = preact + conv_b[None, :, None]
    filtered = jnp.tanh(preact[:, :chan_count])
    gating = jax.nn.sigmoid(preact[:, chan_count:])
    hidden = (filtered * gating).astype(jnp.bfloat16)
    grad_float = sample_grad.astype(jnp.float32)
    packed_one, early_one = forward_start(hidden, send_rows, live_slots)
    received_one = lax.all_to_all(packed_one, "space", split_axis=2, concat_axis=2, tiled=True)
    hop_one = forward_finish(hidden, received_one, adj_tiles, tile_cols)
    packed_two, early_two = forward_start(hop_one, send_rows, live_slots)
    received_two = lax.all_to_all(packed_two, "space", split_axis=2, concat_axis=2, tiled=True)
    hop_two = forward_finish(hop_one, received_two, adj_tiles, tile_cols)
    fields = (hidden, hop_one, hop_two)
    grad_mix_w, grad_mix_b = mixing_grads(sample_grad, fields)
    back_two = jnp.einsum(
        "oc,ton->tcn", mix_w[2], sample_grad, preferred_element_type=jnp.float32
    ).astype(jnp.bfloat16)
    returned_two = lax.all_to_all(
        back_start(back_two, adj_tiles, tile_cols, send_rows),
        "space",
        split_axis=2,
        concat_axis=2,
        tiled=True,
    )
    back_one = jnp.einsum("oc,ton->tcn", mix_w[1], sample_grad, preferred_element_type=jnp.float32)
    back_one = (
        back_one + back_finish(back_two, returned_two, adj_tiles, tile_cols, send_rows, live_slots)
    ).astype(jnp.bfloat16)
    returned_one = lax.all_to_all(
        back_start(back_one, adj_tiles, tile_cols, send_rows),
        "space",
        split_axis=2,
        concat_axis=2,
        tiled=True,
    )
    back_hidden = jnp.einsum(
        "oc,ton->tcn", mix_w[0], sample_grad, preferred_element_type=jnp.float32
    )
    back_hidden = back_hidden + back_finish(
        back_one, returned_one, adj_tiles, tile_cols, send_rows, live_slots
    )
    mixed = sample_input.astype(jnp.float32) + mix_b[None, :, None]
    for index in range(3):
        mixed = mixed + jnp.einsum(
            "oc,tcn->ton", mix_w[index], fields[index], preferred_element_type=jnp.float32
        )
    outputs = mixed.astype(jnp.bfloat16)[None]
    grad_filter = back_hidden * (1.0 - filtered * filtered) * gating
    grad_gate = back_hidden * filtered * gating * (1.0 - gating)
    backward_preactivation = jnp.concatenate([grad_filter, grad_gate], 1).astype(jnp.bfloat16)
    next_border_slice = from_behind(backward_preactivation[:DILATION_SIZE], "tm", -1)
    following_window = jnp.concatenate(
        [backward_preactivation[DILATION_SIZE:], next_border_slice], 0
    )
    grad_inputs = grad_float + jnp.einsum(
        "oc,ton->tcn", conv_w[1], backward_preactivation, preferred_element_type=jnp.float32
    )
    grad_inputs = grad_inputs + jnp.einsum(
        "oc,ton->tcn", conv_w[0], following_window, preferred_element_type=jnp.float32
    )
    grad_inputs = grad_inputs.astype(jnp.bfloat16)[None]
    grad_conv_w = jnp.stack(
        [
            jnp.einsum(
                "ton,tcn->oc",
                backward_preactivation,
                preceding_window,
                preferred_element_type=jnp.float32,
            ),
            jnp.einsum(
                "ton,tcn->oc",
                backward_preactivation,
                sample_input,
                preferred_element_type=jnp.float32,
            ),
        ]
    )
    grad_conv_b = jnp.sum(backward_preactivation.astype(jnp.float32), axis=(0, 2))
    grad_conv_w, grad_conv_b, grad_mix_w, grad_mix_b = lax.psum(
        (grad_conv_w, grad_conv_b, grad_mix_w, grad_mix_b), ("dp", "space", "tm")
    )
    cell_count = (
        inputs.shape[0]
        * timestep_count
        * sensor_count
        * lax.axis_size("dp")
        * lax.axis_size("space")
        * lax.axis_size("tm")
    )
    scale = 1.0 / math.sqrt(cell_count)
    return (
        outputs,
        grad_inputs,
        grad_conv_w * scale,
        grad_conv_b * scale,
        grad_mix_w * scale,
        grad_mix_b * scale,
    )


BF16 = jnp.bfloat16
AXES = ("dp", "space", "tm")
F32 = jnp.float32
NT = (((1,), (1,)), ((), ()))
VMEM_BYTES = 24 * 1024 * 1024


def mm(left, right):
    return jnp.dot(left, right, preferred_element_type=F32)


def mm_nt(left, right):
    return lax.dot_general(left, right, NT, preferred_element_type=F32)


def upper_lanes(shape):
    return lax.broadcasted_iota(jnp.int32, shape, 1) >= shape[1] // 2


def halves(matrix):
    upper = upper_lanes(matrix.shape)
    zero = jnp.zeros_like(matrix)
    return jnp.where(upper, zero, matrix), jnp.where(upper, matrix, zero)


def fold(first, second):
    return jnp.where(upper_lanes(first.shape), second, first)


def times_halves(left, right):
    half = left.shape[0] // 2
    return fold(mm(left[:half], right), mm(left[half:], right))


def link_rows(packed):
    packed = packed.astype(F32)
    turned = pltpu.roll(packed, packed.shape[1] // 2, 1)
    return jnp.concatenate([halves(packed)[0], halves(turned)[0]], 0).astype(BF16)


def column(row):
    size = row.shape[1]
    first = lax.broadcasted_iota(jnp.int32, (size, size), 0)
    second = lax.broadcasted_iota(jnp.int32, (size, size), 1)
    return jnp.sum(jnp.where(first == second, row, 0.0), axis=1, keepdims=True)


def fetch(pairs, sems):
    copies = [
        pltpu.make_async_copy(source, target, sems.at[index])
        for index, (source, target) in enumerate(pairs)
    ]
    for copy in copies:
        copy.start()
    return copies


def prepare_kernel(
    cols_hbm,
    counts_hbm,
    rows_hbm,
    adj_hbm,
    grad_hbm,
    input_hbm,
    packed_ref,
    own_ref,
    halo_ref,
    chosen_ref,
    grad_ref,
    tail_ref,
    adj_ref,
    cols_ref,
    counts_ref,
    rows_ref,
    sems,
):
    row_blocks, slots, tile = adj_ref.shape[:3]
    own_slots = slots // 2
    steps = input_hbm.shape[0]
    copies = fetch(
        [
            (adj_hbm.at[:, pl.ds(own_slots, own_slots)], adj_ref.at[:, pl.ds(own_slots, own_slots)]),
            (cols_hbm, cols_ref),
            (counts_hbm, counts_ref),
            (rows_hbm, rows_ref),
            (adj_hbm.at[:, pl.ds(0, own_slots)], adj_ref.at[:, pl.ds(0, own_slots)]),
            (grad_hbm, grad_ref),
            (input_hbm.at[pl.ds(steps - DILATION_SIZE, DILATION_SIZE)], tail_ref),
        ],
        sems,
    )
    other = 1 - lax.axis_index("space")
    sensors = grad_ref.shape[1]
    rows_count = grad_ref.shape[0]
    slot_count = rows_ref.shape[2]
    upper = upper_lanes((tile, tile)).astype(jnp.int32)
    for copy in copies[:5]:
        copy.wait()
    for r in range(row_blocks):
        far = adj_ref[r, own_slots].astype(F32)
        for k in range(own_slots + 1, slots):
            far = far + adj_ref[r, k].astype(F32)
        far = jnp.where(upper == other, far, pltpu.roll(far, tile // 2, 1))
        halo_ref[r * tile : (r + 1) * tile, :] = far.astype(BF16)
    rows = rows_ref[0, pl.ds(other, 1), :]
    rows = jnp.concatenate([rows, rows], 1)
    lanes = lax.broadcasted_iota(jnp.int32, (1, 2 * slot_count), 1)
    place = lanes - jnp.where(lanes >= slot_count, slot_count, 0)
    rows = jnp.where(place < counts_ref[0, other], rows, -1)
    sensor = lax.broadcasted_iota(jnp.int32, (sensors, 2 * slot_count), 0)
    chosen = jnp.where(sensor == rows, 1.0, 0.0).astype(F32)
    chosen_ref[...] = chosen.astype(BF16)
    turned = jnp.transpose(chosen)[:slot_count].astype(BF16)
    halo = halo_ref[...]
    packed_ref[rows_count:, :] = times_halves(turned, halo).astype(BF16)
    for r in range(row_blocks):
        sums = [jnp.zeros((tile, tile), F32), jnp.zeros((tile, tile), F32)]
        for k in range(own_slots):
            item = adj_ref[r, k].astype(F32)
            for block in range(2):
                share = jnp.where(cols_ref[r, k] == block, 1.0, 0.0).astype(F32)
                sums[block] = sums[block] + item * share
        own_ref[r * tile : (r + 1) * tile, :] = jnp.concatenate(sums, 1).astype(BF16)
    both = fold(halo, mm(own_ref[...], halo).astype(BF16))
    copies[5].wait()
    packed_ref[:rows_count, :] = mm(grad_ref[...], both).astype(BF16)
    copies[6].wait()


def gate_step(t, earlier, input_ref, preact, hidden_ref, slopes_ref, right_ref):
    steps, chans, sensors = input_ref.shape
    at = slice(t * chans, (t + 1) * chans)
    span = slice(t * sensors, (t + 1) * sensors)
    filtered = jnp.tanh(preact[:chans])
    gating = 0.5 * jnp.tanh(0.5 * preact[chans:]) + 0.5
    product = filtered * gating
    hidden = product.astype(BF16)
    hidden_ref[at, :] = hidden
    slopes_ref[t, :chans] = (1.0 - filtered * filtered) * gating
    slopes_ref[t, chans:] = product * (1.0 - gating)
    right_ref[:chans, span] = earlier
    right_ref[chans : 2 * chans, span] = input_ref[t]
    right_ref[2 * chans : 2 * chans + 16, span] = jnp.ones((16, sensors), BF16)
    right_ref[2 * chans + 16 : 3 * chans + 16, span] = hidden
    right_ref[3 * chans + 16 :, span] = hidden


def forward_kernel(
    input_hbm,
    conv_w_hbm,
    conv_b_hbm,
    mix_w_hbm,
    mix_b_hbm,
    grad_ref,
    own_ref,
    chosen_ref,
    hidden_ref,
    slopes_ref,
    right_ref,
    near_ref,
    spread_ref,
    input_ref,
    taps_ref,
    turned_taps_ref,
    bias_ref,
    mix_ref,
    mixing_ref,
    mix_bias_ref,
    mix_wide_ref,
    boundary_ref,
    sems,
):
    copies = fetch(
        [
            (input_hbm, input_ref),
            (conv_w_hbm, taps_ref),
            (conv_b_hbm, bias_ref),
            (mix_w_hbm, mix_ref),
            (mix_b_hbm, mix_bias_ref),
        ],
        sems,
    )
    steps, chans, sensors = input_ref.shape
    own = own_ref[...]
    near = mm(grad_ref[...], own)
    near_ref[:, :sensors] = near
    near_ref[:, sensors:] = mm(near.astype(BF16), own)
    turned = jnp.transpose(chosen_ref[...].astype(F32)).astype(BF16)
    slot_count = turned.shape[0] // 2
    spread_ref[:, :sensors] = jnp.where(
        lax.broadcasted_iota(jnp.int32, turned.shape, 0) < slot_count,
        turned,
        jnp.zeros_like(turned),
    )
    spread_ref[:slot_count, sensors:] = mm(turned[:slot_count], own).astype(BF16)
    spread_ref[slot_count:, sensors:] = turned[slot_count:]
    for copy in copies:
        copy.wait()
    mixing = jnp.transpose(mix_ref[...].reshape(3 * chans, chans).astype(F32))
    mixing_ref[...] = mixing.astype(BF16)
    mix_wide_ref[...] = jnp.concatenate([mix_ref[0], mix_ref[1], mix_ref[2]], 1)
    taps = taps_ref[...].reshape(2 * chans, 2 * chans).astype(F32)
    taps = jnp.transpose(taps).astype(BF16)
    turned_taps_ref[...] = taps
    bias = column(bias_ref[...])
    for t in range(DILATION_SIZE, steps):
        earlier = input_ref[t - DILATION_SIZE]
        preact = mm(taps, jnp.concatenate([earlier, input_ref[t]], 0)) + bias
        gate_step(t, earlier, input_ref, preact, hidden_ref, slopes_ref, right_ref)
    hidden = hidden_ref[DILATION_SIZE * chans :, :]
    boundary_ref[DILATION_SIZE * chans :, :] = boundary_rows(hidden, own, chosen_ref[...])


def backward_kernel(
    grad_ref,
    own_packed_ref,
    packed_ref,
    border_ref,
    near_ref,
    spread_ref,
    input_ref,
    turned_taps_ref,
    bias_ref,
    mixing_ref,
    hidden_old_ref,
    slopes_old_ref,
    right_old_ref,
    kept_ref,
    given_ref,
    back_ref,
    hidden_ref,
    left_scr,
    both_scr,
    slopes_ref,
    right_ref,
):
    steps, wide, sensors = back_ref.shape
    chans = wide // 2
    rows = steps * chans
    border_rows = DILATION_SIZE * chans
    border_span = DILATION_SIZE * sensors
    core = lax.axis_index("dp") % 2
    linked = mm(link_rows(packed_ref[rows:, :]), spread_ref[:, :sensors]).astype(BF16)
    blank = jnp.zeros_like(linked)
    linked = jnp.concatenate([blank, linked], 1)
    spread = jnp.concatenate([spread_ref[...], linked, jnp.zeros_like(linked)], 0)
    packed = jnp.concatenate([packed_ref[:rows, :], own_packed_ref[:rows, :]], 1)
    both_scr[...] = (near_ref[...] + mm(packed, spread)).astype(BF16)
    bias = column(bias_ref[...])
    place = lax.axis_index("tm")
    hidden_ref[border_rows:, :] = hidden_old_ref[border_rows:, :]
    for t in range(DILATION_SIZE):
        earlier = border_ref[t]
        earlier = jnp.where(place > 0, earlier, jnp.zeros_like(earlier))
        window = jnp.concatenate([earlier, input_ref[t]], 0)
        preact = mm(turned_taps_ref[...], window) + bias
        gate_step(t, earlier, input_ref, preact, hidden_ref, slopes_ref, right_ref)
    mixing = mixing_ref[...]
    for t in range(steps):
        at = slice(t * chans, (t + 1) * chans)
        span = slice(t * sensors, (t + 1) * sensors)
        fields = jnp.concatenate(
            [grad_ref[at, :], both_scr[at, :sensors], both_scr[at, sensors:]], 0
        )
        back_hidden = mm(mixing, fields)
        back_hidden = jnp.concatenate([back_hidden, back_hidden], 0)
        slopes = slopes_ref[t] if t < DILATION_SIZE else slopes_old_ref[t]
        back_pre = (back_hidden * slopes).astype(BF16)
        back_ref[t] = back_pre
        left_scr[:wide, span] = back_pre
        left_scr[wide:, span] = fields
    ones = wide + 16
    conv = mm_nt(right_old_ref[:ones, border_span:], left_scr[: wide + chans, border_span:])
    conv = conv + mm_nt(right_ref[:ones, :], left_scr[: wide + chans, :border_span])
    mixes = mm_nt(left_scr[wide:, border_span:], right_old_ref[ones:, border_span:])
    mixes = mixes + mm_nt(left_scr[wide:, :border_span], right_ref[ones:, :])
    sums = conv[wide : wide + 8]
    conv = conv[:wide, :wide]
    zero, first, second = [mixes[k * chans : (k + 1) * chans] for k in range(3)]
    half = chans // 2
    blank = jnp.zeros((8, wide), F32)
    mix_sums = jnp.concatenate([sums[:, wide:], blank[:, :chans]], 1)
    upper_rows = lax.broadcasted_iota(jnp.int32, blank.shape, 0) >= 4
    biases = jnp.where(upper_rows, mix_sums, sums[:, :wide])
    packed = jnp.concatenate(
        [conv, fold(zero, first), fold(second[:half], second[half:]), biases, blank], 0
    )
    cut = packed.shape[0] // 2
    kept_ref[...] = jnp.where(core == 0, packed[:cut], packed[cut:])
    given_ref[...] = jnp.where(core == 0, packed[cut:], packed[:cut])


def boundary_rows(hidden, own, chosen):
    chosen_low, chosen_high = halves(chosen)
    hop = mm_nt(hidden, own).astype(BF16)
    return (mm(hidden, chosen_low) + mm(hop, chosen_high)).astype(BF16)


def early_kernel(back_ref, taps_ref, early_ref):
    for t in range(DILATION_SIZE):
        early_ref[t] = mm(taps_ref[0], back_ref[t]).astype(BF16)


def boundary_kernel(hidden_ref, late_ref, own_ref, chosen_ref, boundary_ref):
    early_rows = DILATION_SIZE * chosen_ref.shape[1] // 2
    hidden = hidden_ref[:early_rows, :]
    boundary_ref[:early_rows, :] = boundary_rows(hidden, own_ref[...], chosen_ref[...])


def hops_kernel(hidden_ref, packed_ref, own_ref, halo_ref, base_ref, spread_ref):
    sensors = own_ref.shape[0]
    slots = halo_ref.shape[1] // 2
    rows = hidden_ref.shape[0]
    own = own_ref[...]
    one = mm_nt(hidden_ref[...], own)
    base_ref[:, :sensors] = one
    base_ref[:, sensors:] = mm_nt(one.astype(BF16), own)
    halo = halo_ref[...]
    link = link_rows(packed_ref[rows:, :])
    link = jnp.concatenate([link, jnp.zeros_like(link)], 0)
    turned = jnp.transpose(jnp.concatenate([halo.astype(F32), mm(halo, link)], 1)).astype(BF16)
    blank = jnp.zeros((slots, sensors), BF16)
    first = turned[:slots]
    spread_ref[:slots, :sensors] = first
    spread_ref[:slots, sensors:] = mm_nt(first, own).astype(BF16)
    for block in range(1, 4):
        at = slice(block * slots, (block + 1) * slots)
        spread_ref[at, :sensors] = blank
        spread_ref[at, sensors:] = turned[at] if block < 3 else blank


def finish_kernel(
    input_ref,
    hidden_ref,
    own_boundary_ref,
    boundary_ref,
    base_ref,
    spread_ref,
    mix_ref,
    bias_ref,
    grad_ref,
    back_ref,
    early_ref,
    taps_ref,
    out_hbm,
    grad_out_hbm,
    out_scr,
    grad_scr,
    both_scr,
    sems,
):
    steps, chans, sensors = input_ref.shape
    has_later = lax.axis_index("tm") < lax.axis_size("tm") - 1
    taps = jnp.concatenate([taps_ref[0], taps_ref[1]], 1)
    chunk = steps // 2
    copies = []

    def send(scratch, target, start):
        span = pl.ds(start, chunk)
        copy = pltpu.make_async_copy(scratch.at[span], target.at[span], sems.at[len(copies)])
        copy.start()
        copies.append(copy)

    for t in range(steps):
        at = slice(t * chans, (t + 1) * chans)
        later = t + DILATION_SIZE
        total = grad_ref[at, :].astype(F32)
        if later < steps:
            total = total + mm(taps, jnp.concatenate([back_ref[later], back_ref[t]], 0))
        else:
            early = early_ref[later - steps].astype(F32)
            early = jnp.where(has_later, early, jnp.zeros_like(early))
            total = total + mm(taps_ref[1], back_ref[t]) + early
        grad_scr[t] = total.astype(BF16)
        if (t + 1) % chunk == 0:
            send(grad_scr, grad_out_hbm, t + 1 - chunk)
    boundary = jnp.concatenate([boundary_ref[...], own_boundary_ref[...]], 1)
    both_scr[...] = (base_ref[...] + mm(boundary, spread_ref[...])).astype(BF16)
    bias = column(bias_ref[...])
    mix = mix_ref[...]
    for t in range(steps):
        at = slice(t * chans, (t + 1) * chans)
        fields = jnp.concatenate(
            [hidden_ref[at, :], both_scr[at, :sensors], both_scr[at, sensors:]], 0
        )
        out_scr[t] = (mm(mix, fields) + bias + input_ref[t].astype(F32)).astype(BF16)
        if (t + 1) % chunk == 0:
            send(out_scr, out_hbm, t + 1 - chunk)
    for copy in copies:
        copy.wait()


def final_kernel(scale, kept_ref, other_ref, conv_w_ref, conv_b_ref, mix_w_ref, mix_b_ref):
    core = lax.axis_index("dp") % 2
    kept = kept_ref[...] * scale
    other = other_ref[...] * scale
    lower = jnp.where(core == 0, kept, other)
    upper = jnp.where(core == 0, other, kept)
    chans, wide = conv_w_ref.shape[1:]
    half = chans // 2
    start = wide - lower.shape[0]
    conv_w_ref[0] = lower[:chans]
    conv_w_ref[1] = jnp.concatenate([lower[chans:], upper[:start]], 0)
    first = upper[start : start + chans]
    second = upper[start + chans : start + chans + half]
    mix_w_ref[0] = first[:, :chans]
    mix_w_ref[1] = pltpu.roll(first, chans, 1)[:, :chans]
    mix_w_ref[2] = jnp.concatenate([second, pltpu.roll(second, chans, 1)], 0)[:, :chans]
    start = start + chans + half
    biases = upper[start : start + 8] + upper[start + 8 :]
    conv_b_ref[...] = biases[:1]
    mix_b_ref[...] = biases[4:5, :chans]


VMEM = pl.BlockSpec(memory_space=pltpu.VMEM)
HBM = pl.BlockSpec(memory_space=pltpu.HBM)
DMA = pltpu.SemaphoreType.DMA


def call(kernel, name, in_specs, out_shape, args, scratch=(), micros=1.0, space=None, aliases=None):
    args = [
        pltpu.with_memory_space_constraint(arg, pltpu.HBM) if spec is HBM else arg
        for spec, arg in zip(in_specs, args)
    ]
    return pl.pallas_call(
        kernel,
        out_shape=out_shape,
        in_specs=in_specs,
        out_specs=jax.tree.map(lambda _: space or VMEM, out_shape),
        scratch_shapes=list(scratch),
        input_output_aliases=aliases or {},
        compiler_params=pltpu.CompilerParams(vmem_limit_bytes=VMEM_BYTES),
        cost_estimate=pl.CostEstimate(
            flops=0, bytes_accessed=int(micros * 3_600_000), transcendentals=0
        ),
        name=name,
    )(*args)


def swap(value, axis, bit):
    count = lax.axis_size(axis)
    return lax.ppermute(value, axis, [(source, source ^ bit) for source in range(count)])


def shift(value, axis, steps):
    count = lax.axis_size(axis)
    return lax.ppermute(value, axis, [(source, (source + steps) % count) for source in range(count)])


def flip(value, mask):
    sizes = [lax.axis_size(axis) for axis in AXES]
    places = list(itertools.product(*[range(size) for size in sizes]))
    index = {place: number for number, place in enumerate(places)}
    pairs = [
        (index[place], index[tuple(part ^ bit for part, bit in zip(place, mask))])
        for place in places
    ]
    return lax.ppermute(value, AXES, pairs)


def groups():
    dp, space, tm = [bits(lax.axis_size(axis)) for axis in AXES]
    first = [(bit, 0, 0) for bit in dp[1:]]
    second = [(0, bit, 0) for bit in space]
    third = [(0, 0, bit) for bit in tm]
    orders = ((2, 0, 1), (1, 0, 2))
    return [closure(masks, order) for masks, order in zip((first + second, third), orders) if masks]


def closure(masks, order):
    found = [(0, 0, 0)]
    for mask in masks:
        found = found + [tuple(left ^ right for left, right in zip(item, mask)) for item in found]
    found = found[1:]
    return [found[place] for place in order] if len(found) == len(order) else found


def bits(count):
    return [1 << place for place in range(count.bit_length() - 1)]


def to_bf16(value):
    return lax.reduce_precision(value, exponent_bits=8, mantissa_bits=7)


def round_sums(sums, has_biases):
    end = sums.shape[0]
    high = sums[end - 16 : end - 8]
    rest = jnp.pad((high - to_bf16(high)) * has_biases, ((end - 8, 0), (0, 0)))
    return to_bf16(sums + rest)


def after(value, *earlier):
    return lax.optimization_barrier((value, *earlier))[0]


def pair_body(inputs, grad_out, conv_w, conv_b, mix_w, mix_b, adj_tiles, tile_cols, send_rows, counts):
    sample_input = inputs[0]
    sample_grad = grad_out[0]
    steps, chans, sensors = sample_input.shape
    rows = steps * chans
    half_rows = rows // 2
    wide = 2 * chans
    shape = jax.ShapeDtypeStruct
    border_rows = DILATION_SIZE * chans
    grad_flat = sample_grad.reshape(rows, sensors)
    taps = jnp.transpose(conv_w, (0, 2, 1))
    packed, own, halo, chosen, grad, tail = call(
        prepare_kernel,
        "prepare",
        [HBM] * 6,
        (
            shape((rows + chans // 2, wide), BF16),
            shape((sensors, sensors), BF16),
            shape((sensors, wide), BF16),
            shape((sensors, wide), BF16),
            shape((rows, sensors), BF16),
            shape((DILATION_SIZE, chans, sensors), BF16),
        ),
        (tile_cols, counts, send_rows, adj_tiles, grad_flat, sample_input),
        scratch=(
            pltpu.VMEM(adj_tiles.shape, BF16),
            pltpu.SMEM(tile_cols.shape, jnp.int32),
            pltpu.SMEM(counts.shape, jnp.int32),
            pltpu.VMEM(send_rows.shape, jnp.int32),
            DMA((7,)),
        ),
        micros=2.0,
    )
    packed_far = swap(packed, "space", 1)
    border = shift(tail, "tm", 1)
    hidden_late, slopes, right, near, spread, kept_input, kept_taps, turned_taps, bias, mix, mixing, mix_bias, mix_wide, boundary_late = call(
        forward_kernel,
        "forward",
        [HBM] * 5 + [VMEM] * 3,
        (
            shape((rows, sensors), BF16),
            shape((steps, wide, sensors), F32),
            shape((2 * wide + 16, steps * sensors), BF16),
            shape((rows, 2 * sensors), F32),
            shape((wide, 2 * sensors), BF16),
            shape(sample_input.shape, BF16),
            shape(taps.shape, BF16),
            shape((wide, wide), BF16),
            shape((1, wide), F32),
            shape(mix_w.shape, BF16),
            shape((chans, 3 * chans), BF16),
            shape((1, chans), F32),
            shape((chans, 3 * chans), BF16),
            shape((rows, wide), BF16),
        ),
        (
            sample_input,
            taps,
            conv_b.reshape(1, wide),
            mix_w,
            mix_b.reshape(1, chans),
            grad,
            own,
            chosen,
        ),
        scratch=(DMA((5,)),),
        micros=1.5,
    )
    border_span = DILATION_SIZE * sensors
    sum_rows = (wide + chans + chans // 2 + 16) // 2
    kept, given, back, hidden = call(
        backward_kernel,
        "backward",
        [VMEM] * 13,
        (
            shape((sum_rows, wide), F32),
            shape((sum_rows, wide), F32),
            shape((steps, wide, sensors), BF16),
            shape((rows, sensors), BF16),
        ),
        (
            grad,
            packed,
            packed_far,
            border,
            near,
            spread,
            kept_input,
            turned_taps,
            bias,
            mixing,
            hidden_late,
            slopes,
            right,
        ),
        scratch=(
            pltpu.VMEM((wide + 3 * chans, steps * sensors), BF16),
            pltpu.VMEM((rows, 2 * sensors), BF16),
            pltpu.VMEM((DILATION_SIZE, wide, sensors), F32),
            pltpu.VMEM((2 * wide + 16, border_span), BF16),
        ),
        micros=2.0,
    )
    total = kept + swap(given.astype(BF16), "dp", 1).astype(F32)
    rounds = groups()
    has_biases = (lax.axis_index("dp") % 2).astype(F32)
    early = call(
        early_kernel,
        "early",
        [VMEM] * 2,
        shape((DILATION_SIZE, chans, sensors), BF16),
        (back, kept_taps),
        micros=0.3,
    )
    early_far = shift(early, "tm", -1)
    boundary_first = call(
        boundary_kernel,
        "boundary",
        [VMEM] * 4,
        shape((rows, wide), BF16),
        (hidden, boundary_late, own, chosen),
        aliases={1: 0},
        micros=0.3,
    )
    first_far = swap(boundary_first, "space", 1)
    base, hop_spread = call(
        hops_kernel,
        "hops",
        [VMEM] * 4,
        (shape((rows, 2 * sensors), F32), shape((2 * wide, 2 * sensors), BF16)),
        (hidden, packed_far, own, halo),
        micros=0.5,
    )
    outputs, grad_inputs = call(
        finish_kernel,
        "finish",
        [VMEM] * 12,
        (shape(sample_input.shape, BF16), shape(sample_grad.shape, BF16)),
        (
            kept_input,
            hidden,
            boundary_first,
            first_far,
            base,
            hop_spread,
            mix_wide,
            mix_bias,
            grad,
            back,
            early_far,
            kept_taps,
        ),
        scratch=(
            pltpu.VMEM(sample_input.shape, BF16),
            pltpu.VMEM(sample_grad.shape, BF16),
            pltpu.VMEM((rows, 2 * sensors), BF16),
            DMA((4,)),
        ),
        micros=2.0,
        space=HBM,
    )
    ready = {-2: (first_far, base), -1: (outputs, grad_inputs)}
    for index, group in enumerate(rounds):
        rounded = round_sums(total, has_biases)
        sent = rounded.astype(BF16)
        parts = [rounded] + [flip(sent, mask).astype(F32) for mask in group]
        parts[1] = after(parts[1], *ready.get(index - len(rounds), ()))
        while len(parts) > 1:
            parts = [left + right for left, right in zip(parts[::2], parts[1::2])]
        total = parts[0]
    total_far = swap(total, "dp", 1)
    cell_count = (
        inputs.shape[0]
        * steps
        * sensors
        * lax.axis_size("dp")
        * lax.axis_size("space")
        * lax.axis_size("tm")
    )
    scale = 1.0 / math.sqrt(cell_count)
    grad_taps, grad_conv_b, grad_mix_w, grad_mix_b = call(
        functools.partial(final_kernel, scale),
        "final",
        [VMEM] * 2,
        (
            shape((2, chans, wide), F32),
            shape((1, wide), F32),
            shape((3, chans, chans), F32),
            shape((1, chans), F32),
        ),
        (total, total_far),
    )
    return (
        outputs[None],
        grad_inputs[None],
        jnp.transpose(grad_taps, (0, 2, 1)),
        grad_conv_b.reshape(wide),
        grad_mix_w,
        grad_mix_b.reshape(chans),
    )


def power_of_two(count):
    return count & (count - 1) == 0


def body(inputs, grad_out, conv_w, conv_b, mix_w, mix_b, adj_tiles, tile_cols, send_rows, counts):
    tile = adj_tiles.shape[2]
    axes = [lax.axis_size(axis) for axis in ("dp", "space", "tm")]
    fits = (
        axes[1] == 2
        and axes[0] % 2 == 0
        and all(power_of_two(count) for count in axes)
        and inputs.shape[0] == 1
        and inputs.shape[3] == 2 * tile
        and inputs.shape[2] * 2 == tile
        and send_rows.shape[2] * 2 == tile
    )
    chosen = pair_body if fits else general_body
    return chosen(
        inputs, grad_out, conv_w, conv_b, mix_w, mix_b, adj_tiles, tile_cols, send_rows, counts
    )


def solution(mesh):
    in_specs = (
        P("dp", "tm", None, "space"),
        P("dp", "tm", None, "space"),
        P(),
        P(),
        P(),
        P(),
        P("space", None, None, None),
        P("space", None),
        P("space", None, None),
        P("space", None),
    )
    out_specs = (P("dp", "tm", None, "space"), P("dp", "tm", None, "space"), P(), P(), P(), P())
    return jax.shard_map(body, mesh=mesh, in_specs=in_specs, out_specs=out_specs, check_vma=False)
```
